128 devices in a mesh: frm: 8 (over y_lo, z), pat: 16 (over x, y_hi, core).
Axes of the slice: x: 4, y: 4 (y_hi: 2, y_lo: 2; y = y_hi * 2 + y_lo), z: 4, core: 2. Of those that a mesh axis runs over, the one named last changes fastest.
Arguments:
- frames: float32 [8, 2048, 2048], P('frm', 'pat'), may hold values from -6 to 6
- shifts: float32 [8, 2], P('frm'), may hold values from -0.5 to 0.5
- coefficients: float32 [8, 512, 40], P('frm', 'pat'), may hold values from -0.9 to 0.9
- anchors: int32 [512, 2], P('pat'), may hold values from 0 to 1960, as said below
- assign: int32 [512], P('pat'), may hold values from 0 to 15, as said below
Outputs:
- new_coefficients: float32 [8, 512, 40], P('frm', 'pat')
- object_spectra: float32 [512, 2, 7744], P(('pat', 'frm'))
The draws below stay inside these ranges and needn't reach their ends.
Inputs may be any that keep to these rules, and one draw needn't show every extreme that they name: `anchors`: the anchor row of patch p lies in p // 32 * 128 to p // 32 * 128 + 127 and is at most 1960; the anchor column is at most 1960. `assign`: among the 32 patches p of one value of p // 32, exactly 2 carry each group number.
All inputs are finite; a program needn't handle non-finite values.
Results may differ from the reference program's by a relative error of at most 0.0003.
Values sent between devices are 32-bit elements; how exact they have to be, the bound alone decides.
A program may use at most 128 MiB of HBM per device.

```python
import math
import jax
import jax.numpy as jnp
from jax import lax

PATCH = 88
MODES = 40
ITERS = 2
COLS = 2048
SH = 128
PPS = 32
FRAMES = 8
ROWS = 2048
PATCHES = 512
N_PAT = 16


def draw_anchors(key, part):
    row_key, col_key = jax.random.split(jax.random.fold_in(key, 11))
    strip_index = jnp.arange(PATCHES, dtype=jnp.int32) // PPS
    lowest = strip_index * SH
    highest = jnp.minimum(lowest + SH, ROWS - PATCH + 1)
    offsets = jax.random.randint(row_key, (PATCHES,), 0, 1 << 20, dtype=jnp.int32)
    row_start = lowest + offsets % (highest - lowest)
    col_start = jax.random.randint(col_key, (PATCHES,), 0, COLS - PATCH + 1, dtype=jnp.int32)
    return jnp.stack([row_start, col_start], axis=1).astype(jnp.int32)


def draw_assign(key, part):
    per_group = PPS // N_PAT
    strip_keys = jax.random.split(jax.random.fold_in(key, 23), N_PAT)
    targets = jnp.arange(PPS, dtype=jnp.int32) // per_group

    def shuffle_strip(strip_key):
        return jax.random.permutation(strip_key, targets)
    return jax.vmap(shuffle_strip)(strip_keys).reshape(PATCHES).astype(jnp.int32)


def shard_levels(key, dims, cuts, least, top_value):
    gain, own = 1.0, jax.random.fold_in(key, 6)
    for axis_at, blocks in cuts:
        draws = jnp.exp(jax.random.uniform(jax.random.fold_in(own, axis_at), (blocks,), jnp.float32, least / len(cuts), top_value / len(cuts)))
        gain = gain * jnp.repeat(draws, dims[axis_at] // blocks).reshape([-1 if axis == axis_at else 1 for axis in range(len(dims))])
    return gain


def normal_values(rng, dims, width, most, shards=(), kind=jnp.bfloat16):
    drawn = jax.random.normal(rng, dims, jnp.float32) * width
    if len(shards) > 0:
        drawn = shard_levels(rng, dims, shards, -0.22, 0.18) * drawn
    return jnp.clip(drawn, min=-most, max=most).astype(kind)


def setup_inputs(seed: int = 0) -> dict:
    seeds = jax.random.split(jax.random.key(seed), 6)
    return {
        "frames": normal_values(seeds[0], (FRAMES, ROWS, COLS), 1.0, 6.0, ((0, 8), (1, 16)), jnp.float32),
        "shifts": jnp.clip(jax.random.uniform(seeds[1], (FRAMES, 2), jnp.float32, -0.5, 0.5) * shard_levels(seeds[1], (FRAMES, 2), ((0, 8),), -0.4, 0.0), -0.5, 0.5),
        "coefficients": normal_values(seeds[2], (FRAMES, PATCHES, MODES), 0.15, 0.9, ((0, 8), (1, 16)), jnp.float32),
        "anchors": draw_anchors(jax.random.fold_in(seeds[5], 71), 0),
        "assign": draw_assign(jax.random.fold_in(seeds[5], 71), 0),
    }


damping = 0.05
step_size = 64.0

def noll_index(j):
    n = 0
    remaining = j - 1
    while remaining > n:
        n += 1
        remaining -= n
    m = (-1) ** j * (n % 2 + 2 * ((remaining + (n + 1) % 2) // 2))
    return (n, m)

def zernike_table(length, number):
    centre = length / 2.0
    coords = (jnp.arange(length, dtype=jnp.float32) - centre) / (length / 4.0)
    row_grid = jnp.broadcast_to(coords[:, None], (length, length))
    col_grid = jnp.broadcast_to(coords[None, :], (length, length))
    radius = jnp.sqrt(row_grid * row_grid + col_grid * col_grid)
    angle_grid = jnp.arctan2(row_grid, col_grid)
    inside = (radius <= 1.0).astype(jnp.float32)
    surfaces = []
    for j in range(2, number + 2):
        n, m = noll_index(j)
        order_abs = abs(m)
        radial = jnp.zeros((length, length), jnp.float32)
        for k in range((n - order_abs) // 2 + 1):
            factor = (-1) ** k * math.factorial(n - k) / (math.factorial(k) * math.factorial((n + order_abs) // 2 - k) * math.factorial((n - order_abs) // 2 - k))
            radial = radial + factor * radius ** (n - 2 * k)
        if m == 0:
            surface = math.sqrt(n + 1) * radial
        elif m > 0:
            surface = math.sqrt(2 * (n + 1)) * radial * jnp.cos(order_abs * angle_grid)
        else:
            surface = math.sqrt(2 * (n + 1)) * radial * jnp.sin(order_abs * angle_grid)
        surfaces.append(surface * inside)
    return (jnp.stack(surfaces), inside)

def window_table(length):
    ramp_index = jnp.arange(length, dtype=jnp.float32)
    profile = 0.5 - 0.5 * jnp.cos(2.0 * jnp.pi * (ramp_index + 0.5) / length)
    return profile[:, None] * profile[None, :]

def signed_frequencies(length):
    ramp_index = jnp.arange(length, dtype=jnp.int32)
    return ((ramp_index + length // 2) % length - length // 2).astype(jnp.float32)

def squared_modulus(values):
    return jnp.real(values) ** 2 + jnp.imag(values) ** 2

def solve_block(frames, shifts, zernike_modes, aperture, spread_scale, anchors_block, start_block):

    def cut_patch(anchor):
        return lax.dynamic_slice(frames, (anchor[0] * 0, anchor[0], anchor[1]), (FRAMES, PATCH, PATCH))
    blocks = jax.vmap(cut_patch)(anchors_block)
    spectra = jnp.fft.fft2(blocks * window_table(PATCH))
    frequencies = signed_frequencies(PATCH)
    ramp_angle = -2.0 * jnp.pi / PATCH * (frequencies[None, :, None] * shifts[:, 0, None, None] + frequencies[None, None, :] * shifts[:, 1, None, None])
    data_spectrum = spectra * jnp.exp(1j * ramp_angle)[None]
    energy = lax.optimization_barrier(jnp.sum(squared_modulus(data_spectrum), axis=(1, 2, 3)))
    current = start_block
    estimate = data_spectrum[:, 0]
    for iteration in range(ITERS):
        phases = jnp.einsum('pfm,mxy->pfxy', current, zernike_modes, precision=lax.Precision.HIGHEST)
        pupil_field = aperture * jnp.exp(1j * phases)
        focal_field = jnp.fft.fft2(pupil_field)
        spread = spread_scale * squared_modulus(focal_field)
        transfer = jnp.fft.fft2(spread)
        numerator = lax.optimization_barrier(jnp.sum(data_spectrum * jnp.conj(transfer), axis=1))
        denominator = lax.optimization_barrier(jnp.sum(squared_modulus(transfer), axis=1)) + damping
        estimate = numerator / denominator
        misfit = data_spectrum - estimate[:, None] * transfer
        grad_transfer = -2.0 * jnp.conj(estimate)[:, None] * misfit
        grad_spread = jnp.real(jnp.fft.ifft2(grad_transfer)) * (PATCH * PATCH)
        grad_focal = 2.0 * spread_scale * grad_spread * focal_field
        grad_pupil = jnp.fft.ifft2(grad_focal) * (PATCH * PATCH)
        grad_phase = jnp.imag(grad_pupil * jnp.conj(pupil_field))
        grad_coef = jnp.einsum('pfxy,mxy->pfm', grad_phase, zernike_modes, precision=lax.Precision.HIGHEST)
        current = current - step_size * FRAMES * grad_coef / energy[:, None, None]
    return (current, jnp.real(estimate), jnp.imag(estimate))

def reference(frames, shifts, coefficients, anchors, assign):
    zernike_modes, aperture = zernike_table(PATCH, MODES)
    spread_scale = 1.0 / (PATCH * PATCH * jnp.sum(aperture))
    blocks_anchor = anchors.reshape(N_PAT, PPS, 2)
    blocks_start = jnp.transpose(coefficients, (1, 0, 2)).reshape(N_PAT, PPS, FRAMES, MODES)

    def per_strip(pieces):
        return solve_block(frames, shifts, zernike_modes, aperture, spread_scale, pieces[0], pieces[1])
    finals, estimate_real, estimate_imag = lax.map(per_strip, (blocks_anchor, blocks_start))
    new_coefficients = jnp.transpose(finals.reshape(PATCHES, FRAMES, MODES), (1, 0, 2))
    ordering = jnp.argsort(assign * PATCHES + jnp.arange(PATCHES, dtype=jnp.int32))
    estimates = jnp.stack([estimate_real.reshape(PATCHES, PATCH * PATCH), estimate_imag.reshape(PATCHES, PATCH * PATCH)], axis=1)
    object_spectra = estimates[ordering] / PATCH
    return (new_coefficients, object_spectra)
```

```python
import functools
import math

import jax
import jax.numpy as jnp
import ml_dtypes
import numpy as np
from jax import lax
from jax.experimental import pallas as pl
from jax.experimental.pallas import tpu as pltpu
from jax.sharding import PartitionSpec as P

N = 88
MODES = 40
ITERS = 2
FRAMES = 8
SH = 128
PPS = 32
GROUPS = 16
LOW = 22
NX = 45
XP = 24
NU = 45
ROWS = 184
DAMPING = 0.05
STEP = 64.0
f32, bf16 = jnp.float32, jnp.bfloat16
MESH = pl.DeviceIdType.MESH


def noll_index(j):
    n = 0
    remaining = j - 1
    while remaining > n:
        n += 1
        remaining -= n
    m = (-1) ** j * (n % 2 + 2 * ((remaining + (n + 1) % 2) // 2))
    return (n, m)


def zernike_values(row, col):
    radius = np.sqrt(row * row + col * col)
    angle = np.arctan2(row, col)
    values = []
    for j in range(2, MODES + 2):
        n, m = noll_index(j)
        k_abs = abs(m)
        radial = np.zeros_like(radius)
        for k in range((n - k_abs) // 2 + 1):
            factor = (
                (-1) ** k
                * math.factorial(n - k)
                / (
                    math.factorial(k)
                    * math.factorial((n + k_abs) // 2 - k)
                    * math.factorial((n - k_abs) // 2 - k)
                )
            )
            radial = radial + factor * radius ** (n - 2 * k)
        if m == 0:
            values.append(math.sqrt(n + 1) * radial)
        elif m > 0:
            values.append(math.sqrt(2 * (n + 1)) * radial * np.cos(k_abs * angle))
        else:
            values.append(math.sqrt(2 * (n + 1)) * radial * np.sin(k_abs * angle))
    return np.stack(values)


def ultraspherical(order, t):
    t = np.asarray(t, np.float64)
    inside = (np.arange(NX) + LOW - 44.0) / 22.0

    def raw(x):
        last, value = np.zeros_like(x), np.ones_like(x)
        for n in range(1, order + 1):
            last, value = value, (2.0 * (n + 2.0) * x * value - (n + 4.0) * last) / n
        return value

    weight = np.sqrt(1.0 - inside**2)
    return raw(t) / np.sqrt(np.sum(weight * raw(inside) ** 2) / np.sum(weight))


PAIRS = [(a, b) for a in range(9) for b in range(9 - a)]


def halves(table):
    hi = table.astype(np.float32).astype(ml_dtypes.bfloat16)
    lo = (table - hi.astype(np.float64)).astype(np.float32).astype(ml_dtypes.bfloat16)
    return hi, lo


def right_table(table):
    hi, lo = halves(table)
    return np.concatenate([hi, hi, lo], axis=0)


def left_table(table):
    hi, lo = halves(table)
    return np.concatenate([hi, hi, lo], axis=1)


@functools.lru_cache
def tables():
    w = 2.0 * np.pi / N
    full = np.arange(N)
    px = LOW + np.arange(NX)
    unit = (px - 44.0) / 22.0
    aperture = (unit[:, None] ** 2 + unit[None, :] ** 2 <= 1.0).astype(np.float64)
    a32 = ((px.astype(np.float32) - np.float32(44)) / np.float32(22)).astype(np.float32)
    r32 = np.sqrt(a32[:, None] * a32[:, None] + a32[None, :] * a32[None, :])
    assert np.array_equal(aperture, (r32 <= 1.0).astype(np.float64))
    scale = 1.0 / (N * N * aperture.sum())
    root = math.sqrt(scale)

    grid = np.linspace(-1.0, 1.0, 31)
    rows, cols = (g.ravel() for g in np.meshgrid(grid, grid, indexing="ij"))
    basis = np.stack([ultraspherical(a, rows) * ultraspherical(b, cols) for a, b in PAIRS], axis=1)
    fit = np.linalg.lstsq(basis, zernike_values(rows, cols).T, rcond=None)[0].T

    out = {}
    spread_ab = np.zeros((MODES, 128))
    spread_ab[:, : len(PAIRS)] = fit
    spread_ab[:, 64 : 64 + len(PAIRS)] = fit
    m1 = np.zeros((128, 128))
    m1[:MODES] = spread_ab
    out["m1"] = fine_table(m1)
    out["m2"] = fine_table(m1.T)

    along = np.zeros((XP, 128))
    mask = np.zeros((XP, 128))
    t3 = np.zeros((128, 128))
    for h in range(2):
        for k, (a, b) in enumerate(PAIRS):
            for i in range(XP):
                if i + XP * h < NX:
                    along[i, 64 * h + k] = ultraspherical(a, unit[i + XP * h])
            t3[64 * h + k, 64 * h : 64 * h + NX] = ultraspherical(b, unit)
        for i in range(XP):
            if i + XP * h < NX:
                mask[i, 64 * h : 64 * h + NX] = aperture[i + XP * h]
    out["along"] = np.repeat(along, FRAMES, axis=0).astype(np.float32)
    out["mask"] = np.repeat(mask, FRAMES, axis=0).astype(np.float32)
    out["t3"] = fine_table(t3)
    out["t18"] = fine_table(t3.T)

    ang = w * (np.outer(px, full) % N)
    c, s = np.cos(ang), np.sin(ang)
    for h in range(2):
        t5 = np.zeros((256, 256))
        lanes = slice(64 * h, 64 * h + NX)
        lanes2 = slice(128 + 64 * h, 128 + 64 * h + NX)
        t5[lanes, :N], t5[lanes2, :N] = c, s
        t5[lanes, 128 : 128 + N], t5[lanes2, 128 : 128 + N] = -s, c
        out[f"t5{h}"] = right_table(t5)
        t16 = np.zeros((256, 256))
        t16[:N, lanes], t16[128 : 128 + N, lanes] = c.T, -s.T
        t16[:N, lanes2], t16[128 : 128 + N, lanes2] = s.T, c.T
        out[f"t16{h}"] = right_table(t16)
    l7 = np.zeros((176, 96))
    l7[:N, :NX], l7[:N, 48 : 48 + NX] = c.T, s.T
    l7[N:, :NX], l7[N:, 48 : 48 + NX] = -s.T, c.T
    out["l7"] = left_table(l7 * root)
    l15 = np.zeros((96, 176))
    l15[:NX, :N], l15[:NX, N:] = c, -s
    l15[48 : 48 + NX, :N], l15[48 : 48 + NX, N:] = s, c
    out["l15"] = left_table(l15)

    ang = w * (np.outer(full, full) % N)
    c, s = np.cos(ang), np.sin(ang)
    t9 = np.zeros((128, 256))
    t9[:N, :N], t9[:N, 128 : 128 + N] = c, -s
    out["t9"] = right_table(t9)
    l10 = np.zeros((96, 176))
    l10[:NU, :N], l10[:NU, N:] = c[:NU], s[:NU]
    l10[48 : 48 + NU, :N], l10[48 : 48 + NU, N:] = -s[:NU], c[:NU]
    out["l10"] = left_table(l10)
    t12 = np.zeros((256, 256))
    t12[:N, :N], t12[128 : 128 + N, :N] = c, -s
    t12[:N, 128 : 128 + N], t12[128 : 128 + N, 128 : 128 + N] = s, c
    out["t12"] = right_table(t12)
    weight = np.full((NU,), 2.0)
    weight[0] = weight[44] = 1.0
    weight = weight * (-2.0) * 2.0 * root
    l13 = np.zeros((96, 96))
    l13[:N, :NU], l13[:N, 48 : 48 + NU] = c[:, :NU] * weight, -s[:, :NU] * weight
    out["l13"] = left_table(l13)

    profile = 0.5 - 0.5 * np.cos(2.0 * np.pi * (full + 0.5) / N)
    window = np.zeros((N, 128), np.float32)
    window[:, :N] = profile[:, None] * profile[None, :]
    out["window"] = window
    signed = (full + 44) % N - 44.0
    freq = np.zeros((2, 48, 128), np.float32)
    freq[0, :NU, :] = signed[:NU, None]
    freq[1, :, :N] = signed[None, :]
    out["freq"] = (freq * (-w)).astype(np.float32)

    flip = np.zeros((128, 128), ml_dtypes.bfloat16)
    for v in range(N):
        flip[(N - v) % N, v] = 1
    out["flip"] = np.concatenate([flip, flip], axis=0)
    place = np.zeros((176, 192), ml_dtypes.bfloat16)
    for u in range(N):
        if u < NU:
            place[u, u] = 1
            place[N + u, 48 + u] = 1
        else:
            place[u, 96 + N - u] = 1
            place[N + u, 144 + N - u] = -1
    out["place"] = np.concatenate([place, place], axis=1)
    return out


def fine_table(table):
    hi = table.astype(np.float32).astype(ml_dtypes.bfloat16)
    rest = table - hi.astype(np.float64)
    mid = rest.astype(np.float32).astype(ml_dtypes.bfloat16)
    low = (rest - mid.astype(np.float64)).astype(np.float32).astype(ml_dtypes.bfloat16)
    return np.concatenate([hi, hi, mid, mid, low, hi], axis=0)


def split(x):
    hi = x.astype(bf16)
    return hi, (x - hi.astype(f32)).astype(bf16)


def dot(a, b):
    return jnp.dot(a, b, preferred_element_type=f32)


def right(x, table):
    hi, lo = split(x)
    return dot(jnp.concatenate([hi, lo, hi], axis=1), table)


def fine(x, table):
    hi = x.astype(bf16)
    rest = x - hi.astype(f32)
    mid = rest.astype(bf16)
    low = (rest - mid.astype(f32)).astype(bf16)
    return dot(jnp.concatenate([hi, mid, hi, mid, hi, low], axis=1), table)


def left(table, x):
    hi, lo = split(x)
    return dot(table, jnp.concatenate([hi, lo, hi], axis=0))


def sincos(x):
    k = jnp.floor(x * (2.0 / math.pi) + 0.5)
    r = x - k * 1.5703125
    r = r - k * 4.8351287841796875e-4
    r = r - k * 3.1385570764541626e-07
    z = r * r
    s = r + r * z * (-1.6666654611e-1 + z * (8.3321608736e-3 + z * -1.9515295891e-4))
    c = 1.0 - 0.5 * z + z * z * (
        4.166664568298827e-2 + z * (-1.388731625493765e-3 + z * 2.443315711809948e-5)
    )
    q = k.astype(jnp.int32)
    swap = (q & 1) == 1
    sin = jnp.where(swap, c, s)
    cos = jnp.where(swap, s, c)
    sin = jnp.where((q & 2) == 2, -sin, sin)
    cos = jnp.where(((q + 1) & 2) == 2, -cos, cos)
    return sin, cos


NAMES = (
    "m1",
    "m2",
    "along",
    "mask",
    "t3",
    "t18",
    "t50",
    "t51",
    "t160",
    "t161",
    "l7",
    "l15",
    "t9",
    "l10",
    "t12",
    "l13",
    "window",
    "freq",
    "flip",
    "place",
)


def maths_kernel(recv, *refs):
    tab = dict(zip(NAMES, refs[: len(NAMES)]))
    new_ref, obj_ref = refs[len(NAMES) : len(NAMES) + 2]
    ramp, ysc, foc, asc, dat, tra, gsc, hsc, pup = refs[len(NAMES) + 2 :]
    j = pl.program_id(0)
    which = lax.rem(j, 2)

    def half_spectra(values):
        asc[...] = right(values, tab["t9"][...])
        for f in range(0, FRAMES, 2):
            stacked = []
            for g in (f, f + 1):
                part = asc[g * N : (g + 1) * N, :]
                stacked.append(jnp.concatenate([part[:, :128], part[:, 128:]], axis=0))
            out = left(tab["l10"][...], jnp.concatenate(stacked, axis=1))
            yield f, out[:, :128]
            yield f + 1, out[:, 128:]

    @pl.when(j == 0)
    def _():
        for f in range(FRAMES):
            angle = (
                tab["freq"][0] * recv[0, f, 178:179, :] + tab["freq"][1] * recv[0, f, 179:180, :]
            )
            sin, cos = sincos(angle)
            ramp[f, 0] = cos
            ramp[f, 1] = sin

    energy = []
    window = tab["window"][...]
    parts = []
    lane = lax.broadcasted_iota(jnp.int32, (N, 128), 1)
    start = pl.multiple_of(which * N, 8)
    total = jnp.zeros((N, 128), f32)
    for f in range(FRAMES):
        part = jnp.where(lane < N, recv[0, f, pl.ds(start, N), :], 0.0) * window
        total = total + part * part
        parts.append(part)
    energy = jnp.sum(total) * float(N * N)
    for f, out in half_spectra(jnp.concatenate(parts, axis=0)):
        re, im = out[:48], out[48:]
        cos, sin = ramp[f, 0], ramp[f, 1]
        dat[f, :48] = re * cos - im * sin
        dat[f, 48:] = re * sin + im * cos
    rows = [recv[0, f, pl.ds(176 + which, 1), :] for f in range(FRAMES)]
    lane8 = lax.broadcasted_iota(jnp.int32, (FRAMES, 128), 1)
    current = jnp.where(lane8 < MODES, jnp.concatenate(rows, axis=0), 0.0)
    step = (STEP * FRAMES) / (jnp.zeros((FRAMES, 128), f32) + energy)

    def iterate(_, current):
        cab = fine(current, tab["m1"][...])
        along = tab["along"][...]
        phase = fine(jnp.concatenate([cab] * XP, axis=0) * along, tab["t3"][...])
        sin, cos = sincos(phase)
        mask = tab["mask"][...]
        pr, pi = cos * mask, sin * mask
        pup[0] = pr
        pup[1] = pi
        hi, lo = split(jnp.concatenate([pr, pi], axis=1))
        stack = jnp.concatenate([hi, lo, hi], axis=1)
        for h in range(2):
            out = dot(stack, tab[f"t5{h}"][...])
            ysc[h] = out[:, :128]
            ysc[2 + h] = out[:, 128:]
        spreads = []
        for f in range(0, FRAMES, 2):
            both = []
            for g in (f, f + 1):
                both.append(
                    jnp.concatenate([ysc[h, pl.ds(g, XP, FRAMES), :] for h in range(4)], axis=0)
                )
            out = left(tab["l7"][...], jnp.concatenate(both, axis=1))
            for g in (0, 1):
                one = out[:, 128 * g : 128 * g + 128]
                foc[f + g] = one
                spreads.append(one[:N] * one[:N] + one[N:] * one[N:])
        cre = jnp.zeros((48, 128), f32)
        cim = jnp.zeros((48, 128), f32)
        den = jnp.full((48, 128), DAMPING, f32)
        for f, out in half_spectra(jnp.concatenate(spreads, axis=0)):
            tra[f] = out
            tre, tim = out[:48], out[48:]
            dre, dim = dat[f, :48], dat[f, 48:]
            cre = cre + (dre * tre + dim * tim)
            cim = cim + (dim * tre - dre * tim)
            den = den + (tre * tre + tim * tim)
        ere, eim = cre / den, cim / den
        obj_ref[0, 0, :48] = ere
        obj_ref[0, 1, :48] = eim
        for f in range(FRAMES):
            tre, tim = tra[f, :48], tra[f, 48:]
            mre = dat[f, :48] - (ere * tre - eim * tim)
            mim = dat[f, 48:] - (ere * tim + eim * tre)
            gsc[f * 48 : f * 48 + 48, :128] = ere * mre + eim * mim
            gsc[f * 48 : f * 48 + 48, 128:] = ere * mim - eim * mre
        gsc[...] = right(gsc[...], tab["t12"][...])
        for f in range(0, FRAMES, 2):
            both = []
            for g in (f, f + 1):
                part = gsc[g * 48 : g * 48 + 48, :]
                both.append(jnp.concatenate([part[:, :128], part[:, 128:]], axis=0))
            grad = left(tab["l13"][...], jnp.concatenate(both, axis=1))[:N]
            both = []
            for g in (0, 1):
                one = grad[:, 128 * g : 128 * g + 128]
                both.append(
                    jnp.concatenate([one * foc[f + g, :N], one * foc[f + g, N:]], axis=0)
                )
            out = left(tab["l15"][...], jnp.concatenate(both, axis=1))
            for g in (0, 1):
                re, im = (out[k : k + 48, 128 * g : 128 * g + 128] for k in (0, 48))
                for h in range(2):
                    rows = slice(XP * h, XP * h + XP)
                    hsc[2 * h, pl.ds(f + g, XP, FRAMES), :] = re[rows]
                    hsc[2 * h + 1, pl.ds(f + g, XP, FRAMES), :] = im[rows]
        back = None
        for h in range(2):
            out = right(
                jnp.concatenate([hsc[2 * h], hsc[2 * h + 1]], axis=1), tab[f"t16{h}"][...]
            )
            back = out if back is None else back + out
        grad = back[:, 128:] * pup[0] - back[:, :128] * pup[1]
        gab = fine(grad, tab["t18"][...]) * tab["along"][...]
        acc = gab[:FRAMES]
        for i in range(1, XP):
            acc = acc + gab[i * FRAMES : (i + 1) * FRAMES]
        return current - step * fine(acc, tab["m2"][...])

    new_ref[0] = lax.fori_loop(0, ITERS, iterate, current)
    half = jnp.concatenate([obj_ref[0, 0, :48], obj_ref[0, 1, :48]], axis=0) * (1.0 / N)
    hi, lo = split(half)
    flipped = dot(jnp.concatenate([hi, lo], axis=1), tab["flip"][...])
    hi, lo = split(jnp.concatenate([half, flipped], axis=0))
    out = dot(tab["place"][...], jnp.concatenate([hi, lo], axis=0))
    obj_ref[0, 0] = out[:N]
    obj_ref[0, 1] = out[N:]


def maths(recv):
    consts = [jnp.asarray(tables()[name]) for name in NAMES]
    whole = [
        pl.BlockSpec(c.shape, functools.partial(lambda d, j: (0,) * d, c.ndim)) for c in consts
    ]
    return pl.pallas_call(
        maths_kernel,
        grid=(4,),
        in_specs=[pl.BlockSpec((1, FRAMES, ROWS, 128), lambda j: (j // 2, 0, 0, 0))] + whole,
        out_specs=[
            pl.BlockSpec((1, FRAMES, 128), lambda j: (j, 0, 0)),
            pl.BlockSpec((1, 2, N, 128), lambda j: (j, 0, 0, 0)),
        ],
        out_shape=[
            jax.ShapeDtypeStruct((4, FRAMES, 128), f32),
            jax.ShapeDtypeStruct((4, 2, N, 128), f32),
        ],
        scratch_shapes=[
            pltpu.VMEM((FRAMES, 2, 48, 128), f32),
            pltpu.VMEM((4, XP * FRAMES, 128), f32),
            pltpu.VMEM((FRAMES, 176, 128), f32),
            pltpu.VMEM((FRAMES * N, 256), f32),
            pltpu.VMEM((FRAMES, 96, 128), f32),
            pltpu.VMEM((FRAMES, 96, 128), f32),
            pltpu.VMEM((FRAMES * 48, 256), f32),
            pltpu.VMEM((4, XP * FRAMES, 128), f32),
            pltpu.VMEM((2, XP * FRAMES, 128), f32),
        ],
        compiler_params=pltpu.CompilerParams(vmem_limit_bytes=48 << 20),
        name="maths",
    )(recv, *consts)


def pair_counts(me_pat, me_frm):
    return lax.div(me_pat, 2) == me_frm


def exchange_kernel(
    frames,
    shifts,
    coefs,
    anchors,
    assign,
    recv,
    strip,
    send,
    load_sem,
    halo_send,
    halo_recv,
    send_sem,
    recv_sem,
    own_sem,
):
    me_frm, me_pat = lax.axis_index("frm"), lax.axis_index("pat")
    target = lax.div(me_pat, 2)
    side = lax.rem(me_pat, 2)
    own = pair_counts(me_pat, me_frm)

    def load(t):
        return pltpu.make_async_copy(
            frames.at[0, :, pl.ds(pl.multiple_of(t * 128, 128), 128)],
            strip.at[t, pl.ds(0, SH), :],
            load_sem.at[t],
        )

    def start_load(t, _):
        load(t).start()
        return 0

    lax.fori_loop(0, 16, start_load, 0)

    barrier = pltpu.get_barrier_semaphore()

    def greet(q, _):
        pat, frm = 2 * me_frm + lax.div(q, 8), lax.rem(q, 8)

        @pl.when(jnp.logical_not((pat == me_pat) & (frm == me_frm)))
        def _():
            pl.semaphore_signal(
                barrier, inc=1, device_id={"frm": frm, "pat": pat}, device_id_type=MESH
            )

        return 0

    lax.fori_loop(0, 16, greet, 0)

    @pl.when(me_pat < GROUPS - 1)
    def _():
        pl.semaphore_signal(
            barrier, inc=1, device_id={"frm": me_frm, "pat": me_pat + 1}, device_id_type=MESH
        )

    send[:, 176:, :] = jnp.zeros((GROUPS, 8, 128), f32)

    @pl.when(me_pat == GROUPS - 1)
    def _():
        strip[:, SH:, :] = jnp.zeros((16, N, 128), f32)

    def end_load(t, _):
        load(t).wait()
        return 0

    lax.fori_loop(0, 16, end_load, 0)
    pl.semaphore_wait(
        barrier, 16 - own.astype(jnp.int32) + (me_pat > 0).astype(jnp.int32)
    )

    def halo():
        return pltpu.make_async_remote_copy(
            src_ref=strip.at[:, pl.ds(0, N), :],
            dst_ref=strip.at[:, pl.ds(SH, N), :],
            send_sem=halo_send,
            recv_sem=halo_recv,
            device_id={"frm": me_frm, "pat": jnp.maximum(me_pat - 1, 0)},
            device_id_type=MESH,
        )

    @pl.when(me_pat > 0)
    def _():
        halo().start()

    @pl.when(me_pat < GROUPS - 1)
    def _():
        halo().wait_recv()

    lane = lax.broadcasted_iota(jnp.int32, (N, 128), 1)
    top = me_pat * SH

    def message(g):
        return pltpu.make_async_remote_copy(
            src_ref=send.at[g],
            dst_ref=recv.at[side, me_frm],
            send_sem=send_sem.at[g],
            recv_sem=recv_sem.at[side * 8 + me_frm],
            device_id={"frm": target, "pat": g},
            device_id_type=MESH,
        )

    def own_message():
        return pltpu.make_async_copy(send.at[me_pat], recv.at[side, me_frm], own_sem)

    def fill(i, _):
        g = lax.rem(me_pat + 1 + i, GROUPS)
        first = jnp.int32(0)
        second = jnp.int32(0)
        for p in range(PPS - 1, -1, -1):
            hit = assign[p] == g
            second = jnp.where(hit, first, second)
            first = jnp.where(hit, p, first)
        for k, p in enumerate((first, second)):
            row = jnp.clip(anchors[p, 0] - top, 0, SH - 1)
            col = anchors[p, 1]
            tile = jnp.clip(lax.shift_right_logical(col, 7), 0, 15)
            off = col & 127
            a = strip[tile, pl.ds(row, N), :]
            b = strip[jnp.minimum(tile + 1, 15), pl.ds(row, N), :]
            turn = (128 - off) & 127
            cut = jnp.where(
                lane < 128 - off, pltpu.roll(a, turn, 1), pltpu.roll(b, turn, 1)
            )
            send[g, k * N : k * N + N, :] = cut
            send[g, 176 + k : 177 + k, :MODES] = coefs[0, pl.ds(p, 1), :]
            send[g, 178 + k : 179 + k, :] = jnp.zeros((1, 128), f32) + shifts[0, k]
        me = own & (g == me_pat)

        @pl.when(jnp.logical_not(me))
        def _():
            message(g).start()

        @pl.when(me)
        def _():
            own_message().start()

        return 0

    lax.fori_loop(0, GROUPS, fill, 0)

    def finish(q, _):
        me = own & (q == me_pat)

        @pl.when(jnp.logical_not(me))
        def _():
            message(q).wait_send()

        @pl.when(me)
        def _():
            own_message().wait()

        pat, frm = 2 * me_frm + lax.div(q, 8), lax.rem(q, 8)

        @pl.when(jnp.logical_not((pat == me_pat) & (frm == me_frm)))
        def _():
            pltpu.make_async_remote_copy(
                src_ref=send.at[q],
                dst_ref=recv.at[lax.div(q, 8), frm],
                send_sem=send_sem.at[q],
                recv_sem=recv_sem.at[q],
                device_id={"frm": frm, "pat": pat},
                device_id_type=MESH,
            ).wait_recv()

        return 0

    lax.fori_loop(0, GROUPS, finish, 0)

    @pl.when(me_pat > 0)
    def _():
        halo().wait_send()


def exchange(frames, shifts, coefficients, anchors, assign):
    smem = pl.BlockSpec(memory_space=pltpu.SMEM)
    return pl.pallas_call(
        exchange_kernel,
        in_specs=[
            pl.BlockSpec(memory_space=pl.ANY),
            smem,
            pl.BlockSpec(memory_space=pltpu.VMEM),
            smem,
            smem,
        ],
        out_specs=pl.BlockSpec(memory_space=pl.ANY),
        out_shape=jax.ShapeDtypeStruct((2, FRAMES, ROWS, 128), f32),
        scratch_shapes=[
            pltpu.VMEM((16, SH + N, 128), f32),
            pltpu.VMEM((GROUPS, ROWS, 128), f32),
            pltpu.SemaphoreType.DMA((16,)),
            pltpu.SemaphoreType.DMA,
            pltpu.SemaphoreType.DMA,
            pltpu.SemaphoreType.DMA((GROUPS,)),
            pltpu.SemaphoreType.DMA((GROUPS,)),
            pltpu.SemaphoreType.DMA,
        ],
        compiler_params=pltpu.CompilerParams(
            collective_id=0, has_side_effects=True, vmem_limit_bytes=32 << 20
        ),
        name="exchange",
    )(frames, shifts, coefficients, anchors, assign)


def back_kernel(new, assign, out, send, recv, place, send_sem, recv_sem, own_sem):
    me_frm, me_pat = lax.axis_index("frm"), lax.axis_index("pat")
    target = lax.div(me_pat, 2)
    side = lax.rem(me_pat, 2)
    own = pair_counts(me_pat, me_frm)
    barrier = pltpu.get_barrier_semaphore()

    def greet(g, _):
        @pl.when(jnp.logical_not(own & (g == me_pat)))
        def _():
            pl.semaphore_signal(
                barrier, inc=1, device_id={"frm": target, "pat": g}, device_id_type=MESH
            )

        return 0

    lax.fori_loop(0, GROUPS, greet, 0)
    send[...] = jnp.zeros((16, 8, 128), f32)
    for k in range(2):
        for f in range(FRAMES):
            for i in range(2):
                send[k * 8 + f, i : i + 1, :] = new[2 * k + i, f : f + 1, :]
    pl.semaphore_wait(barrier, 16 - own.astype(jnp.int32))

    def message(q):
        return pltpu.make_async_remote_copy(
            src_ref=send.at[q],
            dst_ref=recv.at[me_pat],
            send_sem=send_sem.at[q],
            recv_sem=recv_sem.at[me_pat],
            device_id={"frm": lax.rem(q, 8), "pat": 2 * me_frm + lax.div(q, 8)},
            device_id_type=MESH,
        )

    here = side * 8 + me_frm

    def own_message():
        return pltpu.make_async_copy(send.at[here], recv.at[me_pat], own_sem)

    def start(q, _):
        me = own & (q == here)

        @pl.when(jnp.logical_not(me))
        def _():
            message(q).start()

        @pl.when(me)
        def _():
            own_message().start()

        return 0

    lax.fori_loop(0, 16, start, 0)

    def count(p, _):
        mine = assign[p]
        seen = jnp.int32(0)
        for q in range(PPS):
            seen = seen + jnp.where((assign[q] == mine) & (q < p), 1, 0)
        place[p] = jnp.clip(seen, 0, 1)
        return 0

    lax.fori_loop(0, PPS, count, 0)

    def finish(q, _):
        me = own & (q == here)

        @pl.when(jnp.logical_not(me))
        def _():
            message(q).wait_send()

        @pl.when(me)
        def _():
            own_message().wait()

        @pl.when(jnp.logical_not(own & (q == me_pat)))
        def _():
            pltpu.make_async_remote_copy(
                src_ref=send.at[q],
                dst_ref=recv.at[q],
                send_sem=send_sem.at[q],
                recv_sem=recv_sem.at[q],
                device_id={"frm": target, "pat": q},
                device_id_type=MESH,
            ).wait_recv()

        return 0

    lax.fori_loop(0, 16, finish, 0)
    for p in range(PPS):
        out[0, p : p + 1, :] = recv[assign[p], pl.ds(place[p], 1), :][:, :MODES]


def give_back(new, assign):
    return pl.pallas_call(
        back_kernel,
        in_specs=[
            pl.BlockSpec(memory_space=pltpu.VMEM),
            pl.BlockSpec(memory_space=pltpu.SMEM),
        ],
        out_specs=pl.BlockSpec(memory_space=pltpu.VMEM),
        out_shape=jax.ShapeDtypeStruct((1, PPS, MODES), f32),
        scratch_shapes=[
            pltpu.VMEM((16, 8, 128), f32),
            pltpu.VMEM((16, 8, 128), f32),
            pltpu.SMEM((PPS,), jnp.int32),
            pltpu.SemaphoreType.DMA((16,)),
            pltpu.SemaphoreType.DMA((16,)),
            pltpu.SemaphoreType.DMA,
        ],
        compiler_params=pltpu.CompilerParams(collective_id=1, has_side_effects=True),
        name="give_back",
    )(new, assign)


def shards(frames, shifts, coefficients, anchors, assign):
    recv = exchange(frames, shifts, coefficients, anchors, assign)
    new, spectra = maths(recv)
    coefs = give_back(new, assign)
    return coefs, spectra[:, :, :, :N].reshape(4, 2, N * N)


def solution(mesh):
    in_specs = (
        P("frm", "pat", None),
        P("frm", None),
        P("frm", "pat", None),
        P("pat", None),
        P("pat"),
    )
    out_specs = (P("frm", "pat", None), P(("pat", "frm"), None, None))
    return jax.shard_map(shards, mesh=mesh, in_specs=in_specs, out_specs=out_specs, check_vma=False)
```

```python
import functools
import math

import jax
import jax.numpy as jnp
import ml_dtypes
import numpy as np
from jax import lax
from jax.experimental import pallas as pl
from jax.experimental.pallas import tpu as pltpu
from jax.sharding import PartitionSpec as P

N = 88
MODES = 40
ITERS = 2
FRAMES = 8
SH = 128
PPS = 32
GROUPS = 16
LOW = 22
NX = 45
XP = 24
NU = 45
PER = 4
DAMPING = 0.05
STEP = 64.0
f32, bf16 = jnp.float32, jnp.bfloat16
MESH = pl.DeviceIdType.MESH


def noll_index(j):
    n = 0
    remaining = j - 1
    while remaining > n:
        n += 1
        remaining -= n
    m = (-1) ** j * (n % 2 + 2 * ((remaining + (n + 1) % 2) // 2))
    return (n, m)


def zernike_values(row, col):
    radius = np.sqrt(row * row + col * col)
    angle = np.arctan2(row, col)
    values = []
    for j in range(2, MODES + 2):
        n, m = noll_index(j)
        k_abs = abs(m)
        radial = np.zeros_like(radius)
        for k in range((n - k_abs) // 2 + 1):
            factor = (
                (-1) ** k
                * math.factorial(n - k)
                / (
                    math.factorial(k)
                    * math.factorial((n + k_abs) // 2 - k)
                    * math.factorial((n - k_abs) // 2 - k)
                )
            )
            radial = radial + factor * radius ** (n - 2 * k)
        if m == 0:
            values.append(math.sqrt(n + 1) * radial)
        elif m > 0:
            values.append(math.sqrt(2 * (n + 1)) * radial * np.cos(k_abs * angle))
        else:
            values.append(math.sqrt(2 * (n + 1)) * radial * np.sin(k_abs * angle))
    return np.stack(values)


def ultraspherical(order, t):
    t = np.asarray(t, np.float64)
    inside = (np.arange(NX) + LOW - 44.0) / 22.0

    def raw(x):
        last, value = np.zeros_like(x), np.ones_like(x)
        for n in range(1, order + 1):
            last, value = value, (2.0 * (n + 2.0) * x * value - (n + 4.0) * last) / n
        return value

    weight = np.sqrt(1.0 - inside**2)
    return raw(t) / np.sqrt(np.sum(weight * raw(inside) ** 2) / np.sum(weight))


PAIRS = [(a, b) for a in range(9) for b in range(9 - a)]


def halves(table):
    hi = table.astype(np.float32).astype(ml_dtypes.bfloat16)
    lo = (table - hi.astype(np.float64)).astype(np.float32).astype(ml_dtypes.bfloat16)
    return hi, lo


def right_table(table):
    hi, lo = halves(table)
    return np.concatenate([hi, hi, lo], axis=0)


def left_table(table):
    hi, lo = halves(table)
    return np.concatenate([hi, hi, lo], axis=1)


@functools.lru_cache
def tables():
    w = 2.0 * np.pi / N
    full = np.arange(N)
    px = LOW + np.arange(NX)
    unit = (px - 44.0) / 22.0
    aperture = (unit[:, None] ** 2 + unit[None, :] ** 2 <= 1.0).astype(np.float64)
    a32 = ((px.astype(np.float32) - np.float32(44)) / np.float32(22)).astype(np.float32)
    r32 = np.sqrt(a32[:, None] * a32[:, None] + a32[None, :] * a32[None, :])
    assert np.array_equal(aperture, (r32 <= 1.0).astype(np.float64))
    scale = 1.0 / (N * N * aperture.sum())
    root = math.sqrt(scale)

    grid = np.linspace(-1.0, 1.0, 31)
    rows, cols = (g.ravel() for g in np.meshgrid(grid, grid, indexing="ij"))
    basis = np.stack([ultraspherical(a, rows) * ultraspherical(b, cols) for a, b in PAIRS], axis=1)
    fit = np.linalg.lstsq(basis, zernike_values(rows, cols).T, rcond=None)[0].T

    out = {}
    spread_ab = np.zeros((MODES, 128))
    spread_ab[:, : len(PAIRS)] = fit
    spread_ab[:, 64 : 64 + len(PAIRS)] = fit
    m1 = np.zeros((128, 128))
    m1[:MODES] = spread_ab
    out["m1"] = fine_table(m1)
    out["m2"] = fine_table(m1.T)

    along = np.zeros((XP, 128))
    mask = np.zeros((XP, 128))
    t3 = np.zeros((128, 128))
    for h in range(2):
        for k, (a, b) in enumerate(PAIRS):
            for i in range(XP):
                if i + XP * h < NX:
                    along[i, 64 * h + k] = ultraspherical(a, unit[i + XP * h])
            t3[64 * h + k, 64 * h : 64 * h + NX] = ultraspherical(b, unit)
        for i in range(XP):
            if i + XP * h < NX:
                mask[i, 64 * h : 64 * h + NX] = aperture[i + XP * h]
    out["along"] = np.repeat(along, FRAMES, axis=0).astype(np.float32)
    out["mask"] = np.repeat(mask, FRAMES, axis=0).astype(np.float32)
    out["t3"] = fine_table(t3)
    out["t18"] = fine_table(t3.T)

    ang = w * (np.outer(px, full) % N)
    c, s = np.cos(ang), np.sin(ang)
    for h in range(2):
        t5 = np.zeros((256, 256))
        lanes = slice(64 * h, 64 * h + NX)
        lanes2 = slice(128 + 64 * h, 128 + 64 * h + NX)
        t5[lanes, :N], t5[lanes2, :N] = c, s
        t5[lanes, 128 : 128 + N], t5[lanes2, 128 : 128 + N] = -s, c
        out[f"t5{h}"] = right_table(t5)
        t16 = np.zeros((256, 256))
        t16[:N, lanes], t16[128 : 128 + N, lanes] = c.T, -s.T
        t16[:N, lanes2], t16[128 : 128 + N, lanes2] = s.T, c.T
        out[f"t16{h}"] = right_table(t16)
    l7 = np.zeros((176, 96))
    l7[:N, :NX], l7[:N, 48 : 48 + NX] = c.T, s.T
    l7[N:, :NX], l7[N:, 48 : 48 + NX] = -s.T, c.T
    out["l7"] = left_table(l7 * root)
    l15 = np.zeros((96, 176))
    l15[:NX, :N], l15[:NX, N:] = c, -s
    l15[48 : 48 + NX, :N], l15[48 : 48 + NX, N:] = s, c
    out["l15"] = left_table(l15)

    ang = w * (np.outer(full, full) % N)
    c, s = np.cos(ang), np.sin(ang)
    t9 = np.zeros((128, 256))
    t9[:N, :N], t9[:N, 128 : 128 + N] = c, -s
    out["t9"] = right_table(t9)
    l10 = np.zeros((96, 176))
    l10[:NU, :N], l10[:NU, N:] = c[:NU], s[:NU]
    l10[48 : 48 + NU, :N], l10[48 : 48 + NU, N:] = -s[:NU], c[:NU]
    out["l10"] = left_table(l10)
    t12 = np.zeros((256, 256))
    t12[:N, :N], t12[128 : 128 + N, :N] = c, -s
    t12[:N, 128 : 128 + N], t12[128 : 128 + N, 128 : 128 + N] = s, c
    out["t12"] = right_table(t12)
    weight = np.full((NU,), 2.0)
    weight[0] = weight[44] = 1.0
    weight = weight * (-2.0) * 2.0 * root
    l13 = np.zeros((96, 96))
    l13[:N, :NU], l13[:N, 48 : 48 + NU] = c[:, :NU] * weight, -s[:, :NU] * weight
    out["l13"] = left_table(l13)

    profile = 0.5 - 0.5 * np.cos(2.0 * np.pi * (full + 0.5) / N)
    window = np.zeros((N, 128), np.float32)
    window[:, :N] = profile[:, None] * profile[None, :]
    out["window"] = window
    signed = (full + 44) % N - 44.0
    freq = np.zeros((2, 48, 128), np.float32)
    freq[0, :NU, :] = signed[:NU, None]
    freq[1, :, :N] = signed[None, :]
    out["freq"] = (freq * (-w)).astype(np.float32)

    flip = np.zeros((128, 128), ml_dtypes.bfloat16)
    for v in range(N):
        flip[(N - v) % N, v] = 1
    out["flip"] = np.concatenate([flip, flip], axis=0)
    place = np.zeros((176, 192), ml_dtypes.bfloat16)
    for u in range(N):
        if u < NU:
            place[u, u] = 1
            place[N + u, 48 + u] = 1
        else:
            place[u, 96 + N - u] = 1
            place[N + u, 144 + N - u] = -1
    out["place"] = np.concatenate([place, place], axis=1)
    return out


def fine_table(table):
    hi = table.astype(np.float32).astype(ml_dtypes.bfloat16)
    rest = table - hi.astype(np.float64)
    mid = rest.astype(np.float32).astype(ml_dtypes.bfloat16)
    low = (rest - mid.astype(np.float64)).astype(np.float32).astype(ml_dtypes.bfloat16)
    return np.concatenate([hi, hi, mid, mid, low, hi], axis=0)


def split(x):
    hi = x.astype(bf16)
    return hi, (x - hi.astype(f32)).astype(bf16)


def dot(a, b):
    return jnp.dot(a, b, preferred_element_type=f32)


def right(x, table):
    hi, lo = split(x)
    return dot(jnp.concatenate([hi, lo, hi], axis=1), table)


def fine(x, table):
    hi = x.astype(bf16)
    rest = x - hi.astype(f32)
    mid = rest.astype(bf16)
    low = (rest - mid.astype(f32)).astype(bf16)
    return dot(jnp.concatenate([hi, mid, hi, mid, hi, low], axis=1), table)


def left(table, x):
    hi, lo = split(x)
    return dot(table, jnp.concatenate([hi, lo, hi], axis=0))


def sincos(x):
    k = jnp.floor(x * (2.0 / math.pi) + 0.5)
    r = x - k * 1.5703125
    r = r - k * 4.8351287841796875e-4
    r = r - k * 3.1385570764541626e-07
    z = r * r
    s = r + r * z * (-1.6666654611e-1 + z * (8.3321608736e-3 + z * -1.9515295891e-4))
    c = 1.0 - 0.5 * z + z * z * (
        4.166664568298827e-2 + z * (-1.388731625493765e-3 + z * 2.443315711809948e-5)
    )
    q = k.astype(jnp.int32)
    swap = (q & 1) == 1
    sin = jnp.where(swap, c, s)
    cos = jnp.where(swap, s, c)
    sin = jnp.where((q & 2) == 2, -sin, sin)
    cos = jnp.where(((q + 1) & 2) == 2, -cos, cos)
    return sin, cos


PACKS = {
    "narrow": ("m1", "m2", "t3", "t18", "flip"),
    "wide": ("t50", "t51", "t160", "t161", "t12", "t9"),
    "left96": ("l7", "l13"),
    "left176": ("l15", "l10"),
    "order": ("place",),
    "real": ("along", "mask", "window", "freq"),
}


@functools.lru_cache
def packed():
    arrays, where = [], {}
    for index, names in enumerate(PACKS.values()):
        rows = []
        for name in names:
            table = tables()[name]
            table = table.reshape(-1, table.shape[-1])
            where[name] = (index, sum(r.shape[0] for r in rows), table.shape[0])
            rows.append(table)
        arrays.append(np.concatenate(rows, axis=0))
    return arrays, where


def kernel(*refs):
    where = packed()[1]
    count = len(PACKS)
    frames, shifts_in, coefs_in, anchors_in, assign_in = refs[:5]
    packs_in = refs[5 : 5 + count]
    obj, out = refs[5 + count : 7 + count]
    packs = refs[7 + count : 7 + 2 * count]
    (
        shifts,
        coefs,
        anchors,
        assign,
        slots,
        strip,
        send,
        recv,
        csend,
        crecv,
        nsend,
        nrecv,
        esend,
        ramp,
        curs,
        pup,
        foc,
        tra,
        dat,
        ysc,
        asc,
        gsc,
        hsc,
        small_sem,
        pack_sem,
        load_sem,
        halo_send,
        halo_recv,
        msg_send,
        msg_recv,
        c_send,
        c_recv,
        n_send,
        n_recv,
        e_send,
        e_recv,
        e_own,
    ) = refs[7 + 2 * count :]

    def tab(name):
        index, start, rows = where[name]
        return packs[index][start : start + rows, :]

    me_frm, me_pat = lax.axis_index("frm"), lax.axis_index("pat")
    half, side = lax.div(me_pat, 2), lax.rem(me_pat, 2)
    loop = lax.fori_loop

    small = [
        pltpu.make_async_copy(a, b, small_sem.at[i])
        for i, (a, b) in enumerate(
            [(shifts_in, shifts), (coefs_in, coefs), (anchors_in, anchors), (assign_in, assign)]
        )
    ]
    for copy in small:
        copy.start()

    def load(t):
        return pltpu.make_async_copy(
            frames.at[0, :, pl.ds(pl.multiple_of(t * 128, 128), 128)],
            strip.at[t, pl.ds(0, SH), :],
            load_sem.at[t],
        )

    def start_load(t, _):
        load(t).start()
        return 0

    def end_load(t, _):
        load(t).wait()
        return 0

    loop(0, 16, start_load, 0)
    pack_loads = [
        pltpu.make_async_copy(packs_in[i], packs[i], pack_sem.at[i]) for i in range(count)
    ]
    for copy in pack_loads:
        copy.start()

    barrier = pltpu.get_barrier_semaphore()

    def tell(frm, pat):
        pl.semaphore_signal(
            barrier, inc=1, device_id={"frm": frm, "pat": pat}, device_id_type=MESH
        )

    def greet(q, _):
        @pl.when(q != me_frm)
        def _():
            tell(q, me_pat)

        return 0

    loop(0, FRAMES, greet, 0)

    @pl.when(me_pat < GROUPS - 1)
    def _():
        tell(me_frm, me_pat + 1)

    same = half == me_frm

    def greet_late(k, _):
        @pl.when(jnp.logical_not(same & (2 * me_frm + k == me_pat)))
        def _():
            tell(half, 2 * me_frm + k)

        return 0

    loop(0, 2, greet_late, 0)

    @pl.when(me_pat == GROUPS - 1)
    def _():
        strip[:, SH:, :] = jnp.zeros((16, N, 128), f32)

    loop(0, 16, end_load, 0)
    pl.semaphore_wait(
        barrier,
        FRAMES - 1 + (me_pat > 0).astype(jnp.int32) + 2 - same.astype(jnp.int32),
    )

    halo = pltpu.make_async_remote_copy(
        src_ref=strip.at[:, pl.ds(0, N), :],
        dst_ref=strip.at[:, pl.ds(SH, N), :],
        send_sem=halo_send,
        recv_sem=halo_recv,
        device_id={"frm": me_frm, "pat": jnp.maximum(me_pat - 1, 0)},
        device_id_type=MESH,
    )

    @pl.when(me_pat > 0)
    def _():
        halo.start()

    for copy in small:
        copy.wait()

    def order(g, _):
        first = jnp.int32(0)
        second = jnp.int32(0)
        for p in range(PPS - 1, -1, -1):
            hit = assign[p] == g
            second = jnp.where(hit, first, second)
            first = jnp.where(hit, p, first)
        slots[2 * g] = first
        slots[2 * g + 1] = second
        return 0

    loop(0, GROUPS, order, 0)

    def to_peer(source, target, send_sems, recv_sems, q):
        return pltpu.make_async_remote_copy(
            src_ref=source.at[q],
            dst_ref=target.at[me_frm],
            send_sem=send_sems.at[q],
            recv_sem=recv_sems.at[me_frm],
            device_id={"frm": q, "pat": me_pat},
            device_id_type=MESH,
        )

    def from_peer(source, target, send_sems, recv_sems, q):
        return pltpu.make_async_remote_copy(
            src_ref=source.at[q],
            dst_ref=target.at[q],
            send_sem=send_sems.at[q],
            recv_sem=recv_sems.at[q],
            device_id={"frm": q, "pat": me_pat},
            device_id_type=MESH,
        )

    csend[...] = jnp.zeros((FRAMES, 8, 128), f32)

    def send_coefs(i, _):
        q = lax.rem(me_frm + i, FRAMES)
        for j in range(PER):
            csend[q, j : j + 1, :MODES] = coefs[0, pl.ds(slots[PER * q + j], 1), :]
        for k in range(2):
            csend[q, PER + k : PER + k + 1, :] = jnp.zeros((1, 128), f32) + shifts[0, k]

        @pl.when(i > 0)
        def _():
            to_peer(csend, crecv, c_send, c_recv, q).start()

        @pl.when(i == 0)
        def _():
            crecv[me_frm] = csend[me_frm]

        return 0

    loop(0, FRAMES, send_coefs, 0)
    for copy in pack_loads:
        copy.wait()

    def take(source, target, send_sems, recv_sems):
        def one(i, _):
            q = lax.rem(me_frm + i, FRAMES)
            from_peer(source, target, send_sems, recv_sems, q).wait_recv()
            return 0

        loop(1, FRAMES, one, 0)

    def drain(source, target, send_sems, recv_sems):
        def one(i, _):
            q = lax.rem(me_frm + i, FRAMES)
            to_peer(source, target, send_sems, recv_sems, q).wait_send()
            return 0

        loop(1, FRAMES, one, 0)

    take(csend, crecv, c_send, c_recv)
    for j in range(PER):
        curs[j] = jnp.concatenate([crecv[f, j : j + 1, :] for f in range(FRAMES)], axis=0)
    freq = tab("freq")

    def make_ramp(f, _):
        angle = freq[:48] * crecv[f, PER : PER + 1, :] + freq[48:] * crecv[f, PER + 1 : PER + 2, :]
        sin, cos = sincos(angle)
        ramp[f, 0] = cos
        ramp[f, 1] = sin
        return 0

    loop(0, FRAMES, make_ramp, 0)

    def half_spectra(values):
        asc[...] = right(values, tab("t9"))
        for f in range(0, FRAMES, 2):
            stacked = []
            for g in (f, f + 1):
                part = asc[g * N : (g + 1) * N, :]
                stacked.append(jnp.concatenate([part[:, :128], part[:, 128:]], axis=0))
            both = left(tab("l10"), jnp.concatenate(stacked, axis=1))
            yield f, both[:, :128]
            yield f + 1, both[:, 128:]

    def forward(j):
        cab = fine(curs[j], tab("m1"))
        phase = fine(jnp.concatenate([cab] * XP, axis=0) * tab("along"), tab("t3"))
        sin, cos = sincos(phase)
        mask = tab("mask")
        pr, pi = cos * mask, sin * mask
        pup[j, 0] = pr
        pup[j, 1] = pi
        hi, lo = split(jnp.concatenate([pr, pi], axis=1))
        stack = jnp.concatenate([hi, lo, hi], axis=1)
        for h in range(2):
            both = dot(stack, tab(f"t5{h}"))
            ysc[h] = both[:, :128]
            ysc[2 + h] = both[:, 128:]
        spreads = []
        for f in range(0, FRAMES, 2):
            pair = []
            for g in (f, f + 1):
                pair.append(
                    jnp.concatenate([ysc[h, pl.ds(g, XP, FRAMES), :] for h in range(4)], axis=0)
                )
            both = left(tab("l7"), jnp.concatenate(pair, axis=1))
            for g in (0, 1):
                one = both[:, 128 * g : 128 * g + 128]
                foc[j, f + g] = one
                spreads.append(one[:N] * one[:N] + one[N:] * one[N:])
        for f, one in half_spectra(jnp.concatenate(spreads, axis=0)):
            tra[j, f] = one

    def backward(j, step):
        cre = jnp.zeros((48, 128), f32)
        cim = jnp.zeros((48, 128), f32)
        den = jnp.full((48, 128), DAMPING, f32)
        for f in range(FRAMES):
            tre, tim = tra[j, f, :48], tra[j, f, 48:]
            dre, dim = dat[f, :48], dat[f, 48:]
            cre = cre + (dre * tre + dim * tim)
            cim = cim + (dim * tre - dre * tim)
            den = den + (tre * tre + tim * tim)
        ere, eim = cre / den, cim / den
        esend[j, 0, :48] = ere
        esend[j, 1, :48] = eim
        for f in range(FRAMES):
            tre, tim = tra[j, f, :48], tra[j, f, 48:]
            mre = dat[f, :48] - (ere * tre - eim * tim)
            mim = dat[f, 48:] - (ere * tim + eim * tre)
            gsc[f * 48 : f * 48 + 48, :128] = ere * mre + eim * mim
            gsc[f * 48 : f * 48 + 48, 128:] = ere * mim - eim * mre
        gsc[...] = right(gsc[...], tab("t12"))
        for f in range(0, FRAMES, 2):
            pair = []
            for g in (f, f + 1):
                part = gsc[g * 48 : g * 48 + 48, :]
                pair.append(jnp.concatenate([part[:, :128], part[:, 128:]], axis=0))
            grad = left(tab("l13"), jnp.concatenate(pair, axis=1))[:N]
            pair = []
            for g in (0, 1):
                one = grad[:, 128 * g : 128 * g + 128]
                pair.append(
                    jnp.concatenate([one * foc[j, f + g, :N], one * foc[j, f + g, N:]], axis=0)
                )
            both = left(tab("l15"), jnp.concatenate(pair, axis=1))
            for g in (0, 1):
                re, im = (both[k : k + 48, 128 * g : 128 * g + 128] for k in (0, 48))
                for h in range(2):
                    rows = slice(XP * h, XP * h + XP)
                    hsc[2 * h, pl.ds(f + g, XP, FRAMES), :] = re[rows]
                    hsc[2 * h + 1, pl.ds(f + g, XP, FRAMES), :] = im[rows]
        back = None
        for h in range(2):
            one = right(jnp.concatenate([hsc[2 * h], hsc[2 * h + 1]], axis=1), tab(f"t16{h}"))
            back = one if back is None else back + one
        grad = back[:, 128:] * pup[j, 0] - back[:, :128] * pup[j, 1]
        gab = fine(grad, tab("t18")) * tab("along")
        acc = gab[:FRAMES]
        for i in range(1, XP):
            acc = acc + gab[i * FRAMES : (i + 1) * FRAMES]
        curs[j] = curs[j] - step * fine(acc, tab("m2"))

    def first_half(j, _):
        forward(j)
        return 0

    loop(0, EARLY, first_half, 0)

    @pl.when(me_pat < GROUPS - 1)
    def _():
        halo.wait_recv()

    lane = lax.broadcasted_iota(jnp.int32, (N, 128), 1)
    top = me_pat * SH

    def pixels(j, q):
        return pltpu.make_async_remote_copy(
            src_ref=send.at[j, q],
            dst_ref=recv.at[j, me_frm],
            send_sem=msg_send.at[j, q],
            recv_sem=msg_recv.at[j, me_frm],
            device_id={"frm": q, "pat": me_pat},
            device_id_type=MESH,
        )

    def pixels_from(j, q):
        return pltpu.make_async_remote_copy(
            src_ref=send.at[j, q],
            dst_ref=recv.at[j, q],
            send_sem=msg_send.at[j, q],
            recv_sem=msg_recv.at[j, q],
            device_id={"frm": q, "pat": me_pat},
            device_id_type=MESH,
        )

    def cut(n, _):
        j, q = lax.div(n, FRAMES), lax.rem(me_frm + 1 + lax.rem(n, FRAMES), FRAMES)
        p = slots[PER * q + j]
        row = jnp.clip(anchors[0, p] - top, 0, SH - 1)
        col = anchors[1, p]
        tile = jnp.clip(lax.shift_right_logical(col, 7), 0, 15)
        off = col & 127
        a = strip[tile, pl.ds(row, N), :]
        b = strip[jnp.minimum(tile + 1, 15), pl.ds(row, N), :]
        turn = (128 - off) & 127
        patch = jnp.where(lane < 128 - off, pltpu.roll(a, turn, 1), pltpu.roll(b, turn, 1))

        @pl.when(q != me_frm)
        def _():
            send[j, q] = patch
            pixels(j, q).start()

        @pl.when(q == me_frm)
        def _():
            recv[j, me_frm] = patch

        return 0

    loop(0, PER * FRAMES, cut, 0)
    loop(EARLY, PER, first_half, 0)

    def estimate(j):
        return pltpu.make_async_remote_copy(
            src_ref=esend.at[j],
            dst_ref=obj.at[2 * side + lax.rem(j, 2)],
            send_sem=e_send.at[j],
            recv_sem=e_recv.at[2 * side + lax.rem(j, 2)],
            device_id={"frm": half, "pat": 2 * me_frm + lax.div(j, 2)},
            device_id_type=MESH,
        )

    def estimate_here(j):
        return pltpu.make_async_copy(
            esend.at[j], obj.at[2 * side + lax.rem(j, 2)], e_own.at[j]
        )

    def estimate_stays(j):
        return same & (2 * me_frm + lax.div(j, 2) == me_pat)

    def work(j, _):
        def arrived(i, _):
            pixels_from(j, lax.rem(me_frm + i, FRAMES)).wait_recv()
            return 0

        loop(1, FRAMES, arrived, 0)
        window = tab("window")
        parts = []
        total = jnp.zeros((N, 128), f32)
        for f in range(FRAMES):
            part = jnp.where(lane < N, recv[j, f], 0.0) * window
            total = total + part * part
            parts.append(part)
        energy = jnp.sum(total) * float(N * N)
        for f, one in half_spectra(jnp.concatenate(parts, axis=0)):
            re, im = one[:48], one[48:]
            cos, sin = ramp[f, 0], ramp[f, 1]
            dat[f, :48] = re * cos - im * sin
            dat[f, 48:] = re * sin + im * cos
        step = (STEP * FRAMES) / (jnp.zeros((FRAMES, 128), f32) + energy)

        def iterate(t, _):
            backward(j, step)

            @pl.when(t < ITERS - 1)
            def _():
                forward(j)

            return 0

        loop(0, ITERS, iterate, 0)
        spectrum = jnp.concatenate([esend[j, 0, :48], esend[j, 1, :48]], axis=0) * (1.0 / N)
        hi, lo = split(spectrum)
        flipped = dot(jnp.concatenate([hi, lo], axis=1), tab("flip"))
        hi, lo = split(jnp.concatenate([spectrum, flipped], axis=0))
        whole = dot(tab("place"), jnp.concatenate([hi, lo], axis=0))
        esend[j, 0] = whole[:N]
        esend[j, 1] = whole[N:]

        @pl.when(jnp.logical_not(estimate_stays(j)))
        def _():
            estimate(j).start()

        @pl.when(estimate_stays(j))
        def _():
            estimate_here(j).start()

        for f in range(FRAMES):
            nsend[f, pl.ds(j, 1), :] = curs[j, f : f + 1, :]
        return 0

    nsend[...] = jnp.zeros((FRAMES, 8, 128), f32)
    loop(0, PER, work, 0)

    def give(i, _):
        q = lax.rem(me_frm + i, FRAMES)
        to_peer(nsend, nrecv, n_send, n_recv, q).start()
        return 0

    loop(1, FRAMES, give, 0)
    nrecv[me_frm] = nsend[me_frm]

    def end_estimate(j, _):
        stays = estimate_stays(j)

        @pl.when(jnp.logical_not(stays))
        def _():
            estimate(j).wait_send()

        @pl.when(stays)
        def _():
            estimate_here(j).wait()

        return 0

    def end_pixels(n, _):
        j, q = lax.div(n, FRAMES), lax.rem(n, FRAMES)

        @pl.when(q != me_frm)
        def _():
            pixels(j, q).wait_send()

        return 0

    loop(0, PER * FRAMES, end_pixels, 0)
    drain(csend, crecv, c_send, c_recv)

    @pl.when(me_pat > 0)
    def _():
        halo.wait_send()

    take(nsend, nrecv, n_send, n_recv)

    out[...] = jnp.zeros((PPS, 128), f32)
    lane1 = lax.broadcasted_iota(jnp.int32, (PPS, 1), 0)

    def place_back(n, _):
        row = nrecv[lax.div(n, PER), pl.ds(lax.rem(n, PER), 1), :]
        out[...] = jnp.where(lane1 == slots[n], row, out[...])
        return 0

    loop(0, PPS, place_back, 0)
    loop(0, PER, end_estimate, 0)
    drain(nsend, nrecv, n_send, n_recv)

    def estimate_from(k, _):
        source = 2 * me_frm + lax.div(k, 2)

        @pl.when(jnp.logical_not(same & (source == me_pat)))
        def _():
            pltpu.make_async_remote_copy(
                src_ref=esend.at[k],
                dst_ref=obj.at[k],
                send_sem=e_send.at[k],
                recv_sem=e_recv.at[k],
                device_id={"frm": half, "pat": source},
                device_id_type=MESH,
            ).wait_recv()

        return 0

    loop(0, 4, estimate_from, 0)


EARLY = 3


def shards(frames, shifts, coefficients, anchors, assign):
    arrays = packed()[0]
    hbm = pl.BlockSpec(memory_space=pltpu.HBM)
    sems = pltpu.SemaphoreType.DMA
    obj, new = pl.pallas_call(
        kernel,
        in_specs=[hbm] * (5 + len(arrays)),
        out_specs=[hbm, pl.BlockSpec(memory_space=pltpu.VMEM)],
        out_shape=[
            jax.ShapeDtypeStruct((PER, 2, N, 128), f32),
            jax.ShapeDtypeStruct((PPS, 128), f32),
        ],
        scratch_shapes=[pltpu.VMEM(a.shape, a.dtype) for a in arrays]
        + [
            pltpu.SMEM((1, 2), f32),
            pltpu.VMEM((1, PPS, MODES), f32),
            pltpu.SMEM((2, PPS), jnp.int32),
            pltpu.SMEM((PPS,), jnp.int32),
            pltpu.SMEM((PPS,), jnp.int32),
            pltpu.VMEM((16, SH + N, 128), f32),
            pltpu.VMEM((PER, FRAMES, N, 128), f32),
            pltpu.VMEM((PER, FRAMES, N, 128), f32),
            pltpu.VMEM((FRAMES, 8, 128), f32),
            pltpu.VMEM((FRAMES, 8, 128), f32),
            pltpu.VMEM((FRAMES, 8, 128), f32),
            pltpu.VMEM((FRAMES, 8, 128), f32),
            pltpu.VMEM((PER, 2, N, 128), f32),
            pltpu.VMEM((FRAMES, 2, 48, 128), f32),
            pltpu.VMEM((PER, FRAMES, 128), f32),
            pltpu.VMEM((PER, 2, XP * FRAMES, 128), f32),
            pltpu.VMEM((PER, FRAMES, 176, 128), f32),
            pltpu.VMEM((PER, FRAMES, 96, 128), f32),
            pltpu.VMEM((FRAMES, 96, 128), f32),
            pltpu.VMEM((4, XP * FRAMES, 128), f32),
            pltpu.VMEM((FRAMES * N, 256), f32),
            pltpu.VMEM((FRAMES * 48, 256), f32),
            pltpu.VMEM((4, XP * FRAMES, 128), f32),
            sems((4,)),
            sems((len(arrays),)),
            sems((16,)),
            sems,
            sems,
            sems((PER, FRAMES)),
            sems((PER, FRAMES)),
            sems((FRAMES,)),
            sems((FRAMES,)),
            sems((FRAMES,)),
            sems((FRAMES,)),
            sems((PER,)),
            sems((PER,)),
            sems((PER,)),
        ],
        compiler_params=pltpu.CompilerParams(
            collective_id=0, has_side_effects=True, vmem_limit_bytes=56 << 20
        ),
        name="deconvolve",
    )(frames, shifts, coefficients, anchors.T, assign, *[jnp.asarray(a) for a in arrays])
    return new[None, :, :MODES], obj[:, :, :, :N].reshape(PER, 2, N * N)


def solution(mesh):
    in_specs = (
        P("frm", "pat", None),
        P("frm", None),
        P("frm", "pat", None),
        P("pat", None),
        P("pat"),
    )
    out_specs = (P("frm", "pat", None), P(("pat", "frm"), None, None))
    return jax.shard_map(shards, mesh=mesh, in_specs=in_specs, out_specs=out_specs, check_vma=False)
```

```python
import functools
import math

import jax
import jax.numpy as jnp
import ml_dtypes
import numpy as np
from jax import lax
from jax.experimental import pallas as pl
from jax.experimental.pallas import tpu as pltpu
from jax.sharding import PartitionSpec as P

N = 88
MODES = 40
ITERS = 2
FRAMES = 8
SH = 128
PPS = 32
GROUPS = 16
LOW = 22
NX = 45
XP = 24
NU = 45
PER = 4
DAMPING = 0.05
STEP = 64.0
f32, bf16 = jnp.float32, jnp.bfloat16
MESH = pl.DeviceIdType.MESH


def noll_index(j):
    n = 0
    remaining = j - 1
    while remaining > n:
        n += 1
        remaining -= n
    m = (-1) ** j * (n % 2 + 2 * ((remaining + (n + 1) % 2) // 2))
    return (n, m)


def zernike_values(row, col):
    radius = np.sqrt(row * row + col * col)
    angle = np.arctan2(row, col)
    values = []
    for j in range(2, MODES + 2):
        n, m = noll_index(j)
        k_abs = abs(m)
        radial = np.zeros_like(radius)
        for k in range((n - k_abs) // 2 + 1):
            factor = (
                (-1) ** k
                * math.factorial(n - k)
                / (
                    math.factorial(k)
                    * math.factorial((n + k_abs) // 2 - k)
                    * math.factorial((n - k_abs) // 2 - k)
                )
            )
            radial = radial + factor * radius ** (n - 2 * k)
        if m == 0:
            values.append(math.sqrt(n + 1) * radial)
        elif m > 0:
            values.append(math.sqrt(2 * (n + 1)) * radial * np.cos(k_abs * angle))
        else:
            values.append(math.sqrt(2 * (n + 1)) * radial * np.sin(k_abs * angle))
    return np.stack(values)


def ultraspherical(order, t):
    t = np.asarray(t, np.float64)
    inside = (np.arange(NX) + LOW - 44.0) / 22.0

    def raw(x):
        last, value = np.zeros_like(x), np.ones_like(x)
        for n in range(1, order + 1):
            last, value = value, (2.0 * (n + 2.0) * x * value - (n + 4.0) * last) / n
        return value

    weight = np.sqrt(1.0 - inside**2)
    return raw(t) / np.sqrt(np.sum(weight * raw(inside) ** 2) / np.sum(weight))


PAIRS = [(a, b) for a in range(9) for b in range(9 - a)]


def halves(table):
    hi = table.astype(np.float32).astype(ml_dtypes.bfloat16)
    lo = (table - hi.astype(np.float64)).astype(np.float32).astype(ml_dtypes.bfloat16)
    return hi, lo


def right_table(table):
    hi, lo = halves(table)
    return np.concatenate([hi, hi, lo], axis=0)


def left_table(table):
    hi, lo = halves(table)
    return np.concatenate([hi, hi, lo], axis=1)


@functools.lru_cache
def tables():
    w = 2.0 * np.pi / N
    full = np.arange(N)
    px = LOW + np.arange(NX)
    unit = (px - 44.0) / 22.0
    aperture = (unit[:, None] ** 2 + unit[None, :] ** 2 <= 1.0).astype(np.float64)
    a32 = ((px.astype(np.float32) - np.float32(44)) / np.float32(22)).astype(np.float32)
    r32 = np.sqrt(a32[:, None] * a32[:, None] + a32[None, :] * a32[None, :])
    assert np.array_equal(aperture, (r32 <= 1.0).astype(np.float64))
    scale = 1.0 / (N * N * aperture.sum())
    root = math.sqrt(scale)

    grid = np.linspace(-1.0, 1.0, 31)
    rows, cols = (g.ravel() for g in np.meshgrid(grid, grid, indexing="ij"))
    basis = np.stack([ultraspherical(a, rows) * ultraspherical(b, cols) for a, b in PAIRS], axis=1)
    fit = np.linalg.lstsq(basis, zernike_values(rows, cols).T, rcond=None)[0].T

    out = {}
    spread_ab = np.zeros((MODES, 128))
    spread_ab[:, : len(PAIRS)] = fit
    spread_ab[:, 64 : 64 + len(PAIRS)] = fit
    m1 = np.zeros((128, 128))
    m1[:MODES] = spread_ab
    out["m1"] = fine_table(m1)
    out["m2"] = fine_table(m1.T)

    along = np.zeros((XP, 128))
    mask = np.zeros((XP, 128))
    t3 = np.zeros((128, 128))
    for h in range(2):
        for k, (a, b) in enumerate(PAIRS):
            for i in range(XP):
                if i + XP * h < NX:
                    along[i, 64 * h + k] = ultraspherical(a, unit[i + XP * h])
            t3[64 * h + k, 64 * h : 64 * h + NX] = ultraspherical(b, unit)
        for i in range(XP):
            if i + XP * h < NX:
                mask[i, 64 * h : 64 * h + NX] = aperture[i + XP * h]
    out["along"] = np.repeat(along, FRAMES, axis=0).astype(np.float32)
    out["mask"] = np.repeat(mask, FRAMES, axis=0).astype(np.float32)
    out["t3"] = fine_table(t3)
    out["t18"] = fine_table(t3.T)

    ang = w * (np.outer(px, full) % N)
    c, s = np.cos(ang), np.sin(ang)
    for h in range(2):
        t5 = np.zeros((256, 256))
        lanes = slice(64 * h, 64 * h + NX)
        lanes2 = slice(128 + 64 * h, 128 + 64 * h + NX)
        t5[lanes, :N], t5[lanes2, :N] = c, s
        t5[lanes, 128 : 128 + N], t5[lanes2, 128 : 128 + N] = -s, c
        out[f"t5{h}"] = right_table(t5)
        t16 = np.zeros((256, 256))
        t16[:N, lanes], t16[128 : 128 + N, lanes] = c.T, -s.T
        t16[:N, lanes2], t16[128 : 128 + N, lanes2] = s.T, c.T
        out[f"t16{h}"] = right_table(t16)
    l7 = np.zeros((176, 96))
    l7[:N, :NX], l7[:N, 48 : 48 + NX] = c.T, s.T
    l7[N:, :NX], l7[N:, 48 : 48 + NX] = -s.T, c.T
    out["l7"] = left_table(l7 * root)
    l15 = np.zeros((96, 176))
    l15[:NX, :N], l15[:NX, N:] = c, -s
    l15[48 : 48 + NX, :N], l15[48 : 48 + NX, N:] = s, c
    out["l15"] = left_table(l15)

    ang = w * (np.outer(full, full) % N)
    c, s = np.cos(ang), np.sin(ang)
    t9 = np.zeros((128, 256))
    t9[:N, :N], t9[:N, 128 : 128 + N] = c, -s
    out["t9"] = right_table(t9)
    l10 = np.zeros((96, 176))
    l10[:NU, :N], l10[:NU, N:] = c[:NU], s[:NU]
    l10[48 : 48 + NU, :N], l10[48 : 48 + NU, N:] = -s[:NU], c[:NU]
    out["l10"] = left_table(l10)
    t12 = np.zeros((256, 256))
    t12[:N, :N], t12[128 : 128 + N, :N] = c, -s
    t12[:N, 128 : 128 + N], t12[128 : 128 + N, 128 : 128 + N] = s, c
    out["t12"] = right_table(t12)
    weight = np.full((NU,), 2.0)
    weight[0] = weight[44] = 1.0
    weight = weight * (-2.0) * 2.0 * root
    l13 = np.zeros((96, 96))
    l13[:N, :NU], l13[:N, 48 : 48 + NU] = c[:, :NU] * weight, -s[:, :NU] * weight
    out["l13"] = left_table(l13)

    profile = 0.5 - 0.5 * np.cos(2.0 * np.pi * (full + 0.5) / N)
    window = np.zeros((N, 128), np.float32)
    window[:, :N] = profile[:, None] * profile[None, :]
    out["window"] = window
    signed = (full + 44) % N - 44.0
    freq = np.zeros((2, 48, 128), np.float32)
    freq[0, :NU, :] = signed[:NU, None]
    freq[1, :, :N] = signed[None, :]
    out["freq"] = (freq * (-w)).astype(np.float32)

    flip = np.zeros((128, 128), ml_dtypes.bfloat16)
    for v in range(N):
        flip[(N - v) % N, v] = 1
    out["flip"] = np.concatenate([flip, flip], axis=0)
    place = np.zeros((176, 192), ml_dtypes.bfloat16)
    for u in range(N):
        if u < NU:
            place[u, u] = 1
            place[N + u, 48 + u] = 1
        else:
            place[u, 96 + N - u] = 1
            place[N + u, 144 + N - u] = -1
    out["place"] = np.concatenate([place, place], axis=1)
    return out


def fine_table(table):
    hi = table.astype(np.float32).astype(ml_dtypes.bfloat16)
    rest = table - hi.astype(np.float64)
    mid = rest.astype(np.float32).astype(ml_dtypes.bfloat16)
    low = (rest - mid.astype(np.float64)).astype(np.float32).astype(ml_dtypes.bfloat16)
    return np.concatenate([hi, hi, mid, mid, low, hi], axis=0)


def split(x):
    hi = x.astype(bf16)
    return hi, (x - hi.astype(f32)).astype(bf16)


def dot(a, b):
    return jnp.dot(a, b, preferred_element_type=f32)


def right(x, table):
    hi, lo = split(x)
    return dot(jnp.concatenate([hi, lo, hi], axis=1), table)


def fine(x, table):
    hi = x.astype(bf16)
    rest = x - hi.astype(f32)
    mid = rest.astype(bf16)
    low = (rest - mid.astype(f32)).astype(bf16)
    return dot(jnp.concatenate([hi, mid, hi, mid, hi, low], axis=1), table)


def left(table, x):
    hi, lo = split(x)
    return dot(table, jnp.concatenate([hi, lo, hi], axis=0))


def sincos(x):
    k = jnp.floor(x * (2.0 / math.pi) + 0.5)
    r = x - k * 1.5703125
    r = r - k * 4.8351287841796875e-4
    r = r - k * 3.1385570764541626e-07
    z = r * r
    s = r + r * z * (-1.6666654611e-1 + z * (8.3321608736e-3 + z * -1.9515295891e-4))
    c = 1.0 - 0.5 * z + z * z * (
        4.166664568298827e-2 + z * (-1.388731625493765e-3 + z * 2.443315711809948e-5)
    )
    q = k.astype(jnp.int32)
    swap = (q & 1) == 1
    sin = jnp.where(swap, c, s)
    cos = jnp.where(swap, s, c)
    sin = jnp.where((q & 2) == 2, -sin, sin)
    cos = jnp.where(((q + 1) & 2) == 2, -cos, cos)
    return sin, cos


PACKS = {
    "narrow": ("m1", "m2", "t3", "t18", "flip"),
    "wide": ("t50", "t51", "t160", "t161", "t12", "t9"),
    "left96": ("l7", "l13"),
    "left176": ("l15", "l10"),
    "order": ("place",),
    "real": ("along", "mask", "window", "freq"),
}


@functools.lru_cache
def packed():
    arrays, where = [], {}
    for index, names in enumerate(PACKS.values()):
        rows = []
        for name in names:
            table = tables()[name]
            table = table.reshape(-1, table.shape[-1])
            where[name] = (index, sum(r.shape[0] for r in rows), table.shape[0])
            rows.append(table)
        arrays.append(np.concatenate(rows, axis=0))
    return arrays, where


def kernel(*refs):
    where = packed()[1]
    count = len(PACKS)
    frames, shifts_in, coefs_in, anchors_in, assign_in = refs[:5]
    packs_in = refs[5 : 5 + count]
    obj, out = refs[5 + count : 7 + count]
    packs = refs[7 + count : 7 + 2 * count]
    (
        shifts,
        coefs,
        anchors,
        assign,
        slots,
        strip,
        send,
        recv,
        csend,
        crecv,
        nsend,
        nrecv,
        esend,
        ramp,
        curs,
        pup,
        foc,
        tra,
        dat,
        ysc,
        asc,
        gsc,
        hsc,
        small_sem,
        pack_sem,
        load_sem,
        halo_send,
        halo_recv,
        msg_send,
        msg_recv,
        c_send,
        c_recv,
        n_send,
        n_recv,
        e_send,
        e_recv,
        e_own,
    ) = refs[7 + 2 * count :]

    def tab(name):
        index, start, rows = where[name]
        return packs[index][start : start + rows, :]

    me_frm, me_pat = lax.axis_index("frm"), lax.axis_index("pat")
    half, side = lax.div(me_pat, 2), lax.rem(me_pat, 2)
    loop = lax.fori_loop

    small = [
        pltpu.make_async_copy(a, b, small_sem.at[i])
        for i, (a, b) in enumerate(
            [(shifts_in, shifts), (coefs_in, coefs), (anchors_in, anchors), (assign_in, assign)]
        )
    ]
    for copy in small:
        copy.start()

    def load(t):
        return pltpu.make_async_copy(
            frames.at[0, :, pl.ds(pl.multiple_of(t * 128, 128), 128)],
            strip.at[t, pl.ds(0, SH), :],
            load_sem.at[t],
        )

    def start_load(t, _):
        load(t).start()
        return 0

    def end_load(t, _):
        load(t).wait()
        return 0

    loop(0, 16, start_load, 0)
    pack_loads = [
        pltpu.make_async_copy(packs_in[i], packs[i], pack_sem.at[i]) for i in range(count)
    ]
    for copy in pack_loads:
        copy.start()

    barrier = pltpu.get_barrier_semaphore()

    def tell(frm, pat):
        pl.semaphore_signal(
            barrier, inc=1, device_id={"frm": frm, "pat": pat}, device_id_type=MESH
        )

    def greet(q, _):
        @pl.when(q != me_frm)
        def _():
            tell(q, me_pat)

        return 0

    loop(0, FRAMES, greet, 0)

    @pl.when(me_pat < GROUPS - 1)
    def _():
        tell(me_frm, me_pat + 1)

    same = half == me_frm

    def greet_late(k, _):
        @pl.when(jnp.logical_not(same & (2 * me_frm + k == me_pat)))
        def _():
            tell(half, 2 * me_frm + k)

        return 0

    loop(0, 2, greet_late, 0)

    for copy in small:
        copy.wait()

    def order(g, _):
        first = jnp.int32(0)
        second = jnp.int32(0)
        for p in range(PPS - 1, -1, -1):
            hit = assign[p] == g
            second = jnp.where(hit, first, second)
            first = jnp.where(hit, p, first)
        slots[2 * g] = first
        slots[2 * g + 1] = second
        return 0

    loop(0, GROUPS, order, 0)

    def to_peer(source, target, send_sems, recv_sems, q):
        return pltpu.make_async_remote_copy(
            src_ref=source.at[q],
            dst_ref=target.at[me_frm],
            send_sem=send_sems.at[q],
            recv_sem=recv_sems.at[me_frm],
            device_id={"frm": q, "pat": me_pat},
            device_id_type=MESH,
        )

    def from_peer(source, target, send_sems, recv_sems, q):
        return pltpu.make_async_remote_copy(
            src_ref=source.at[q],
            dst_ref=target.at[q],
            send_sem=send_sems.at[q],
            recv_sem=recv_sems.at[q],
            device_id={"frm": q, "pat": me_pat},
            device_id_type=MESH,
        )

    csend[...] = jnp.zeros((FRAMES, 8, 128), f32)

    def fill_coefs(q, _):
        for j in range(PER):
            csend[q, j : j + 1, :MODES] = coefs[0, pl.ds(slots[PER * q + j], 1), :]
        for k in range(2):
            csend[q, PER + k : PER + k + 1, :] = jnp.zeros((1, 128), f32) + shifts[0, k]
        return 0

    loop(0, FRAMES, fill_coefs, 0)
    crecv[me_frm] = csend[me_frm]

    @pl.when(me_pat == GROUPS - 1)
    def _():
        strip[:, SH:, :] = jnp.zeros((16, N, 128), f32)

    loop(0, 16, end_load, 0)
    pl.semaphore_wait(
        barrier,
        FRAMES - 1 + (me_pat > 0).astype(jnp.int32) + 2 - same.astype(jnp.int32),
    )

    def send_coefs(i, _):
        to_peer(csend, crecv, c_send, c_recv, lax.rem(me_frm + i, FRAMES)).start()
        return 0

    loop(1, FRAMES, send_coefs, 0)

    halo = pltpu.make_async_remote_copy(
        src_ref=strip.at[:, pl.ds(0, N), :],
        dst_ref=strip.at[:, pl.ds(SH, N), :],
        send_sem=halo_send,
        recv_sem=halo_recv,
        device_id={"frm": me_frm, "pat": jnp.maximum(me_pat - 1, 0)},
        device_id_type=MESH,
    )

    @pl.when(me_pat > 0)
    def _():
        halo.start()

    for copy in pack_loads:
        copy.wait()

    def take(source, target, send_sems, recv_sems):
        def one(i, _):
            q = lax.rem(me_frm + i, FRAMES)
            from_peer(source, target, send_sems, recv_sems, q).wait_recv()
            return 0

        loop(1, FRAMES, one, 0)

    def drain(source, target, send_sems, recv_sems):
        def one(i, _):
            q = lax.rem(me_frm + i, FRAMES)
            to_peer(source, target, send_sems, recv_sems, q).wait_send()
            return 0

        loop(1, FRAMES, one, 0)

    take(csend, crecv, c_send, c_recv)
    for j in range(PER):
        curs[j] = jnp.concatenate([crecv[f, j : j + 1, :] for f in range(FRAMES)], axis=0)
    freq = tab("freq")

    def make_ramp(f, _):
        angle = freq[:48] * crecv[f, PER : PER + 1, :] + freq[48:] * crecv[f, PER + 1 : PER + 2, :]
        sin, cos = sincos(angle)
        ramp[f, 0] = cos
        ramp[f, 1] = sin
        return 0

    loop(0, FRAMES, make_ramp, 0)

    def half_spectra(values):
        asc[...] = right(values, tab("t9"))
        for f in range(0, FRAMES, 2):
            stacked = []
            for g in (f, f + 1):
                part = asc[g * N : (g + 1) * N, :]
                stacked.append(jnp.concatenate([part[:, :128], part[:, 128:]], axis=0))
            both = left(tab("l10"), jnp.concatenate(stacked, axis=1))
            yield f, both[:, :128]
            yield f + 1, both[:, 128:]

    def forward(j):
        cab = fine(curs[j], tab("m1"))
        phase = fine(jnp.concatenate([cab] * XP, axis=0) * tab("along"), tab("t3"))
        sin, cos = sincos(phase)
        mask = tab("mask")
        pr, pi = cos * mask, sin * mask
        pup[j, 0] = pr
        pup[j, 1] = pi
        hi, lo = split(jnp.concatenate([pr, pi], axis=1))
        stack = jnp.concatenate([hi, lo, hi], axis=1)
        for h in range(2):
            both = dot(stack, tab(f"t5{h}"))
            ysc[h] = both[:, :128]
            ysc[2 + h] = both[:, 128:]
        spreads = []
        for f in range(0, FRAMES, 2):
            pair = []
            for g in (f, f + 1):
                pair.append(
                    jnp.concatenate([ysc[h, pl.ds(g, XP, FRAMES), :] for h in range(4)], axis=0)
                )
            both = left(tab("l7"), jnp.concatenate(pair, axis=1))
            for g in (0, 1):
                one = both[:, 128 * g : 128 * g + 128]
                foc[j, f + g] = one
                spreads.append(one[:N] * one[:N] + one[N:] * one[N:])
        for f, one in half_spectra(jnp.concatenate(spreads, axis=0)):
            tra[j, f] = one

    def estimate(j):
        return pltpu.make_async_remote_copy(
            src_ref=esend.at[j],
            dst_ref=obj.at[2 * side + lax.rem(j, 2)],
            send_sem=e_send.at[j],
            recv_sem=e_recv.at[2 * side + lax.rem(j, 2)],
            device_id={"frm": half, "pat": 2 * me_frm + lax.div(j, 2)},
            device_id_type=MESH,
        )

    def estimate_here(j):
        return pltpu.make_async_copy(
            esend.at[j], obj.at[2 * side + lax.rem(j, 2)], e_own.at[j]
        )

    def estimate_stays(j):
        return same & (2 * me_frm + lax.div(j, 2) == me_pat)

    def send_estimate(j, ere, eim):
        spectrum = jnp.concatenate([ere, eim], axis=0) * (1.0 / N)
        hi, lo = split(spectrum)
        flipped = dot(jnp.concatenate([hi, lo], axis=1), tab("flip"))
        hi, lo = split(jnp.concatenate([spectrum, flipped], axis=0))
        whole = dot(tab("place"), jnp.concatenate([hi, lo], axis=0))
        esend[j, 0] = whole[:N]
        esend[j, 1] = whole[N:]

        @pl.when(jnp.logical_not(estimate_stays(j)))
        def _():
            estimate(j).start()

        @pl.when(estimate_stays(j))
        def _():
            estimate_here(j).start()

    def backward(j, step, last):
        cre = jnp.zeros((48, 128), f32)
        cim = jnp.zeros((48, 128), f32)
        den = jnp.full((48, 128), DAMPING, f32)
        for f in range(FRAMES):
            tre, tim = tra[j, f, :48], tra[j, f, 48:]
            dre, dim = dat[f, :48], dat[f, 48:]
            cre = cre + (dre * tre + dim * tim)
            cim = cim + (dim * tre - dre * tim)
            den = den + (tre * tre + tim * tim)
        ere, eim = cre / den, cim / den
        if last:
            send_estimate(j, ere, eim)
        for f in range(FRAMES):
            tre, tim = tra[j, f, :48], tra[j, f, 48:]
            mre = dat[f, :48] - (ere * tre - eim * tim)
            mim = dat[f, 48:] - (ere * tim + eim * tre)
            gsc[f * 48 : f * 48 + 48, :128] = ere * mre + eim * mim
            gsc[f * 48 : f * 48 + 48, 128:] = ere * mim - eim * mre
        gsc[...] = right(gsc[...], tab("t12"))
        for f in range(0, FRAMES, 2):
            pair = []
            for g in (f, f + 1):
                part = gsc[g * 48 : g * 48 + 48, :]
                pair.append(jnp.concatenate([part[:, :128], part[:, 128:]], axis=0))
            grad = left(tab("l13"), jnp.concatenate(pair, axis=1))[:N]
            pair = []
            for g in (0, 1):
                one = grad[:, 128 * g : 128 * g + 128]
                pair.append(
                    jnp.concatenate([one * foc[j, f + g, :N], one * foc[j, f + g, N:]], axis=0)
                )
            both = left(tab("l15"), jnp.concatenate(pair, axis=1))
            for g in (0, 1):
                re, im = (both[k : k + 48, 128 * g : 128 * g + 128] for k in (0, 48))
                for h in range(2):
                    rows = slice(XP * h, XP * h + XP)
                    hsc[2 * h, pl.ds(f + g, XP, FRAMES), :] = re[rows]
                    hsc[2 * h + 1, pl.ds(f + g, XP, FRAMES), :] = im[rows]
        back = None
        for h in range(2):
            one = right(jnp.concatenate([hsc[2 * h], hsc[2 * h + 1]], axis=1), tab(f"t16{h}"))
            back = one if back is None else back + one
        grad = back[:, 128:] * pup[j, 0] - back[:, :128] * pup[j, 1]
        gab = fine(grad, tab("t18")) * tab("along")
        acc = gab[:FRAMES]
        for i in range(1, XP):
            acc = acc + gab[i * FRAMES : (i + 1) * FRAMES]
        curs[j] = curs[j] - step * fine(acc, tab("m2"))

    def first_half(j, _):
        forward(j)
        return 0

    loop(0, EARLY, first_half, 0)

    @pl.when(me_pat < GROUPS - 1)
    def _():
        halo.wait_recv()

    lane = lax.broadcasted_iota(jnp.int32, (N, 128), 1)
    top = me_pat * SH

    def pixels(j, q):
        return pltpu.make_async_remote_copy(
            src_ref=send.at[j, q],
            dst_ref=recv.at[j, me_frm],
            send_sem=msg_send.at[j, q],
            recv_sem=msg_recv.at[j, me_frm],
            device_id={"frm": q, "pat": me_pat},
            device_id_type=MESH,
        )

    def pixels_from(j, q):
        return pltpu.make_async_remote_copy(
            src_ref=send.at[j, q],
            dst_ref=recv.at[j, q],
            send_sem=msg_send.at[j, q],
            recv_sem=msg_recv.at[j, q],
            device_id={"frm": q, "pat": me_pat},
            device_id_type=MESH,
        )

    def cut(n, _):
        j, q = lax.div(n, FRAMES), lax.rem(me_frm + 1 + lax.rem(n, FRAMES), FRAMES)
        p = slots[PER * q + j]
        row = jnp.clip(anchors[0, p] - top, 0, SH - 1)
        col = anchors[1, p]
        tile = jnp.clip(lax.shift_right_logical(col, 7), 0, 15)
        off = col & 127
        a = strip[tile, pl.ds(row, N), :]
        b = strip[jnp.minimum(tile + 1, 15), pl.ds(row, N), :]
        turn = (128 - off) & 127
        patch = jnp.where(lane < 128 - off, pltpu.roll(a, turn, 1), pltpu.roll(b, turn, 1))

        @pl.when(q != me_frm)
        def _():
            send[j, q] = patch
            pixels(j, q).start()

        @pl.when(q == me_frm)
        def _():
            recv[j, me_frm] = patch

        return 0

    loop(0, PER * FRAMES, cut, 0)
    loop(EARLY, PER, first_half, 0)

    def work(j, _):
        def arrived(i, _):
            pixels_from(j, lax.rem(me_frm + i, FRAMES)).wait_recv()
            return 0

        loop(1, FRAMES, arrived, 0)
        window = tab("window")
        parts = []
        total = jnp.zeros((N, 128), f32)
        for f in range(FRAMES):
            part = jnp.where(lane < N, recv[j, f], 0.0) * window
            total = total + part * part
            parts.append(part)
        energy = jnp.sum(total) * float(N * N)
        for f, one in half_spectra(jnp.concatenate(parts, axis=0)):
            re, im = one[:48], one[48:]
            cos, sin = ramp[f, 0], ramp[f, 1]
            dat[f, :48] = re * cos - im * sin
            dat[f, 48:] = re * sin + im * cos
        step = (STEP * FRAMES) / (jnp.zeros((FRAMES, 128), f32) + energy)

        for t in range(ITERS):
            if t > 0:
                forward(j)
            backward(j, step, t == ITERS - 1)
        for f in range(FRAMES):
            nsend[f, pl.ds(j, 1), :] = curs[j, f : f + 1, :]
        return 0

    nsend[...] = jnp.zeros((FRAMES, 8, 128), f32)
    loop(0, PER, work, 0)

    def give(i, _):
        q = lax.rem(me_frm + i, FRAMES)
        to_peer(nsend, nrecv, n_send, n_recv, q).start()
        return 0

    loop(1, FRAMES, give, 0)
    nrecv[me_frm] = nsend[me_frm]

    def end_estimate(j, _):
        stays = estimate_stays(j)

        @pl.when(jnp.logical_not(stays))
        def _():
            estimate(j).wait_send()

        @pl.when(stays)
        def _():
            estimate_here(j).wait()

        return 0

    def end_pixels(n, _):
        j, q = lax.div(n, FRAMES), lax.rem(n, FRAMES)

        @pl.when(q != me_frm)
        def _():
            pixels(j, q).wait_send()

        return 0

    loop(0, PER * FRAMES, end_pixels, 0)
    drain(csend, crecv, c_send, c_recv)

    @pl.when(me_pat > 0)
    def _():
        halo.wait_send()

    take(nsend, nrecv, n_send, n_recv)

    out[...] = jnp.zeros((PPS, 128), f32)
    lane1 = lax.broadcasted_iota(jnp.int32, (PPS, 1), 0)

    def place_back(n, _):
        row = nrecv[lax.div(n, PER), pl.ds(lax.rem(n, PER), 1), :]
        out[...] = jnp.where(lane1 == slots[n], row, out[...])
        return 0

    loop(0, PPS, place_back, 0)
    loop(0, PER, end_estimate, 0)
    drain(nsend, nrecv, n_send, n_recv)

    def estimate_from(k, _):
        source = 2 * me_frm + lax.div(k, 2)

        @pl.when(jnp.logical_not(same & (source == me_pat)))
        def _():
            pltpu.make_async_remote_copy(
                src_ref=esend.at[k],
                dst_ref=obj.at[k],
                send_sem=e_send.at[k],
                recv_sem=e_recv.at[k],
                device_id={"frm": half, "pat": source},
                device_id_type=MESH,
            ).wait_recv()

        return 0

    loop(0, 4, estimate_from, 0)


EARLY = 3


def shards(frames, shifts, coefficients, anchors, assign):
    arrays = packed()[0]
    hbm = pl.BlockSpec(memory_space=pltpu.HBM)
    sems = pltpu.SemaphoreType.DMA
    obj, new = pl.pallas_call(
        kernel,
        in_specs=[hbm] * (5 + len(arrays)),
        out_specs=[hbm, pl.BlockSpec(memory_space=pltpu.VMEM)],
        out_shape=[
            jax.ShapeDtypeStruct((PER, 2, N, 128), f32),
            jax.ShapeDtypeStruct((PPS, 128), f32),
        ],
        scratch_shapes=[pltpu.VMEM(a.shape, a.dtype) for a in arrays]
        + [
            pltpu.SMEM((1, 2), f32),
            pltpu.VMEM((1, PPS, MODES), f32),
            pltpu.SMEM((2, PPS), jnp.int32),
            pltpu.SMEM((PPS,), jnp.int32),
            pltpu.SMEM((PPS,), jnp.int32),
            pltpu.VMEM((16, SH + N, 128), f32),
            pltpu.VMEM((PER, FRAMES, N, 128), f32),
            pltpu.VMEM((PER, FRAMES, N, 128), f32),
            pltpu.VMEM((FRAMES, 8, 128), f32),
            pltpu.VMEM((FRAMES, 8, 128), f32),
            pltpu.VMEM((FRAMES, 8, 128), f32),
            pltpu.VMEM((FRAMES, 8, 128), f32),
            pltpu.VMEM((PER, 2, N, 128), f32),
            pltpu.VMEM((FRAMES, 2, 48, 128), f32),
            pltpu.VMEM((PER, FRAMES, 128), f32),
            pltpu.VMEM((PER, 2, XP * FRAMES, 128), f32),
            pltpu.VMEM((PER, FRAMES, 176, 128), f32),
            pltpu.VMEM((PER, FRAMES, 96, 128), f32),
            pltpu.VMEM((FRAMES, 96, 128), f32),
            pltpu.VMEM((4, XP * FRAMES, 128), f32),
            pltpu.VMEM((FRAMES * N, 256), f32),
            pltpu.VMEM((FRAMES * 48, 256), f32),
            pltpu.VMEM((4, XP * FRAMES, 128), f32),
            sems((4,)),
            sems((len(arrays),)),
            sems((16,)),
            sems,
            sems,
            sems((PER, FRAMES)),
            sems((PER, FRAMES)),
            sems((FRAMES,)),
            sems((FRAMES,)),
            sems((FRAMES,)),
            sems((FRAMES,)),
            sems((PER,)),
            sems((PER,)),
            sems((PER,)),
        ],
        compiler_params=pltpu.CompilerParams(
            collective_id=0, has_side_effects=True, vmem_limit_bytes=56 << 20
        ),
        name="deconvolve",
    )(frames, shifts, coefficients, anchors.T, assign, *[jnp.asarray(a) for a in arrays])
    return new[None, :, :MODES], obj[:, :, :, :N].reshape(PER, 2, N * N)


def solution(mesh):
    in_specs = (
        P("frm", "pat", None),
        P("frm", None),
        P("frm", "pat", None),
        P("pat", None),
        P("pat"),
    )
    out_specs = (P("frm", "pat", None), P(("pat", "frm"), None, None))
    return jax.shard_map(shards, mesh=mesh, in_specs=in_specs, out_specs=out_specs, check_vma=False)
```

```python
import functools
import math

import jax
import jax.numpy as jnp
import ml_dtypes
import numpy as np
from jax import lax
from jax.experimental import pallas as pl
from jax.experimental.pallas import tpu as pltpu
from jax.sharding import PartitionSpec as P

N = 88
MODES = 40
ITERS = 2
FRAMES = 8
ITEMS = 16
TEAMS = 2
SH = 128
PPS = 32
GROUPS = 16
LOW = 22
NX = 45
XP = 24
NU = 45
PER = 4
DAMPING = 0.05
STEP = 64.0
f32, bf16 = jnp.float32, jnp.bfloat16
MESH = pl.DeviceIdType.MESH


def noll_index(j):
    n = 0
    remaining = j - 1
    while remaining > n:
        n += 1
        remaining -= n
    m = (-1) ** j * (n % 2 + 2 * ((remaining + (n + 1) % 2) // 2))
    return (n, m)


def zernike_values(row, col):
    radius = np.sqrt(row * row + col * col)
    angle = np.arctan2(row, col)
    values = []
    for j in range(2, MODES + 2):
        n, m = noll_index(j)
        k_abs = abs(m)
        radial = np.zeros_like(radius)
        for k in range((n - k_abs) // 2 + 1):
            factor = (
                (-1) ** k
                * math.factorial(n - k)
                / (
                    math.factorial(k)
                    * math.factorial((n + k_abs) // 2 - k)
                    * math.factorial((n - k_abs) // 2 - k)
                )
            )
            radial = radial + factor * radius ** (n - 2 * k)
        if m == 0:
            values.append(math.sqrt(n + 1) * radial)
        elif m > 0:
            values.append(math.sqrt(2 * (n + 1)) * radial * np.cos(k_abs * angle))
        else:
            values.append(math.sqrt(2 * (n + 1)) * radial * np.sin(k_abs * angle))
    return np.stack(values)


def ultraspherical(order, t):
    t = np.asarray(t, np.float64)
    inside = (np.arange(NX) + LOW - 44.0) / 22.0

    def raw(x):
        last, value = np.zeros_like(x), np.ones_like(x)
        for n in range(1, order + 1):
            last, value = value, (2.0 * (n + 2.0) * x * value - (n + 4.0) * last) / n
        return value

    weight = np.sqrt(1.0 - inside**2)
    return raw(t) / np.sqrt(np.sum(weight * raw(inside) ** 2) / np.sum(weight))


PAIRS = [(a, b) for a in range(9) for b in range(9 - a)]


def halves(table):
    hi = table.astype(np.float32).astype(ml_dtypes.bfloat16)
    lo = (table - hi.astype(np.float64)).astype(np.float32).astype(ml_dtypes.bfloat16)
    return hi, lo


def right_table(table):
    hi, lo = halves(table)
    return np.concatenate([hi, hi, lo], axis=0)


def left_table(table):
    hi, lo = halves(table)
    return np.concatenate([hi, hi, lo], axis=1)


@functools.lru_cache
def tables():
    w = 2.0 * np.pi / N
    full = np.arange(N)
    px = LOW + np.arange(NX)
    unit = (px - 44.0) / 22.0
    aperture = (unit[:, None] ** 2 + unit[None, :] ** 2 <= 1.0).astype(np.float64)
    a32 = ((px.astype(np.float32) - np.float32(44)) / np.float32(22)).astype(np.float32)
    r32 = np.sqrt(a32[:, None] * a32[:, None] + a32[None, :] * a32[None, :])
    assert np.array_equal(aperture, (r32 <= 1.0).astype(np.float64))
    scale = 1.0 / (N * N * aperture.sum())
    root = math.sqrt(scale)

    grid = np.linspace(-1.0, 1.0, 31)
    rows, cols = (g.ravel() for g in np.meshgrid(grid, grid, indexing="ij"))
    basis = np.stack([ultraspherical(a, rows) * ultraspherical(b, cols) for a, b in PAIRS], axis=1)
    fit = np.linalg.lstsq(basis, zernike_values(rows, cols).T, rcond=None)[0].T

    out = {}
    spread_ab = np.zeros((MODES, 128))
    spread_ab[:, : len(PAIRS)] = fit
    spread_ab[:, 64 : 64 + len(PAIRS)] = fit
    m1 = np.zeros((128, 128))
    m1[:MODES] = spread_ab
    out["m1"] = fine_table(m1)
    out["m2"] = fine_table(m1.T)

    along = np.zeros((XP, 128))
    mask = np.zeros((XP, 128))
    t3 = np.zeros((128, 128))
    for h in range(2):
        for k, (a, b) in enumerate(PAIRS):
            for i in range(XP):
                if i + XP * h < NX:
                    along[i, 64 * h + k] = ultraspherical(a, unit[i + XP * h])
            t3[64 * h + k, 64 * h : 64 * h + NX] = ultraspherical(b, unit)
        for i in range(XP):
            if i + XP * h < NX:
                mask[i, 64 * h : 64 * h + NX] = aperture[i + XP * h]
    out["along"] = np.repeat(along, ITEMS, axis=0).astype(np.float32)
    out["mask"] = np.repeat(mask, ITEMS, axis=0).astype(np.float32)
    out["t3"] = fine_table(t3)
    out["t18"] = fine_table(t3.T)

    ang = w * (np.outer(px, full) % N)
    c, s = np.cos(ang), np.sin(ang)
    t5p = np.zeros((128, 256))
    t5p[:NX, :N], t5p[64 : 64 + NX, :N] = c, s
    t5p[:NX, 128 : 128 + N], t5p[64 : 64 + NX, 128 : 128 + N] = -s, c
    out["t5p"] = right_table(t5p)
    t16p = np.zeros((256, 128))
    t16p[:N, :NX], t16p[128 : 128 + N, :NX] = c.T, -s.T
    t16p[:N, 64 : 64 + NX], t16p[128 : 128 + N, 64 : 64 + NX] = s.T, c.T
    hi, lo = halves(t16p)
    out["t16p"] = np.concatenate(
        [np.concatenate([hi, lo], axis=1), np.concatenate([hi, 0 * hi], axis=1)], axis=0
    )
    l7 = np.zeros((176, 96))
    l7[:N, :NX], l7[:N, 48 : 48 + NX] = c.T, s.T
    l7[N:, :NX], l7[N:, 48 : 48 + NX] = -s.T, c.T
    out["l7"] = left_table(l7 * root)
    l15 = np.zeros((96, 176))
    l15[:NX, :N], l15[:NX, N:] = c, -s
    l15[48 : 48 + NX, :N], l15[48 : 48 + NX, N:] = s, c
    out["l15"] = left_table(l15)

    ang = w * (np.outer(full, full) % N)
    c, s = np.cos(ang), np.sin(ang)
    t9 = np.zeros((128, 256))
    t9[:N, :N], t9[:N, 128 : 128 + N] = c, -s
    out["t9"] = right_table(t9)
    l10 = np.zeros((96, 176))
    l10[:NU, :N], l10[:NU, N:] = c[:NU], s[:NU]
    l10[48 : 48 + NU, :N], l10[48 : 48 + NU, N:] = -s[:NU], c[:NU]
    out["l10"] = left_table(l10)
    t12 = np.zeros((256, 256))
    t12[:N, :N], t12[128 : 128 + N, :N] = c, -s
    t12[:N, 128 : 128 + N], t12[128 : 128 + N, 128 : 128 + N] = s, c
    out["t12"] = right_table(t12)
    weight = np.full((NU,), 2.0)
    weight[0] = weight[44] = 1.0
    weight = weight * (-2.0) * 2.0 * root
    l13 = np.zeros((96, 96))
    l13[:N, :NU], l13[:N, 48 : 48 + NU] = c[:, :NU] * weight, -s[:, :NU] * weight
    out["l13"] = left_table(l13)

    profile = 0.5 - 0.5 * np.cos(2.0 * np.pi * (full + 0.5) / N)
    window = np.zeros((N, 128), np.float32)
    window[:, :N] = profile[:, None] * profile[None, :]
    out["window"] = window
    signed = (full + 44) % N - 44.0
    freq = np.zeros((2, 48, 128), np.float32)
    freq[0, :NU, :] = signed[:NU, None]
    freq[1, :, :N] = signed[None, :]
    out["freq"] = (freq * (-w)).astype(np.float32)

    flip = np.zeros((128, 128), ml_dtypes.bfloat16)
    for v in range(N):
        flip[(N - v) % N, v] = 1
    out["flip"] = np.concatenate([flip, flip], axis=0)
    place = np.zeros((176, 192), ml_dtypes.bfloat16)
    for u in range(N):
        if u < NU:
            place[u, u] = 1
            place[N + u, 48 + u] = 1
        else:
            place[u, 96 + N - u] = 1
            place[N + u, 144 + N - u] = -1
    out["place"] = np.concatenate([place, place], axis=1)
    return out


def fine_table(table):
    hi = table.astype(np.float32).astype(ml_dtypes.bfloat16)
    rest = table - hi.astype(np.float64)
    mid = rest.astype(np.float32).astype(ml_dtypes.bfloat16)
    low = (rest - mid.astype(np.float64)).astype(np.float32).astype(ml_dtypes.bfloat16)
    return np.concatenate([hi, hi, mid, mid, low, hi], axis=0)


def split(x):
    hi = x.astype(bf16)
    return hi, (x - hi.astype(f32)).astype(bf16)


def dot(a, b):
    return jnp.dot(a, b, preferred_element_type=f32)


def right(x, table):
    hi, lo = split(x)
    return dot(jnp.concatenate([hi, lo, hi], axis=1), table)


def fine(x, table):
    hi = x.astype(bf16)
    rest = x - hi.astype(f32)
    mid = rest.astype(bf16)
    low = (rest - mid.astype(f32)).astype(bf16)
    k = x.shape[1]
    t2 = jnp.concatenate([table[:k], table[2 * k : 3 * k]], axis=1)
    tl = table[4 * k : 5 * k]
    two = dot(jnp.concatenate([hi, mid], axis=1), jnp.concatenate([t2, t2], axis=0))
    rest = dot(jnp.concatenate([hi, low], axis=1), jnp.concatenate([tl, table[:k]], axis=0))
    return two[:, :128] + (two[:, 128:] + rest)


def left(table, x):
    hi, lo = split(x)
    k, m = x.shape[0], table.shape[0]
    if k > 128:
        t2 = jnp.concatenate([table[:, :k], table[:, 2 * k:]], axis=0)
        a = dot(t2, hi)
        return a[:m] + (a[m:] + dot(table[:, :k], lo))
    rest = jnp.concatenate([table[:, 2 * k:], jnp.zeros((m, k), bf16)], axis=1)
    a = dot(jnp.concatenate([table[:, :2 * k], rest], axis=0), jnp.concatenate([hi, lo], axis=0))
    return a[:m] + a[m:]


def sincos(x):
    k = jnp.floor(x * (2.0 / math.pi) + 0.5)
    r = x - k * 1.5703125
    r = r - k * 4.8351287841796875e-4
    r = r - k * 3.1385570764541626e-07
    z = r * r
    s = r + r * z * (-1.6666654611e-1 + z * (8.3321608736e-3 + z * -1.9515295891e-4))
    c = 1.0 - 0.5 * z + z * z * (
        4.166664568298827e-2 + z * (-1.388731625493765e-3 + z * 2.443315711809948e-5)
    )
    q = k.astype(jnp.int32)
    swap = (q & 1) == 1
    sin = jnp.where(swap, c, s)
    cos = jnp.where(swap, s, c)
    sin = jnp.where((q & 2) == 2, -sin, sin)
    cos = jnp.where(((q + 1) & 2) == 2, -cos, cos)
    return sin, cos


PACKS = {
    "narrow": ("m1", "m2", "t3", "t18", "flip"),
    "wide": ("t5p", "t16p", "t12", "t9"),
    "left96": ("l7", "l13"),
    "left176": ("l15", "l10"),
    "order": ("place",),
    "real": ("along", "mask", "window", "freq"),
}


@functools.lru_cache
def packed():
    arrays, where = [], {}
    for index, names in enumerate(PACKS.values()):
        rows = []
        for name in names:
            table = tables()[name]
            table = table.reshape(-1, table.shape[-1])
            where[name] = (index, sum(r.shape[0] for r in rows), table.shape[0])
            rows.append(table)
        arrays.append(np.concatenate(rows, axis=0))
    return arrays, where


def kernel(*refs):
    where = packed()[1]
    count = len(PACKS)
    frames, shifts_in, coefs_in, anchors_in, assign_in = refs[:5]
    packs_in = refs[5 : 5 + count]
    obj, out = refs[5 + count : 7 + count]
    packs = refs[7 + count : 7 + 2 * count]
    (
        shifts,
        coefs,
        anchors,
        assign,
        slots,
        strip,
        send,
        recv,
        csend,
        crecv,
        nsend,
        nrecv,
        esend,
        ramp,
        curs,
        pup,
        foc,
        tra,
        dat,
        ysc,
        asc,
        gsc,
        hsc,
        small_sem,
        pack_sem,
        load_sem,
        halo_send,
        halo_recv,
        msg_send,
        msg_recv,
        c_send,
        c_recv,
        n_send,
        n_recv,
        e_send,
        e_recv,
        e_own,
    ) = refs[7 + 2 * count :]

    def tab(name):
        index, start, rows = where[name]
        return packs[index][start : start + rows, :]

    me_frm, me_pat = lax.axis_index("frm"), lax.axis_index("pat")
    half, side = lax.div(me_pat, 2), lax.rem(me_pat, 2)
    loop = lax.fori_loop

    small = [
        pltpu.make_async_copy(a, b, small_sem.at[i])
        for i, (a, b) in enumerate(
            [(shifts_in, shifts), (coefs_in, coefs), (anchors_in, anchors), (assign_in, assign)]
        )
    ]
    for copy in small:
        copy.start()

    def load(t):
        return pltpu.make_async_copy(
            frames.at[0, :, pl.ds(pl.multiple_of(t * 128, 128), 128)],
            strip.at[t, pl.ds(0, SH), :],
            load_sem.at[t],
        )

    def start_load(t, _):
        load(t).start()
        return 0

    def end_load(t, _):
        load(t).wait()
        return 0

    loop(0, 16, start_load, 0)
    pack_loads = [
        pltpu.make_async_copy(packs_in[i], packs[i], pack_sem.at[i]) for i in range(count)
    ]
    for copy in pack_loads:
        copy.start()

    barrier = pltpu.get_barrier_semaphore()

    def tell(frm, pat):
        pl.semaphore_signal(
            barrier, inc=1, device_id={"frm": frm, "pat": pat}, device_id_type=MESH
        )

    def greet(q, _):
        @pl.when(q != me_frm)
        def _():
            tell(q, me_pat)

        return 0

    loop(0, FRAMES, greet, 0)

    @pl.when(me_pat < GROUPS - 1)
    def _():
        tell(me_frm, me_pat + 1)

    same = half == me_frm

    def greet_late(k, _):
        @pl.when(jnp.logical_not(same & (2 * me_frm + k == me_pat)))
        def _():
            tell(half, 2 * me_frm + k)

        return 0

    loop(0, 2, greet_late, 0)

    for copy in small:
        copy.wait()

    def order(g, _):
        first = jnp.int32(0)
        second = jnp.int32(0)
        for p in range(PPS - 1, -1, -1):
            hit = assign[p] == g
            second = jnp.where(hit, first, second)
            first = jnp.where(hit, p, first)
        slots[2 * g] = first
        slots[2 * g + 1] = second
        return 0

    loop(0, GROUPS, order, 0)

    def to_peer(source, target, send_sems, recv_sems, q):
        return pltpu.make_async_remote_copy(
            src_ref=source.at[q],
            dst_ref=target.at[me_frm],
            send_sem=send_sems.at[q],
            recv_sem=recv_sems.at[me_frm],
            device_id={"frm": q, "pat": me_pat},
            device_id_type=MESH,
        )

    def from_peer(source, target, send_sems, recv_sems, q):
        return pltpu.make_async_remote_copy(
            src_ref=source.at[q],
            dst_ref=target.at[q],
            send_sem=send_sems.at[q],
            recv_sem=recv_sems.at[q],
            device_id={"frm": q, "pat": me_pat},
            device_id_type=MESH,
        )

    csend[...] = jnp.zeros((FRAMES, 8, 128), f32)

    def fill_coefs(q, _):
        for j in range(PER):
            csend[q, j : j + 1, :MODES] = coefs[0, pl.ds(slots[PER * q + j], 1), :]
        for k in range(2):
            csend[q, PER + k : PER + k + 1, :] = jnp.zeros((1, 128), f32) + shifts[0, k]
        return 0

    loop(0, FRAMES, fill_coefs, 0)
    crecv[me_frm] = csend[me_frm]

    @pl.when(me_pat == GROUPS - 1)
    def _():
        strip[:, SH:, :] = jnp.zeros((16, N, 128), f32)

    loop(0, 16, end_load, 0)
    pl.semaphore_wait(
        barrier,
        FRAMES - 1 + (me_pat > 0).astype(jnp.int32) + 2 - same.astype(jnp.int32),
    )

    def send_coefs(i, _):
        to_peer(csend, crecv, c_send, c_recv, lax.rem(me_frm + i, FRAMES)).start()
        return 0

    loop(1, FRAMES, send_coefs, 0)

    halo = pltpu.make_async_remote_copy(
        src_ref=strip.at[:, pl.ds(0, N), :],
        dst_ref=strip.at[:, pl.ds(SH, N), :],
        send_sem=halo_send,
        recv_sem=halo_recv,
        device_id={"frm": me_frm, "pat": jnp.maximum(me_pat - 1, 0)},
        device_id_type=MESH,
    )

    @pl.when(me_pat > 0)
    def _():
        halo.start()

    for copy in pack_loads:
        copy.wait()

    def take(source, target, send_sems, recv_sems):
        def one(i, _):
            q = lax.rem(me_frm + i, FRAMES)
            from_peer(source, target, send_sems, recv_sems, q).wait_recv()
            return 0

        loop(1, FRAMES, one, 0)

    def drain(source, target, send_sems, recv_sems):
        def one(i, _):
            q = lax.rem(me_frm + i, FRAMES)
            to_peer(source, target, send_sems, recv_sems, q).wait_send()
            return 0

        loop(1, FRAMES, one, 0)

    take(csend, crecv, c_send, c_recv)
    for b in range(TEAMS):
        curs[b] = jnp.concatenate(
            [crecv[f, 2 * b + i : 2 * b + i + 1, :] for i in range(2) for f in range(FRAMES)],
            axis=0,
        )
    freq = tab("freq")

    def make_ramp(f, _):
        angle = freq[:48] * crecv[f, PER : PER + 1, :] + freq[48:] * crecv[f, PER + 1 : PER + 2, :]
        sin, cos = sincos(angle)
        ramp[f, 0] = cos
        ramp[f, 1] = sin
        return 0

    loop(0, FRAMES, make_ramp, 0)

    def half_spectra(values):
        asc[...] = right(values, tab("t9"))
        for f in range(0, ITEMS, 2):
            stacked = []
            for g in (f, f + 1):
                part = asc[g * N : (g + 1) * N, :]
                stacked.append(jnp.concatenate([part[:, :128], part[:, 128:]], axis=0))
            both = left(tab("l10"), jnp.concatenate(stacked, axis=1))
            yield f, both[:, :128]
            yield f + 1, both[:, 128:]

    low_lanes = lax.broadcasted_iota(jnp.int32, (XP * ITEMS, 128), 1) < 64

    def forward(b):
        cab = fine(curs[b], tab("m1"))
        phase = fine(jnp.concatenate([cab] * XP, axis=0) * tab("along"), tab("t3"))
        sin, cos = sincos(phase)
        mask = tab("mask")
        pr, pi = cos * mask, sin * mask
        pup[b, 0] = pr
        pup[b, 1] = pi
        for h in range(2):
            if h == 0:
                mix = jnp.where(low_lanes, pr, pltpu.roll(pi, 64, 1))
            else:
                mix = jnp.where(low_lanes, pltpu.roll(pr, 64, 1), pi)
            both = right(mix, tab("t5p"))
            ysc[h] = both[:, :128]
            ysc[2 + h] = both[:, 128:]
        spreads = []
        for f in range(0, ITEMS, 2):
            pair = []
            for g in (f, f + 1):
                pair.append(
                    jnp.concatenate([ysc[h, pl.ds(g, XP, ITEMS), :] for h in range(4)], axis=0)
                )
            both = left(tab("l7"), jnp.concatenate(pair, axis=1))
            for g in (0, 1):
                one = both[:, 128 * g : 128 * g + 128]
                foc[b, f + g] = one
                spreads.append(one[:N] * one[:N] + one[N:] * one[N:])
        for f, one in half_spectra(jnp.concatenate(spreads, axis=0)):
            tra[b, f] = one

    def estimate(j):
        return pltpu.make_async_remote_copy(
            src_ref=esend.at[j],
            dst_ref=obj.at[2 * side + lax.rem(j, 2)],
            send_sem=e_send.at[j],
            recv_sem=e_recv.at[2 * side + lax.rem(j, 2)],
            device_id={"frm": half, "pat": 2 * me_frm + lax.div(j, 2)},
            device_id_type=MESH,
        )

    def estimate_here(j):
        return pltpu.make_async_copy(
            esend.at[j], obj.at[2 * side + lax.rem(j, 2)], e_own.at[j]
        )

    def estimate_stays(j):
        return same & (2 * me_frm + lax.div(j, 2) == me_pat)

    def fill_estimate(j, ere, eim):
        spectrum = jnp.concatenate([ere, eim], axis=0) * (1.0 / N)
        hi, lo = split(spectrum)
        flipped = dot(jnp.concatenate([hi, lo], axis=1), tab("flip"))
        hi, lo = split(jnp.concatenate([spectrum, flipped], axis=0))
        whole = dot(tab("place"), jnp.concatenate([hi, lo], axis=0))
        esend[j, 0] = whole[:N]
        esend[j, 1] = whole[N:]

    def send_estimate(j):
        @pl.when(jnp.logical_not(estimate_stays(j)))
        def _():
            estimate(j).start()

        @pl.when(estimate_stays(j))
        def _():
            estimate_here(j).start()

    def backward(b, step, last):
        for i in range(2):
            cre = jnp.zeros((48, 128), f32)
            cim = jnp.zeros((48, 128), f32)
            den = jnp.full((48, 128), DAMPING, f32)
            for f in range(FRAMES * i, FRAMES * (i + 1)):
                tre, tim = tra[b, f, :48], tra[b, f, 48:]
                dre, dim = dat[f, :48], dat[f, 48:]
                cre = cre + (dre * tre + dim * tim)
                cim = cim + (dim * tre - dre * tim)
                den = den + (tre * tre + tim * tim)
            ere, eim = cre / den, cim / den
            for f in range(FRAMES * i, FRAMES * (i + 1)):
                tre, tim = tra[b, f, :48], tra[b, f, 48:]
                mre = dat[f, :48] - (ere * tre - eim * tim)
                mim = dat[f, 48:] - (ere * tim + eim * tre)
                gsc[f * 48 : f * 48 + 48, :128] = ere * mre + eim * mim
                gsc[f * 48 : f * 48 + 48, 128:] = ere * mim - eim * mre
            if last:
                fill_estimate(2 * b + i, ere, eim)
        if last:
            send_estimate(2 * b)
            send_estimate(2 * b + 1)
        gsc[...] = right(gsc[...], tab("t12"))
        for f in range(0, ITEMS, 2):
            pair = []
            for g in (f, f + 1):
                part = gsc[g * 48 : g * 48 + 48, :]
                pair.append(jnp.concatenate([part[:, :128], part[:, 128:]], axis=0))
            grad = left(tab("l13"), jnp.concatenate(pair, axis=1))[:N]
            pair = []
            for g in (0, 1):
                one = grad[:, 128 * g : 128 * g + 128]
                pair.append(
                    jnp.concatenate([one * foc[b, f + g, :N], one * foc[b, f + g, N:]], axis=0)
                )
            both = left(tab("l15"), jnp.concatenate(pair, axis=1))
            for g in (0, 1):
                re, im = (both[k : k + 48, 128 * g : 128 * g + 128] for k in (0, 48))
                for h in range(2):
                    rows = slice(XP * h, XP * h + XP)
                    hsc[2 * h, pl.ds(f + g, XP, ITEMS), :] = re[rows]
                    hsc[2 * h + 1, pl.ds(f + g, XP, ITEMS), :] = im[rows]
        sides = []
        for h in range(2):
            hi, lo = split(jnp.concatenate([hsc[2 * h], hsc[2 * h + 1]], axis=1))
            one = dot(jnp.concatenate([hi, lo], axis=1), tab("t16p"))
            sides.append(one[:, :128] + one[:, 128:])
        gre = jnp.where(low_lanes, sides[0], pltpu.roll(sides[1], 64, 1))
        gim = jnp.where(low_lanes, pltpu.roll(sides[0], 64, 1), sides[1])
        grad = gim * pup[b, 0] - gre * pup[b, 1]
        gab = fine(grad, tab("t18")) * tab("along")
        acc = gab[:ITEMS]
        for i in range(1, XP):
            acc = acc + gab[i * ITEMS : (i + 1) * ITEMS]
        curs[b] = curs[b] - step * fine(acc, tab("m2"))

    def first_half(j, _):
        forward(j)
        return 0

    loop(0, EARLY, first_half, 0)

    @pl.when(me_pat < GROUPS - 1)
    def _():
        halo.wait_recv()

    lane = lax.broadcasted_iota(jnp.int32, (N, 128), 1)
    top = me_pat * SH

    def pixels(j, q):
        return pltpu.make_async_remote_copy(
            src_ref=send.at[j, q],
            dst_ref=recv.at[j, me_frm],
            send_sem=msg_send.at[j, q],
            recv_sem=msg_recv.at[j, me_frm],
            device_id={"frm": q, "pat": me_pat},
            device_id_type=MESH,
        )

    def pixels_from(j, q):
        return pltpu.make_async_remote_copy(
            src_ref=send.at[j, q],
            dst_ref=recv.at[j, q],
            send_sem=msg_send.at[j, q],
            recv_sem=msg_recv.at[j, q],
            device_id={"frm": q, "pat": me_pat},
            device_id_type=MESH,
        )

    def cut(n, _):
        j, q = lax.div(n, FRAMES), lax.rem(me_frm + 1 + lax.rem(n, FRAMES), FRAMES)
        p = slots[PER * q + j]
        row = jnp.clip(anchors[0, p] - top, 0, SH - 1)
        col = anchors[1, p]
        tile = jnp.clip(lax.shift_right_logical(col, 7), 0, 15)
        off = col & 127
        a = strip[tile, pl.ds(row, N), :]
        b = strip[jnp.minimum(tile + 1, 15), pl.ds(row, N), :]
        turn = (128 - off) & 127
        patch = jnp.where(lane < 128 - off, pltpu.roll(a, turn, 1), pltpu.roll(b, turn, 1))

        @pl.when(q != me_frm)
        def _():
            send[j, q] = patch
            pixels(j, q).start()

        @pl.when(q == me_frm)
        def _():
            recv[j, me_frm] = patch

        return 0

    loop(0, PER * FRAMES, cut, 0)
    loop(EARLY, TEAMS, first_half, 0)

    def work(b, _):
        def arrived(i, _):
            for k in range(2):
                pixels_from(2 * b + k, lax.rem(me_frm + i, FRAMES)).wait_recv()
            return 0

        loop(1, FRAMES, arrived, 0)
        window = tab("window")
        parts, steps = [], []
        for i in range(2):
            total = jnp.zeros((N, 128), f32)
            for f in range(FRAMES):
                part = jnp.where(lane < N, recv[2 * b + i, f], 0.0) * window
                total = total + part * part
                parts.append(part)
            energy = jnp.sum(total) * float(N * N)
            steps.append((STEP * FRAMES) / (jnp.zeros((FRAMES, 128), f32) + energy))
        for f, one in half_spectra(jnp.concatenate(parts, axis=0)):
            re, im = one[:48], one[48:]
            cos, sin = ramp[f % FRAMES, 0], ramp[f % FRAMES, 1]
            dat[f, :48] = re * cos - im * sin
            dat[f, 48:] = re * sin + im * cos
        step = jnp.concatenate(steps, axis=0)
        for t in range(ITERS):
            if t > 0:
                forward(b)
            backward(b, step, t == ITERS - 1)
        for i in range(2):
            for f in range(FRAMES):
                row = FRAMES * i + f
                nsend[f, pl.ds(2 * b + i, 1), :] = curs[b, row : row + 1, :]
        return 0

    nsend[...] = jnp.zeros((FRAMES, 8, 128), f32)
    loop(0, TEAMS, work, 0)

    def give(i, _):
        q = lax.rem(me_frm + i, FRAMES)
        to_peer(nsend, nrecv, n_send, n_recv, q).start()
        return 0

    loop(1, FRAMES, give, 0)
    nrecv[me_frm] = nsend[me_frm]

    def end_estimate(j, _):
        stays = estimate_stays(j)

        @pl.when(jnp.logical_not(stays))
        def _():
            estimate(j).wait_send()

        @pl.when(stays)
        def _():
            estimate_here(j).wait()

        return 0

    def end_pixels(n, _):
        j, q = lax.div(n, FRAMES), lax.rem(n, FRAMES)

        @pl.when(q != me_frm)
        def _():
            pixels(j, q).wait_send()

        return 0

    loop(0, PER * FRAMES, end_pixels, 0)
    drain(csend, crecv, c_send, c_recv)

    @pl.when(me_pat > 0)
    def _():
        halo.wait_send()

    take(nsend, nrecv, n_send, n_recv)

    out[...] = jnp.zeros((PPS, 128), f32)
    lane1 = lax.broadcasted_iota(jnp.int32, (PPS, 1), 0)

    def place_back(n, _):
        row = nrecv[lax.div(n, PER), pl.ds(lax.rem(n, PER), 1), :]
        out[...] = jnp.where(lane1 == slots[n], row, out[...])
        return 0

    loop(0, PPS, place_back, 0)
    loop(0, PER, end_estimate, 0)
    drain(nsend, nrecv, n_send, n_recv)

    def estimate_from(k, _):
        source = 2 * me_frm + lax.div(k, 2)

        @pl.when(jnp.logical_not(same & (source == me_pat)))
        def _():
            pltpu.make_async_remote_copy(
                src_ref=esend.at[k],
                dst_ref=obj.at[k],
                send_sem=e_send.at[k],
                recv_sem=e_recv.at[k],
                device_id={"frm": half, "pat": source},
                device_id_type=MESH,
            ).wait_recv()

        return 0

    loop(0, 4, estimate_from, 0)


EARLY = 0


def shards(frames, shifts, coefficients, anchors, assign):
    arrays = packed()[0]
    hbm = pl.BlockSpec(memory_space=pltpu.HBM)
    sems = pltpu.SemaphoreType.DMA
    obj, new = pl.pallas_call(
        kernel,
        in_specs=[hbm] * (5 + len(arrays)),
        out_specs=[hbm, pl.BlockSpec(memory_space=pltpu.VMEM)],
        out_shape=[
            jax.ShapeDtypeStruct((PER, 2, N, 128), f32),
            jax.ShapeDtypeStruct((PPS, 128), f32),
        ],
        scratch_shapes=[pltpu.VMEM(a.shape, a.dtype) for a in arrays]
        + [
            pltpu.SMEM((1, 2), f32),
            pltpu.VMEM((1, PPS, MODES), f32),
            pltpu.SMEM((2, PPS), jnp.int32),
            pltpu.SMEM((PPS,), jnp.int32),
            pltpu.SMEM((PPS,), jnp.int32),
            pltpu.VMEM((16, SH + N, 128), f32),
            pltpu.VMEM((PER, FRAMES, N, 128), f32),
            pltpu.VMEM((PER, FRAMES, N, 128), f32),
            pltpu.VMEM((FRAMES, 8, 128), f32),
            pltpu.VMEM((FRAMES, 8, 128), f32),
            pltpu.VMEM((FRAMES, 8, 128), f32),
            pltpu.VMEM((FRAMES, 8, 128), f32),
            pltpu.VMEM((PER, 2, N, 128), f32),
            pltpu.VMEM((FRAMES, 2, 48, 128), f32),
            pltpu.VMEM((TEAMS, ITEMS, 128), f32),
            pltpu.VMEM((TEAMS, 2, XP * ITEMS, 128), f32),
            pltpu.VMEM((TEAMS, ITEMS, 176, 128), f32),
            pltpu.VMEM((TEAMS, ITEMS, 96, 128), f32),
            pltpu.VMEM((ITEMS, 96, 128), f32),
            pltpu.VMEM((4, XP * ITEMS, 128), f32),
            pltpu.VMEM((ITEMS * N, 256), f32),
            pltpu.VMEM((ITEMS * 48, 256), f32),
            pltpu.VMEM((4, XP * ITEMS, 128), f32),
            sems((4,)),
            sems((len(arrays),)),
            sems((16,)),
            sems,
            sems,
            sems((PER, FRAMES)),
            sems((PER, FRAMES)),
            sems((FRAMES,)),
            sems((FRAMES,)),
            sems((FRAMES,)),
            sems((FRAMES,)),
            sems((PER,)),
            sems((PER,)),
            sems((PER,)),
        ],
        compiler_params=pltpu.CompilerParams(
            collective_id=0, has_side_effects=True, vmem_limit_bytes=56 << 20
        ),
        name="deconvolve",
    )(frames, shifts, coefficients, anchors.T, assign, *[jnp.asarray(a) for a in arrays])
    return new[None, :, :MODES], obj[:, :, :, :N].reshape(PER, 2, N * N)


def solution(mesh):
    in_specs = (
        P("frm", "pat", None),
        P("frm", None),
        P("frm", "pat", None),
        P("pat", None),
        P("pat"),
    )
    out_specs = (P("frm", "pat", None), P(("pat", "frm"), None, None))
    return jax.shard_map(shards, mesh=mesh, in_specs=in_specs, out_specs=out_specs, check_vma=False)
```

```python
import functools
import math

import jax
import jax.numpy as jnp
import ml_dtypes
import numpy as np
from jax import lax
from jax.experimental import pallas as pl
from jax.experimental.pallas import tpu as pltpu
from jax.sharding import PartitionSpec as P

N = 88
MODES = 40
ITERS = 2
FRAMES = 8
ITEMS = 16
TEAMS = 2
SH = 128
PPS = 32
GROUPS = 16
LOW = 22
NX = 45
XP = 24
NU = 45
PER = 4
ROWS = 136
DAMPING = 0.05
STEP = 64.0
f32, bf16 = jnp.float32, jnp.bfloat16
MESH = pl.DeviceIdType.MESH


def noll_index(j):
    n = 0
    remaining = j - 1
    while remaining > n:
        n += 1
        remaining -= n
    m = (-1) ** j * (n % 2 + 2 * ((remaining + (n + 1) % 2) // 2))
    return (n, m)


def zernike_values(row, col):
    radius = np.sqrt(row * row + col * col)
    angle = np.arctan2(row, col)
    values = []
    for j in range(2, MODES + 2):
        n, m = noll_index(j)
        k_abs = abs(m)
        radial = np.zeros_like(radius)
        for k in range((n - k_abs) // 2 + 1):
            factor = (
                (-1) ** k
                * math.factorial(n - k)
                / (
                    math.factorial(k)
                    * math.factorial((n + k_abs) // 2 - k)
                    * math.factorial((n - k_abs) // 2 - k)
                )
            )
            radial = radial + factor * radius ** (n - 2 * k)
        if m == 0:
            values.append(math.sqrt(n + 1) * radial)
        elif m > 0:
            values.append(math.sqrt(2 * (n + 1)) * radial * np.cos(k_abs * angle))
        else:
            values.append(math.sqrt(2 * (n + 1)) * radial * np.sin(k_abs * angle))
    return np.stack(values)


def ultraspherical(order, t):
    t = np.asarray(t, np.float64)
    inside = (np.arange(NX) + LOW - 44.0) / 22.0

    def raw(x):
        last, value = np.zeros_like(x), np.ones_like(x)
        for n in range(1, order + 1):
            last, value = value, (2.0 * (n + 2.0) * x * value - (n + 4.0) * last) / n
        return value

    weight = np.sqrt(1.0 - inside**2)
    return raw(t) / np.sqrt(np.sum(weight * raw(inside) ** 2) / np.sum(weight))


PAIRS = [(a, b) for a in range(9) for b in range(9 - a)]


def halves(table):
    hi = table.astype(np.float32).astype(ml_dtypes.bfloat16)
    lo = (table - hi.astype(np.float64)).astype(np.float32).astype(ml_dtypes.bfloat16)
    return hi, lo


def right_table(table):
    hi, lo = halves(table)
    return np.concatenate([hi, hi, lo], axis=0)


def left_table(table):
    hi, lo = halves(table)
    return np.concatenate([hi, hi, lo], axis=1)


@functools.lru_cache
def tables():
    w = 2.0 * np.pi / N
    full = np.arange(N)
    px = LOW + np.arange(NX)
    unit = (px - 44.0) / 22.0
    aperture = (unit[:, None] ** 2 + unit[None, :] ** 2 <= 1.0).astype(np.float64)
    a32 = ((px.astype(np.float32) - np.float32(44)) / np.float32(22)).astype(np.float32)
    r32 = np.sqrt(a32[:, None] * a32[:, None] + a32[None, :] * a32[None, :])
    assert np.array_equal(aperture, (r32 <= 1.0).astype(np.float64))
    scale = 1.0 / (N * N * aperture.sum())
    root = math.sqrt(scale)

    grid = np.linspace(-1.0, 1.0, 31)
    rows, cols = (g.ravel() for g in np.meshgrid(grid, grid, indexing="ij"))
    basis = np.stack([ultraspherical(a, rows) * ultraspherical(b, cols) for a, b in PAIRS], axis=1)
    fit = np.linalg.lstsq(basis, zernike_values(rows, cols).T, rcond=None)[0].T

    out = {}
    spread_ab = np.zeros((MODES, 128))
    spread_ab[:, : len(PAIRS)] = fit
    spread_ab[:, 64 : 64 + len(PAIRS)] = fit
    m1 = np.zeros((128, 128))
    m1[:MODES] = spread_ab
    out["m1"] = fine_table(m1)
    out["m2"] = fine_table(m1.T)

    along = np.zeros((XP, 128))
    mask = np.zeros((XP, 128))
    t3 = np.zeros((128, 128))
    for h in range(2):
        for k, (a, b) in enumerate(PAIRS):
            for i in range(XP):
                if i + XP * h < NX:
                    along[i, 64 * h + k] = ultraspherical(a, unit[i + XP * h])
            t3[64 * h + k, 64 * h : 64 * h + NX] = ultraspherical(b, unit)
        for i in range(XP):
            if i + XP * h < NX:
                mask[i, 64 * h : 64 * h + NX] = aperture[i + XP * h]
    out["along"] = np.repeat(along, ITEMS, axis=0).astype(np.float32)
    out["mask"] = np.repeat(mask, ITEMS, axis=0).astype(np.float32)
    out["t3"] = fine_table(t3)
    out["t18"] = fine_table(t3.T)

    ang = w * (np.outer(px, full) % N)
    c, s = np.cos(ang), np.sin(ang)
    t5p = np.zeros((128, 256))
    t5p[:NX, :N], t5p[64 : 64 + NX, :N] = c, s
    t5p[:NX, 128 : 128 + N], t5p[64 : 64 + NX, 128 : 128 + N] = -s, c
    out["t5p"] = right_table(t5p)
    t16p = np.zeros((256, 128))
    t16p[:N, :NX], t16p[128 : 128 + N, :NX] = c.T, -s.T
    t16p[:N, 64 : 64 + NX], t16p[128 : 128 + N, 64 : 64 + NX] = s.T, c.T
    hi, lo = halves(t16p)
    out["t16p"] = np.concatenate(
        [np.concatenate([hi, lo], axis=1), np.concatenate([hi, 0 * hi], axis=1)], axis=0
    )
    l7 = np.zeros((176, 96))
    l7[:N, :NX], l7[:N, 48 : 48 + NX] = c.T, s.T
    l7[N:, :NX], l7[N:, 48 : 48 + NX] = -s.T, c.T
    out["l7"] = left_table(l7 * root)
    l15 = np.zeros((96, 176))
    l15[:NX, :N], l15[:NX, N:] = c, -s
    l15[48 : 48 + NX, :N], l15[48 : 48 + NX, N:] = s, c
    out["l15"] = left_table(l15)

    ang = w * (np.outer(full, full) % N)
    c, s = np.cos(ang), np.sin(ang)
    t9 = np.zeros((128, 256))
    t9[:N, :N], t9[:N, 128 : 128 + N] = c, -s
    out["t9"] = right_table(t9)
    l10 = np.zeros((96, 176))
    l10[:NU, :N], l10[:NU, N:] = c[:NU], s[:NU]
    l10[48 : 48 + NU, :N], l10[48 : 48 + NU, N:] = -s[:NU], c[:NU]
    out["l10"] = left_table(l10)
    t12 = np.zeros((256, 256))
    t12[:N, :N], t12[128 : 128 + N, :N] = c, -s
    t12[:N, 128 : 128 + N], t12[128 : 128 + N, 128 : 128 + N] = s, c
    out["t12"] = right_table(t12)
    weight = np.full((NU,), 2.0)
    weight[0] = weight[44] = 1.0
    weight = weight * (-2.0) * 2.0 * root
    l13 = np.zeros((96, 96))
    l13[:N, :NU], l13[:N, 48 : 48 + NU] = c[:, :NU] * weight, -s[:, :NU] * weight
    out["l13"] = left_table(l13)

    profile = 0.5 - 0.5 * np.cos(2.0 * np.pi * (full + 0.5) / N)
    window = np.zeros((N, 128), np.float32)
    window[:, :N] = profile[:, None] * profile[None, :]
    out["window"] = window
    signed = (full + 44) % N - 44.0
    freq = np.zeros((2, 48, 128), np.float32)
    freq[0, :NU, :] = signed[:NU, None]
    freq[1, :, :N] = signed[None, :]
    out["freq"] = (freq * (-w)).astype(np.float32)

    flip = np.zeros((128, 128), ml_dtypes.bfloat16)
    for v in range(N):
        flip[(N - v) % N, v] = 1
    out["flip"] = np.concatenate([flip, flip], axis=0)
    place = np.zeros((176, 192), ml_dtypes.bfloat16)
    for u in range(N):
        if u < NU:
            place[u, u] = 1
            place[N + u, 48 + u] = 1
        else:
            place[u, 96 + N - u] = 1
            place[N + u, 144 + N - u] = -1
    out["place"] = np.concatenate([place, place], axis=1)
    return out


def fine_table(table):
    hi = table.astype(np.float32).astype(ml_dtypes.bfloat16)
    rest = table - hi.astype(np.float64)
    mid = rest.astype(np.float32).astype(ml_dtypes.bfloat16)
    low = (rest - mid.astype(np.float64)).astype(np.float32).astype(ml_dtypes.bfloat16)
    return np.concatenate([hi, hi, mid, mid, low, hi], axis=0)


def split(x):
    hi = x.astype(bf16)
    return hi, (x - hi.astype(f32)).astype(bf16)


def dot(a, b):
    return jnp.dot(a, b, preferred_element_type=f32)


def right(x, table):
    hi, lo = split(x)
    return dot(jnp.concatenate([hi, lo, hi], axis=1), table)


def fine(x, table):
    hi = x.astype(bf16)
    rest = x - hi.astype(f32)
    mid = rest.astype(bf16)
    low = (rest - mid.astype(f32)).astype(bf16)
    k = x.shape[1]
    t2 = jnp.concatenate([table[:k], table[2 * k : 3 * k]], axis=1)
    tl = table[4 * k : 5 * k]
    two = dot(jnp.concatenate([hi, mid], axis=1), jnp.concatenate([t2, t2], axis=0))
    rest = dot(jnp.concatenate([hi, low], axis=1), jnp.concatenate([tl, table[:k]], axis=0))
    return two[:, :128] + (two[:, 128:] + rest)


def left(table, x):
    hi, lo = split(x)
    k, m = x.shape[0], table.shape[0]
    if k > 128:
        t2 = jnp.concatenate([table[:, :k], table[:, 2 * k:]], axis=0)
        a = dot(t2, hi)
        return a[:m] + (a[m:] + dot(table[:, :k], lo))
    rest = jnp.concatenate([table[:, 2 * k:], jnp.zeros((m, k), bf16)], axis=1)
    a = dot(jnp.concatenate([table[:, :2 * k], rest], axis=0), jnp.concatenate([hi, lo], axis=0))
    return a[:m] + a[m:]


def sincos(x):
    k = jnp.floor(x * (2.0 / math.pi) + 0.5)
    r = x - k * 1.5703125
    r = r - k * 4.8351287841796875e-4
    r = r - k * 3.1385570764541626e-07
    z = r * r
    s = r + r * z * (-1.6666654611e-1 + z * (8.3321608736e-3 + z * -1.9515295891e-4))
    c = 1.0 - 0.5 * z + z * z * (
        4.166664568298827e-2 + z * (-1.388731625493765e-3 + z * 2.443315711809948e-5)
    )
    q = k.astype(jnp.int32)
    swap = (q & 1) == 1
    sin = jnp.where(swap, c, s)
    cos = jnp.where(swap, s, c)
    sin = jnp.where((q & 2) == 2, -sin, sin)
    cos = jnp.where(((q + 1) & 2) == 2, -cos, cos)
    return sin, cos


PACKS = {
    "narrow": ("m1", "m2", "t3", "t18", "flip"),
    "wide": ("t5p", "t16p", "t12", "t9"),
    "left96": ("l7", "l13"),
    "left176": ("l15", "l10"),
    "order": ("place",),
    "real": ("along", "mask", "window", "freq"),
}


@functools.lru_cache
def packed():
    arrays, where = [], {}
    for index, names in enumerate(PACKS.values()):
        rows = []
        for name in names:
            table = tables()[name]
            table = table.reshape(-1, table.shape[-1])
            where[name] = (index, sum(r.shape[0] for r in rows), table.shape[0])
            rows.append(table)
        arrays.append(np.concatenate(rows, axis=0))
    return arrays, where


def kernel(*refs):
    where = packed()[1]
    count = len(PACKS)
    frames, shifts_in, coefs_in, anchors_in, assign_in = refs[:5]
    packs_in = refs[5 : 5 + count]
    obj, out = refs[5 + count : 7 + count]
    packs = refs[7 + count : 7 + 2 * count]
    (
        shifts,
        coefs,
        anchors,
        assign,
        slots,
        strip,
        send,
        recv,
        csend,
        crecv,
        nsend,
        nrecv,
        esend,
        ramp,
        curs,
        pup,
        foc,
        tra,
        dat,
        ysc,
        asc,
        gsc,
        hsc,
        small_sem,
        pack_sem,
        load_sem,
        halo_send,
        halo_recv,
        msg_send,
        msg_recv,
        c_send,
        c_recv,
        n_send,
        n_recv,
        e_send,
        e_recv,
        e_own,
    ) = refs[7 + 2 * count :]

    def tab(name):
        index, start, rows = where[name]
        return packs[index][start : start + rows, :]

    me_frm, me_pat = lax.axis_index("frm"), lax.axis_index("pat")
    half, side = lax.div(me_pat, 2), lax.rem(me_pat, 2)
    loop = lax.fori_loop

    small = [
        pltpu.make_async_copy(a, b, small_sem.at[i])
        for i, (a, b) in enumerate(
            [(shifts_in, shifts), (coefs_in, coefs), (anchors_in, anchors), (assign_in, assign)]
        )
    ]
    for copy in small:
        copy.start()

    def load(t):
        return pltpu.make_async_copy(
            frames.at[0, :, pl.ds(pl.multiple_of(t * 128, 128), 128)],
            strip.at[t, pl.ds(0, SH), :],
            load_sem.at[t],
        )

    def start_load(t, _):
        load(t).start()
        return 0

    def end_load(t, _):
        load(t).wait()
        return 0

    loop(0, 16, start_load, 0)
    pack_loads = [
        pltpu.make_async_copy(packs_in[i], packs[i], pack_sem.at[i]) for i in range(count)
    ]
    for copy in pack_loads:
        copy.start()

    barrier = pltpu.get_barrier_semaphore()

    def tell(frm, pat):
        pl.semaphore_signal(
            barrier, inc=1, device_id={"frm": frm, "pat": pat}, device_id_type=MESH
        )

    def greet(q, _):
        @pl.when(q != me_frm)
        def _():
            tell(q, me_pat)

        return 0

    loop(0, FRAMES, greet, 0)

    @pl.when(me_pat < GROUPS - 1)
    def _():
        tell(me_frm, me_pat + 1)

    same = half == me_frm

    def greet_late(k, _):
        @pl.when(jnp.logical_not(same & (2 * me_frm + k == me_pat)))
        def _():
            tell(half, 2 * me_frm + k)

        return 0

    loop(0, 2, greet_late, 0)

    for copy in small:
        copy.wait()

    def order(g, _):
        first = jnp.int32(0)
        second = jnp.int32(0)
        for p in range(PPS - 1, -1, -1):
            hit = assign[p] == g
            second = jnp.where(hit, first, second)
            first = jnp.where(hit, p, first)
        slots[2 * g] = first
        slots[2 * g + 1] = second
        return 0

    loop(0, GROUPS, order, 0)

    def to_peer(source, target, send_sems, recv_sems, q):
        return pltpu.make_async_remote_copy(
            src_ref=source.at[q],
            dst_ref=target.at[me_frm],
            send_sem=send_sems.at[q],
            recv_sem=recv_sems.at[me_frm],
            device_id={"frm": q, "pat": me_pat},
            device_id_type=MESH,
        )

    def from_peer(source, target, send_sems, recv_sems, q):
        return pltpu.make_async_remote_copy(
            src_ref=source.at[q],
            dst_ref=target.at[q],
            send_sem=send_sems.at[q],
            recv_sem=recv_sems.at[q],
            device_id={"frm": q, "pat": me_pat},
            device_id_type=MESH,
        )

    csend[...] = jnp.zeros((FRAMES, 8, 128), f32)

    def fill_coefs(q, _):
        for j in range(PER):
            csend[q, j : j + 1, :MODES] = coefs[0, pl.ds(slots[PER * q + j], 1), :]
        for k in range(2):
            csend[q, PER + k : PER + k + 1, :] = jnp.zeros((1, 128), f32) + shifts[0, k]
        return 0

    loop(0, FRAMES, fill_coefs, 0)
    crecv[me_frm] = csend[me_frm]

    @pl.when(me_pat == GROUPS - 1)
    def _():
        strip[:, SH:, :] = jnp.zeros((16, N, 128), f32)

    loop(0, 16, end_load, 0)
    pl.semaphore_wait(
        barrier,
        FRAMES - 1 + (me_pat > 0).astype(jnp.int32) + 2 - same.astype(jnp.int32),
    )

    def send_coefs(i, _):
        to_peer(csend, crecv, c_send, c_recv, lax.rem(me_frm + i, FRAMES)).start()
        return 0

    loop(1, FRAMES, send_coefs, 0)

    halo = pltpu.make_async_remote_copy(
        src_ref=strip.at[:, pl.ds(0, N), :],
        dst_ref=strip.at[:, pl.ds(SH, N), :],
        send_sem=halo_send,
        recv_sem=halo_recv,
        device_id={"frm": me_frm, "pat": jnp.maximum(me_pat - 1, 0)},
        device_id_type=MESH,
    )

    @pl.when(me_pat > 0)
    def _():
        halo.start()

    for copy in pack_loads:
        copy.wait()

    def take(source, target, send_sems, recv_sems):
        def one(i, _):
            q = lax.rem(me_frm + i, FRAMES)
            from_peer(source, target, send_sems, recv_sems, q).wait_recv()
            return 0

        loop(1, FRAMES, one, 0)

    def drain(source, target, send_sems, recv_sems):
        def one(i, _):
            q = lax.rem(me_frm + i, FRAMES)
            to_peer(source, target, send_sems, recv_sems, q).wait_send()
            return 0

        loop(1, FRAMES, one, 0)

    take(csend, crecv, c_send, c_recv)
    for b in range(TEAMS):
        curs[b] = jnp.concatenate(
            [crecv[f, 2 * b + i : 2 * b + i + 1, :] for i in range(2) for f in range(FRAMES)],
            axis=0,
        )
    freq = tab("freq")

    def make_ramp(f, _):
        angle = freq[:48] * crecv[f, PER : PER + 1, :] + freq[48:] * crecv[f, PER + 1 : PER + 2, :]
        sin, cos = sincos(angle)
        ramp[f, 0] = cos
        ramp[f, 1] = sin
        return 0

    loop(0, FRAMES, make_ramp, 0)

    def half_spectra(values):
        asc[...] = right(values, tab("t9"))
        for f in range(0, ITEMS, 2):
            stacked = []
            for g in (f, f + 1):
                part = asc[g * N : (g + 1) * N, :]
                stacked.append(jnp.concatenate([part[:, :128], part[:, 128:]], axis=0))
            both = left(tab("l10"), jnp.concatenate(stacked, axis=1))
            yield f, both[:, :128]
            yield f + 1, both[:, 128:]

    low_lanes = lax.broadcasted_iota(jnp.int32, (XP * ITEMS, 128), 1) < 64

    def forward(b):
        cab = fine(curs[b], tab("m1"))
        phase = fine(jnp.concatenate([cab] * XP, axis=0) * tab("along"), tab("t3"))
        sin, cos = sincos(phase)
        mask = tab("mask")
        pr, pi = cos * mask, sin * mask
        pup[b, 0] = pr
        pup[b, 1] = pi
        for h in range(2):
            if h == 0:
                mix = jnp.where(low_lanes, pr, pltpu.roll(pi, 64, 1))
            else:
                mix = jnp.where(low_lanes, pltpu.roll(pr, 64, 1), pi)
            both = right(mix, tab("t5p"))
            ysc[h] = both[:, :128]
            ysc[2 + h] = both[:, 128:]
        spreads = []
        for f in range(0, ITEMS, 2):
            pair = []
            for g in (f, f + 1):
                pair.append(
                    jnp.concatenate([ysc[h, pl.ds(g, XP, ITEMS), :] for h in range(4)], axis=0)
                )
            both = left(tab("l7"), jnp.concatenate(pair, axis=1))
            for g in (0, 1):
                one = both[:, 128 * g : 128 * g + 128]
                foc[b, f + g] = one
                spreads.append(one[:N] * one[:N] + one[N:] * one[N:])
        for f, one in half_spectra(jnp.concatenate(spreads, axis=0)):
            tra[b, f] = one

    def estimate(j):
        return pltpu.make_async_remote_copy(
            src_ref=esend.at[j],
            dst_ref=obj.at[2 * side + lax.rem(j, 2)],
            send_sem=e_send.at[j],
            recv_sem=e_recv.at[2 * side + lax.rem(j, 2)],
            device_id={"frm": half, "pat": 2 * me_frm + lax.div(j, 2)},
            device_id_type=MESH,
        )

    def estimate_here(j):
        return pltpu.make_async_copy(
            esend.at[j], obj.at[2 * side + lax.rem(j, 2)], e_own.at[j]
        )

    def estimate_stays(j):
        return same & (2 * me_frm + lax.div(j, 2) == me_pat)

    def fill_estimate(j, ere, eim):
        spectrum = jnp.concatenate([ere, eim], axis=0) * (1.0 / N)
        hi, lo = split(spectrum)
        flipped = dot(jnp.concatenate([hi, lo], axis=1), tab("flip"))
        hi, lo = split(jnp.concatenate([spectrum, flipped], axis=0))
        whole = dot(tab("place"), jnp.concatenate([hi, lo], axis=0))
        esend[j, 0] = whole[:N]
        esend[j, 1] = whole[N:]

    def send_estimate(j):
        @pl.when(jnp.logical_not(estimate_stays(j)))
        def _():
            estimate(j).start()

        @pl.when(estimate_stays(j))
        def _():
            estimate_here(j).start()

    def backward(b, step, last):
        for i in range(2):
            cre = jnp.zeros((48, 128), f32)
            cim = jnp.zeros((48, 128), f32)
            den = jnp.full((48, 128), DAMPING, f32)
            for f in range(FRAMES * i, FRAMES * (i + 1)):
                tre, tim = tra[b, f, :48], tra[b, f, 48:]
                dre, dim = dat[f, :48], dat[f, 48:]
                cre = cre + (dre * tre + dim * tim)
                cim = cim + (dim * tre - dre * tim)
                den = den + (tre * tre + tim * tim)
            ere, eim = cre / den, cim / den
            for f in range(FRAMES * i, FRAMES * (i + 1)):
                tre, tim = tra[b, f, :48], tra[b, f, 48:]
                mre = dat[f, :48] - (ere * tre - eim * tim)
                mim = dat[f, 48:] - (ere * tim + eim * tre)
                gsc[f * 48 : f * 48 + 48, :128] = ere * mre + eim * mim
                gsc[f * 48 : f * 48 + 48, 128:] = ere * mim - eim * mre
            if last:
                fill_estimate(2 * b + i, ere, eim)
        if last:
            send_estimate(2 * b)
            send_estimate(2 * b + 1)
        gsc[...] = right(gsc[...], tab("t12"))
        for f in range(0, ITEMS, 2):
            pair = []
            for g in (f, f + 1):
                part = gsc[g * 48 : g * 48 + 48, :]
                pair.append(jnp.concatenate([part[:, :128], part[:, 128:]], axis=0))
            grad = left(tab("l13"), jnp.concatenate(pair, axis=1))[:N]
            pair = []
            for g in (0, 1):
                one = grad[:, 128 * g : 128 * g + 128]
                pair.append(
                    jnp.concatenate([one * foc[b, f + g, :N], one * foc[b, f + g, N:]], axis=0)
                )
            both = left(tab("l15"), jnp.concatenate(pair, axis=1))
            for g in (0, 1):
                re, im = (both[k : k + 48, 128 * g : 128 * g + 128] for k in (0, 48))
                for h in range(2):
                    rows = slice(XP * h, XP * h + XP)
                    hsc[2 * h, pl.ds(f + g, XP, ITEMS), :] = re[rows]
                    hsc[2 * h + 1, pl.ds(f + g, XP, ITEMS), :] = im[rows]
        sides = []
        for h in range(2):
            hi, lo = split(jnp.concatenate([hsc[2 * h], hsc[2 * h + 1]], axis=1))
            one = dot(jnp.concatenate([hi, lo], axis=1), tab("t16p"))
            sides.append(one[:, :128] + one[:, 128:])
        gre = jnp.where(low_lanes, sides[0], pltpu.roll(sides[1], 64, 1))
        gim = jnp.where(low_lanes, pltpu.roll(sides[0], 64, 1), sides[1])
        grad = gim * pup[b, 0] - gre * pup[b, 1]
        gab = fine(grad, tab("t18")) * tab("along")
        acc = gab[:ITEMS]
        for i in range(1, XP):
            acc = acc + gab[i * ITEMS : (i + 1) * ITEMS]
        curs[b] = curs[b] - step * fine(acc, tab("m2"))

    def first_half(j, _):
        forward(j)
        return 0

    @pl.when(me_pat < GROUPS - 1)
    def _():
        halo.wait_recv()

    lane = lax.broadcasted_iota(jnp.int32, (N, 128), 1)
    top = me_pat * SH

    def pixels(b, q):
        return pltpu.make_async_remote_copy(
            src_ref=send.at[b, q],
            dst_ref=recv.at[b, me_frm],
            send_sem=msg_send.at[b, q],
            recv_sem=msg_recv.at[b, me_frm],
            device_id={"frm": q, "pat": me_pat},
            device_id_type=MESH,
        )

    def pixels_from(b, q):
        return pltpu.make_async_remote_copy(
            src_ref=send.at[b, q],
            dst_ref=recv.at[b, q],
            send_sem=msg_send.at[b, q],
            recv_sem=msg_recv.at[b, q],
            device_id={"frm": q, "pat": me_pat},
            device_id_type=MESH,
        )

    def patch(slot):
        p = slots[slot]
        row = jnp.clip(anchors[0, p] - top, 0, SH - 1)
        col = anchors[1, p]
        tile = jnp.clip(lax.shift_right_logical(col, 7), 0, 15)
        off = col & 127
        a = strip[tile, pl.ds(row, N), :]
        b = strip[jnp.minimum(tile + 1, 15), pl.ds(row, N), :]
        turn = (128 - off) & 127
        return jnp.where(lane < 128 - off, pltpu.roll(a, turn, 1), pltpu.roll(b, turn, 1))

    def cut(n, _):
        b, q = lax.div(n, FRAMES), lax.rem(me_frm + 1 + lax.rem(n, FRAMES), FRAMES)
        one = patch(PER * q + 2 * b)
        two = pltpu.roll(patch(PER * q + 2 * b + 1), N, 1)
        upper = jnp.where(lane < N, one, two)
        lower = jnp.where(
            lane[:48] < 64,
            two[:48],
            pltpu.roll(jnp.concatenate([two[48:], two[80:]], axis=0), 64, 1),
        )

        @pl.when(q != me_frm)
        def _():
            send[b, q, :N] = upper
            send[b, q, N:] = lower
            pixels(b, q).start()

        @pl.when(q == me_frm)
        def _():
            recv[b, me_frm, :N] = upper
            recv[b, me_frm, N:] = lower

        return 0

    loop(0, TEAMS * FRAMES, cut, 0)
    loop(0, TEAMS, first_half, 0)

    def work(b, _):
        def arrived(i, _):
            pixels_from(b, lax.rem(me_frm + i, FRAMES)).wait_recv()
            return 0

        loop(1, FRAMES, arrived, 0)
        window = tab("window")
        parts, steps = [], []
        for i in range(2):
            total = jnp.zeros((N, 128), f32)
            for f in range(FRAMES):
                if i == 0:
                    part = recv[b, f, :N]
                else:
                    rest = recv[b, f, N:]
                    part = jnp.concatenate([rest, pltpu.roll(rest, 64, 1)[:40]], axis=0)
                    part = pltpu.roll(jnp.where(lane < N, part, recv[b, f, :N]), 40, 1)
                part = jnp.where(lane < N, part, 0.0) * window
                total = total + part * part
                parts.append(part)
            energy = jnp.sum(total) * float(N * N)
            steps.append((STEP * FRAMES) / (jnp.zeros((FRAMES, 128), f32) + energy))
        for f, one in half_spectra(jnp.concatenate(parts, axis=0)):
            re, im = one[:48], one[48:]
            cos, sin = ramp[f % FRAMES, 0], ramp[f % FRAMES, 1]
            dat[f, :48] = re * cos - im * sin
            dat[f, 48:] = re * sin + im * cos
        step = jnp.concatenate(steps, axis=0)
        for t in range(ITERS):
            if t > 0:
                forward(b)
            backward(b, step, t == ITERS - 1)
        for i in range(2):
            for f in range(FRAMES):
                row = FRAMES * i + f
                nsend[f, pl.ds(2 * b + i, 1), :] = curs[b, row : row + 1, :]
        return 0

    nsend[...] = jnp.zeros((FRAMES, 8, 128), f32)
    loop(0, TEAMS, work, 0)

    def give(i, _):
        q = lax.rem(me_frm + i, FRAMES)
        to_peer(nsend, nrecv, n_send, n_recv, q).start()
        return 0

    loop(1, FRAMES, give, 0)
    nrecv[me_frm] = nsend[me_frm]

    def end_estimate(j, _):
        stays = estimate_stays(j)

        @pl.when(jnp.logical_not(stays))
        def _():
            estimate(j).wait_send()

        @pl.when(stays)
        def _():
            estimate_here(j).wait()

        return 0

    def end_pixels(n, _):
        j, q = lax.div(n, FRAMES), lax.rem(n, FRAMES)

        @pl.when(q != me_frm)
        def _():
            pixels(j, q).wait_send()

        return 0

    loop(0, TEAMS * FRAMES, end_pixels, 0)
    drain(csend, crecv, c_send, c_recv)

    @pl.when(me_pat > 0)
    def _():
        halo.wait_send()

    take(nsend, nrecv, n_send, n_recv)

    out[...] = jnp.zeros((PPS, 128), f32)
    lane1 = lax.broadcasted_iota(jnp.int32, (PPS, 1), 0)

    def place_back(n, _):
        row = nrecv[lax.div(n, PER), pl.ds(lax.rem(n, PER), 1), :]
        out[...] = jnp.where(lane1 == slots[n], row, out[...])
        return 0

    loop(0, PPS, place_back, 0)
    loop(0, PER, end_estimate, 0)
    drain(nsend, nrecv, n_send, n_recv)

    def estimate_from(k, _):
        source = 2 * me_frm + lax.div(k, 2)

        @pl.when(jnp.logical_not(same & (source == me_pat)))
        def _():
            pltpu.make_async_remote_copy(
                src_ref=esend.at[k],
                dst_ref=obj.at[k],
                send_sem=e_send.at[k],
                recv_sem=e_recv.at[k],
                device_id={"frm": half, "pat": source},
                device_id_type=MESH,
            ).wait_recv()

        return 0

    loop(0, 4, estimate_from, 0)


def shards(frames, shifts, coefficients, anchors, assign):
    arrays = packed()[0]
    hbm = pl.BlockSpec(memory_space=pltpu.HBM)
    sems = pltpu.SemaphoreType.DMA
    obj, new = pl.pallas_call(
        kernel,
        in_specs=[hbm] * (5 + len(arrays)),
        out_specs=[hbm, pl.BlockSpec(memory_space=pltpu.VMEM)],
        out_shape=[
            jax.ShapeDtypeStruct((PER, 2, N, 128), f32),
            jax.ShapeDtypeStruct((PPS, 128), f32),
        ],
        scratch_shapes=[pltpu.VMEM(a.shape, a.dtype) for a in arrays]
        + [
            pltpu.SMEM((1, 2), f32),
            pltpu.VMEM((1, PPS, MODES), f32),
            pltpu.SMEM((2, PPS), jnp.int32),
            pltpu.SMEM((PPS,), jnp.int32),
            pltpu.SMEM((PPS,), jnp.int32),
            pltpu.VMEM((16, SH + N, 128), f32),
            pltpu.VMEM((TEAMS, FRAMES, ROWS, 128), f32),
            pltpu.VMEM((TEAMS, FRAMES, ROWS, 128), f32),
            pltpu.VMEM((FRAMES, 8, 128), f32),
            pltpu.VMEM((FRAMES, 8, 128), f32),
            pltpu.VMEM((FRAMES, 8, 128), f32),
            pltpu.VMEM((FRAMES, 8, 128), f32),
            pltpu.VMEM((PER, 2, N, 128), f32),
            pltpu.VMEM((FRAMES, 2, 48, 128), f32),
            pltpu.VMEM((TEAMS, ITEMS, 128), f32),
            pltpu.VMEM((TEAMS, 2, XP * ITEMS, 128), f32),
            pltpu.VMEM((TEAMS, ITEMS, 176, 128), f32),
            pltpu.VMEM((TEAMS, ITEMS, 96, 128), f32),
            pltpu.VMEM((ITEMS, 96, 128), f32),
            pltpu.VMEM((4, XP * ITEMS, 128), f32),
            pltpu.VMEM((ITEMS * N, 256), f32),
            pltpu.VMEM((ITEMS * 48, 256), f32),
            pltpu.VMEM((4, XP * ITEMS, 128), f32),
            sems((4,)),
            sems((len(arrays),)),
            sems((16,)),
            sems,
            sems,
            sems((TEAMS, FRAMES)),
            sems((TEAMS, FRAMES)),
            sems((FRAMES,)),
            sems((FRAMES,)),
            sems((FRAMES,)),
            sems((FRAMES,)),
            sems((PER,)),
            sems((PER,)),
            sems((PER,)),
        ],
        compiler_params=pltpu.CompilerParams(
            collective_id=0, has_side_effects=True, vmem_limit_bytes=56 << 20
        ),
        name="deconvolve",
    )(frames, shifts, coefficients, anchors.T, assign, *[jnp.asarray(a) for a in arrays])
    return new[None, :, :MODES], obj[:, :, :, :N].reshape(PER, 2, N * N)


def solution(mesh):
    in_specs = (
        P("frm", "pat", None),
        P("frm", None),
        P("frm", "pat", None),
        P("pat", None),
        P("pat"),
    )
    out_specs = (P("frm", "pat", None), P(("pat", "frm"), None, None))
    return jax.shard_map(shards, mesh=mesh, in_specs=in_specs, out_specs=out_specs, check_vma=False)
```

```python
import functools
import math

import jax
import jax.numpy as jnp
import ml_dtypes
import numpy as np
from jax import lax
from jax.experimental import pallas as pl
from jax.experimental.pallas import tpu as pltpu
from jax.sharding import PartitionSpec as P

N = 88
MODES = 40
ITERS = 2
FRAMES = 8
ITEMS = 16
TEAMS = 2
SH = 128
PPS = 32
GROUPS = 16
LOW = 22
NX = 45
XP = 24
NU = 45
PER = 4
ROWS = 136
DAMPING = 0.05
STEP = 64.0
f32, bf16 = jnp.float32, jnp.bfloat16
MESH = pl.DeviceIdType.MESH


def noll_index(j):
    n = 0
    remaining = j - 1
    while remaining > n:
        n += 1
        remaining -= n
    m = (-1) ** j * (n % 2 + 2 * ((remaining + (n + 1) % 2) // 2))
    return (n, m)


def zernike_values(row, col):
    radius = np.sqrt(row * row + col * col)
    angle = np.arctan2(row, col)
    values = []
    for j in range(2, MODES + 2):
        n, m = noll_index(j)
        k_abs = abs(m)
        radial = np.zeros_like(radius)
        for k in range((n - k_abs) // 2 + 1):
            factor = (
                (-1) ** k
                * math.factorial(n - k)
                / (
                    math.factorial(k)
                    * math.factorial((n + k_abs) // 2 - k)
                    * math.factorial((n - k_abs) // 2 - k)
                )
            )
            radial = radial + factor * radius ** (n - 2 * k)
        if m == 0:
            values.append(math.sqrt(n + 1) * radial)
        elif m > 0:
            values.append(math.sqrt(2 * (n + 1)) * radial * np.cos(k_abs * angle))
        else:
            values.append(math.sqrt(2 * (n + 1)) * radial * np.sin(k_abs * angle))
    return np.stack(values)


def ultraspherical(order, t):
    t = np.asarray(t, np.float64)
    inside = (np.arange(NX) + LOW - 44.0) / 22.0

    def raw(x):
        last, value = np.zeros_like(x), np.ones_like(x)
        for n in range(1, order + 1):
            last, value = value, (2.0 * (n + 2.0) * x * value - (n + 4.0) * last) / n
        return value

    weight = np.sqrt(1.0 - inside**2)
    return raw(t) / np.sqrt(np.sum(weight * raw(inside) ** 2) / np.sum(weight))


PAIRS = [(a, b) for a in range(9) for b in range(9 - a)]


def halves(table):
    hi = table.astype(np.float32).astype(ml_dtypes.bfloat16)
    lo = (table - hi.astype(np.float64)).astype(np.float32).astype(ml_dtypes.bfloat16)
    return hi, lo


def right_table(table):
    hi, lo = halves(table)
    return np.concatenate([hi, hi, lo], axis=0)


def left_table(table):
    hi, lo = halves(table)
    return np.concatenate([hi, hi, lo], axis=1)


@functools.lru_cache
def tables():
    w = 2.0 * np.pi / N
    full = np.arange(N)
    px = LOW + np.arange(NX)
    unit = (px - 44.0) / 22.0
    aperture = (unit[:, None] ** 2 + unit[None, :] ** 2 <= 1.0).astype(np.float64)
    a32 = ((px.astype(np.float32) - np.float32(44)) / np.float32(22)).astype(np.float32)
    r32 = np.sqrt(a32[:, None] * a32[:, None] + a32[None, :] * a32[None, :])
    assert np.array_equal(aperture, (r32 <= 1.0).astype(np.float64))
    scale = 1.0 / (N * N * aperture.sum())
    root = math.sqrt(scale)

    grid = np.linspace(-1.0, 1.0, 31)
    rows, cols = (g.ravel() for g in np.meshgrid(grid, grid, indexing="ij"))
    basis = np.stack([ultraspherical(a, rows) * ultraspherical(b, cols) for a, b in PAIRS], axis=1)
    fit = np.linalg.lstsq(basis, zernike_values(rows, cols).T, rcond=None)[0].T

    out = {}
    spread_ab = np.zeros((MODES, 128))
    spread_ab[:, : len(PAIRS)] = fit
    spread_ab[:, 64 : 64 + len(PAIRS)] = fit
    m1 = np.zeros((128, 128))
    m1[:MODES] = spread_ab
    out["m1"] = fine_table(m1)
    out["m2"] = fine_table(m1.T)

    along = np.zeros((XP, 128))
    mask = np.zeros((XP, 128))
    t3 = np.zeros((128, 128))
    for h in range(2):
        for k, (a, b) in enumerate(PAIRS):
            for i in range(XP):
                if i + XP * h < NX:
                    along[i, 64 * h + k] = ultraspherical(a, unit[i + XP * h])
            t3[64 * h + k, 64 * h : 64 * h + NX] = ultraspherical(b, unit)
        for i in range(XP):
            if i + XP * h < NX:
                mask[i, 64 * h : 64 * h + NX] = aperture[i + XP * h]
    out["along"] = np.repeat(along, ITEMS, axis=0).astype(np.float32)
    out["mask"] = np.repeat(mask, ITEMS, axis=0).astype(np.float32)
    out["t3"] = fine_table(t3)
    out["t18"] = fine_table(t3.T)

    ang = w * (np.outer(px, full) % N)
    c, s = np.cos(ang), np.sin(ang)
    t5p = np.zeros((128, 256))
    t5p[:NX, :N], t5p[64 : 64 + NX, :N] = c, s
    t5p[:NX, 128 : 128 + N], t5p[64 : 64 + NX, 128 : 128 + N] = -s, c
    out["t5p"] = right_table(t5p)
    t16p = np.zeros((256, 128))
    t16p[:N, :NX], t16p[128 : 128 + N, :NX] = c.T, -s.T
    t16p[:N, 64 : 64 + NX], t16p[128 : 128 + N, 64 : 64 + NX] = s.T, c.T
    hi, lo = halves(t16p)
    out["t16p"] = np.concatenate(
        [np.concatenate([hi, lo], axis=1), np.concatenate([hi, 0 * hi], axis=1)], axis=0
    )
    l7 = np.zeros((176, 96))
    l7[:N, :NX], l7[:N, 48 : 48 + NX] = c.T, s.T
    l7[N:, :NX], l7[N:, 48 : 48 + NX] = -s.T, c.T
    out["l7"] = left_table(l7 * root)
    l15 = np.zeros((96, 176))
    l15[:NX, :N], l15[:NX, N:] = c, -s
    l15[48 : 48 + NX, :N], l15[48 : 48 + NX, N:] = s, c
    out["l15"] = left_table(l15)

    ang = w * (np.outer(full, full) % N)
    c, s = np.cos(ang), np.sin(ang)
    t9 = np.zeros((128, 256))
    t9[:N, :N], t9[:N, 128 : 128 + N] = c, -s
    out["t9"] = right_table(t9)
    l10 = np.zeros((96, 176))
    l10[:NU, :N], l10[:NU, N:] = c[:NU], s[:NU]
    l10[48 : 48 + NU, :N], l10[48 : 48 + NU, N:] = -s[:NU], c[:NU]
    out["l10"] = left_table(l10)
    t12 = np.zeros((256, 256))
    t12[:N, :N], t12[128 : 128 + N, :N] = c, -s
    t12[:N, 128 : 128 + N], t12[128 : 128 + N, 128 : 128 + N] = s, c
    out["t12"] = right_table(t12)
    weight = np.full((NU,), 2.0)
    weight[0] = weight[44] = 1.0
    weight = weight * (-2.0) * 2.0 * root
    l13 = np.zeros((96, 96))
    l13[:N, :NU], l13[:N, 48 : 48 + NU] = c[:, :NU] * weight, -s[:, :NU] * weight
    out["l13"] = left_table(l13)

    profile = 0.5 - 0.5 * np.cos(2.0 * np.pi * (full + 0.5) / N)
    window = np.zeros((N, 128), np.float32)
    window[:, :N] = profile[:, None] * profile[None, :]
    out["window"] = window
    signed = (full + 44) % N - 44.0
    freq = np.zeros((2, 48, 128), np.float32)
    freq[0, :NU, :] = signed[:NU, None]
    freq[1, :, :N] = signed[None, :]
    out["freq"] = (freq * (-w)).astype(np.float32)

    flip = np.zeros((128, 128), ml_dtypes.bfloat16)
    for v in range(N):
        flip[(N - v) % N, v] = 1
    out["flip"] = np.concatenate([flip, flip], axis=0)
    place = np.zeros((176, 192), ml_dtypes.bfloat16)
    for u in range(N):
        if u < NU:
            place[u, u] = 1
            place[N + u, 48 + u] = 1
        else:
            place[u, 96 + N - u] = 1
            place[N + u, 144 + N - u] = -1
    out["place"] = np.concatenate([place, place], axis=1)
    return out


def fine_table(table):
    hi = table.astype(np.float32).astype(ml_dtypes.bfloat16)
    rest = table - hi.astype(np.float64)
    mid = rest.astype(np.float32).astype(ml_dtypes.bfloat16)
    low = (rest - mid.astype(np.float64)).astype(np.float32).astype(ml_dtypes.bfloat16)
    return np.concatenate([hi, hi, mid, mid, low, hi], axis=0)


def split(x):
    hi = x.astype(bf16)
    return hi, (x - hi.astype(f32)).astype(bf16)


def dot(a, b):
    return jnp.dot(a, b, preferred_element_type=f32)


def right(x, table):
    hi, lo = split(x)
    return dot(jnp.concatenate([hi, lo, hi], axis=1), table)


def fine(x, table):
    hi = x.astype(bf16)
    rest = x - hi.astype(f32)
    mid = rest.astype(bf16)
    low = (rest - mid.astype(f32)).astype(bf16)
    k = x.shape[1]
    t2 = jnp.concatenate([table[:k], table[2 * k : 3 * k]], axis=1)
    tl = table[4 * k : 5 * k]
    two = dot(jnp.concatenate([hi, mid], axis=1), jnp.concatenate([t2, t2], axis=0))
    rest = dot(jnp.concatenate([hi, low], axis=1), jnp.concatenate([tl, table[:k]], axis=0))
    return two[:, :128] + (two[:, 128:] + rest)


def left(table, x):
    hi, lo = split(x)
    k, m = x.shape[0], table.shape[0]
    if k > 128:
        t2 = jnp.concatenate([table[:, :k], table[:, 2 * k:]], axis=0)
        a = dot(t2, hi)
        return a[:m] + (a[m:] + dot(table[:, :k], lo))
    rest = jnp.concatenate([table[:, 2 * k:], jnp.zeros((m, k), bf16)], axis=1)
    a = dot(jnp.concatenate([table[:, :2 * k], rest], axis=0), jnp.concatenate([hi, lo], axis=0))
    return a[:m] + a[m:]


def sincos(x):
    k = jnp.floor(x * (2.0 / math.pi) + 0.5)
    r = x - k * 1.5703125
    r = r - k * 4.8351287841796875e-4
    r = r - k * 3.1385570764541626e-07
    z = r * r
    s = r + r * z * (-1.6666654611e-1 + z * (8.3321608736e-3 + z * -1.9515295891e-4))
    c = 1.0 - 0.5 * z + z * z * (
        4.166664568298827e-2 + z * (-1.388731625493765e-3 + z * 2.443315711809948e-5)
    )
    q = k.astype(jnp.int32)
    swap = (q & 1) == 1
    sin = jnp.where(swap, c, s)
    cos = jnp.where(swap, s, c)
    sin = jnp.where((q & 2) == 2, -sin, sin)
    cos = jnp.where(((q + 1) & 2) == 2, -cos, cos)
    return sin, cos


PACKS = {
    "narrow": ("m1", "m2", "t3", "t18", "flip"),
    "wide": ("t5p", "t16p", "t12", "t9"),
    "left96": ("l7", "l13"),
    "left176": ("l15", "l10"),
    "order": ("place",),
    "real": ("along", "mask", "window", "freq"),
}


@functools.lru_cache
def packed():
    arrays, where = [], {}
    for index, names in enumerate(PACKS.values()):
        rows = []
        for name in names:
            table = tables()[name]
            table = table.reshape(-1, table.shape[-1])
            where[name] = (index, sum(r.shape[0] for r in rows), table.shape[0])
            rows.append(table)
        arrays.append(np.concatenate(rows, axis=0))
    return arrays, where


def kernel(*refs):
    where = packed()[1]
    count = len(PACKS)
    frames, shifts_in, coefs_in, anchors_in, assign_in = refs[:5]
    packs_in = refs[5 : 5 + count]
    obj, out = refs[5 + count : 7 + count]
    packs = refs[7 + count : 7 + 2 * count]
    (
        shifts,
        coefs,
        anchors,
        assign,
        slots,
        strip,
        send,
        recv,
        csend,
        crecv,
        nsend,
        nrecv,
        esend,
        ramp,
        curs,
        pup,
        foc,
        tra,
        dat,
        ysc,
        asc,
        gsc,
        hsc,
        small_sem,
        pack_sem,
        load_sem,
        halo_send,
        halo_recv,
        msg_send,
        msg_recv,
        c_send,
        c_recv,
        n_send,
        n_recv,
        e_send,
        e_recv,
        e_own,
    ) = refs[7 + 2 * count :]

    def tab(name):
        index, start, rows = where[name]
        return packs[index][start : start + rows, :]

    me_frm, me_pat = lax.axis_index("frm"), lax.axis_index("pat")
    half, side = lax.div(me_pat, 2), lax.rem(me_pat, 2)
    loop = lax.fori_loop

    small = [
        pltpu.make_async_copy(a, b, small_sem.at[i])
        for i, (a, b) in enumerate(
            [(shifts_in, shifts), (coefs_in, coefs), (anchors_in, anchors), (assign_in, assign)]
        )
    ]
    for copy in small:
        copy.start()

    def load(t):
        return pltpu.make_async_copy(
            frames.at[0, :, pl.ds(pl.multiple_of(t * 128, 128), 128)],
            strip.at[t, pl.ds(0, SH), :],
            load_sem.at[t],
        )

    def start_load(t, _):
        load(t).start()
        return 0

    def end_load(t, _):
        load(t).wait()
        return 0

    loop(0, 16, start_load, 0)
    pack_loads = [
        pltpu.make_async_copy(packs_in[i], packs[i], pack_sem.at[i]) for i in range(count)
    ]
    for copy in pack_loads:
        copy.start()

    barrier = pltpu.get_barrier_semaphore()

    def tell(frm, pat):
        pl.semaphore_signal(
            barrier, inc=1, device_id={"frm": frm, "pat": pat}, device_id_type=MESH
        )

    def greet(q, _):
        @pl.when(q != me_frm)
        def _():
            tell(q, me_pat)

        return 0

    loop(0, FRAMES, greet, 0)

    @pl.when(me_pat < GROUPS - 1)
    def _():
        tell(me_frm, me_pat + 1)

    same = half == me_frm

    def greet_late(k, _):
        @pl.when(jnp.logical_not(same & (2 * me_frm + k == me_pat)))
        def _():
            tell(half, 2 * me_frm + k)

        return 0

    loop(0, 2, greet_late, 0)

    for copy in small:
        copy.wait()

    def order(g, _):
        first = jnp.int32(0)
        second = jnp.int32(0)
        for p in range(PPS - 1, -1, -1):
            hit = assign[p] == g
            second = jnp.where(hit, first, second)
            first = jnp.where(hit, p, first)
        slots[2 * g] = first
        slots[2 * g + 1] = second
        return 0

    loop(0, GROUPS, order, 0)

    def to_peer(source, target, send_sems, recv_sems, q):
        return pltpu.make_async_remote_copy(
            src_ref=source.at[q],
            dst_ref=target.at[me_frm],
            send_sem=send_sems.at[q],
            recv_sem=recv_sems.at[me_frm],
            device_id={"frm": q, "pat": me_pat},
            device_id_type=MESH,
        )

    def from_peer(source, target, send_sems, recv_sems, q):
        return pltpu.make_async_remote_copy(
            src_ref=source.at[q],
            dst_ref=target.at[q],
            send_sem=send_sems.at[q],
            recv_sem=recv_sems.at[q],
            device_id={"frm": q, "pat": me_pat},
            device_id_type=MESH,
        )

    csend[...] = jnp.zeros((FRAMES, 8, 128), f32)

    def fill_coefs(q, _):
        for j in range(PER):
            csend[q, j : j + 1, :MODES] = coefs[0, pl.ds(slots[PER * q + j], 1), :]
        for k in range(2):
            csend[q, PER + k : PER + k + 1, :] = jnp.zeros((1, 128), f32) + shifts[0, k]
        return 0

    loop(0, FRAMES, fill_coefs, 0)
    crecv[me_frm] = csend[me_frm]

    @pl.when(me_pat == GROUPS - 1)
    def _():
        strip[:, SH:, :] = jnp.zeros((16, N, 128), f32)

    loop(0, 16, end_load, 0)
    pl.semaphore_wait(
        barrier,
        FRAMES - 1 + (me_pat > 0).astype(jnp.int32) + 2 - same.astype(jnp.int32),
    )

    def send_coefs(i, _):
        to_peer(csend, crecv, c_send, c_recv, lax.rem(me_frm + i, FRAMES)).start()
        return 0

    loop(1, FRAMES, send_coefs, 0)

    halo = pltpu.make_async_remote_copy(
        src_ref=strip.at[:, pl.ds(0, N), :],
        dst_ref=strip.at[:, pl.ds(SH, N), :],
        send_sem=halo_send,
        recv_sem=halo_recv,
        device_id={"frm": me_frm, "pat": jnp.maximum(me_pat - 1, 0)},
        device_id_type=MESH,
    )

    @pl.when(me_pat > 0)
    def _():
        halo.start()

    for copy in pack_loads:
        copy.wait()

    def take(source, target, send_sems, recv_sems):
        def one(i, _):
            q = lax.rem(me_frm + i, FRAMES)
            from_peer(source, target, send_sems, recv_sems, q).wait_recv()
            return 0

        loop(1, FRAMES, one, 0)

    def drain(source, target, send_sems, recv_sems):
        def one(i, _):
            q = lax.rem(me_frm + i, FRAMES)
            to_peer(source, target, send_sems, recv_sems, q).wait_send()
            return 0

        loop(1, FRAMES, one, 0)

    take(csend, crecv, c_send, c_recv)
    for b in range(TEAMS):
        curs[b] = jnp.concatenate(
            [crecv[f, 2 * b + i : 2 * b + i + 1, :] for i in range(2) for f in range(FRAMES)],
            axis=0,
        )
    freq = tab("freq")

    def make_ramp(f, _):
        angle = freq[:48] * crecv[f, PER : PER + 1, :] + freq[48:] * crecv[f, PER + 1 : PER + 2, :]
        sin, cos = sincos(angle)
        ramp[f, 0] = cos
        ramp[f, 1] = sin
        return 0

    loop(0, FRAMES, make_ramp, 0)

    def half_spectra(values):
        asc[...] = right(values, tab("t9"))
        for f in range(0, ITEMS, 2):
            stacked = []
            for g in (f, f + 1):
                part = asc[g * N : (g + 1) * N, :]
                stacked.append(jnp.concatenate([part[:, :128], part[:, 128:]], axis=0))
            both = left(tab("l10"), jnp.concatenate(stacked, axis=1))
            yield f, both[:, :128]
            yield f + 1, both[:, 128:]

    low_lanes = lax.broadcasted_iota(jnp.int32, (XP * ITEMS, 128), 1) < 64

    def forward(b):
        cab = fine(curs[b], tab("m1"))
        phase = fine(jnp.concatenate([cab] * XP, axis=0) * tab("along"), tab("t3"))
        sin, cos = sincos(phase)
        mask = tab("mask")
        pr, pi = cos * mask, sin * mask
        pup[b, 0] = pr
        pup[b, 1] = pi
        for h in range(2):
            if h == 0:
                mix = jnp.where(low_lanes, pr, pltpu.roll(pi, 64, 1))
            else:
                mix = jnp.where(low_lanes, pltpu.roll(pr, 64, 1), pi)
            both = right(mix, tab("t5p"))
            ysc[h] = both[:, :128]
            ysc[2 + h] = both[:, 128:]
        spreads = []
        for f in range(0, ITEMS, 2):
            pair = []
            for g in (f, f + 1):
                pair.append(
                    jnp.concatenate([ysc[h, pl.ds(g, XP, ITEMS), :] for h in range(4)], axis=0)
                )
            both = left(tab("l7"), jnp.concatenate(pair, axis=1))
            for g in (0, 1):
                one = both[:, 128 * g : 128 * g + 128]
                foc[b, f + g] = one
                spreads.append(one[:N] * one[:N] + one[N:] * one[N:])
        for f, one in half_spectra(jnp.concatenate(spreads, axis=0)):
            tra[b, f] = one

    def estimate(j):
        return pltpu.make_async_remote_copy(
            src_ref=esend.at[j],
            dst_ref=obj.at[2 * side + lax.rem(j, 2)],
            send_sem=e_send.at[j],
            recv_sem=e_recv.at[2 * side + lax.rem(j, 2)],
            device_id={"frm": half, "pat": 2 * me_frm + lax.div(j, 2)},
            device_id_type=MESH,
        )

    def estimate_here(j):
        return pltpu.make_async_copy(
            esend.at[j], obj.at[2 * side + lax.rem(j, 2)], e_own.at[j]
        )

    def estimate_stays(j):
        return same & (2 * me_frm + lax.div(j, 2) == me_pat)

    def fill_estimate(j, ere, eim):
        spectrum = jnp.concatenate([ere, eim], axis=0) * (1.0 / N)
        hi, lo = split(spectrum)
        flipped = dot(jnp.concatenate([hi, lo], axis=1), tab("flip"))
        hi, lo = split(jnp.concatenate([spectrum, flipped], axis=0))
        whole = dot(tab("place"), jnp.concatenate([hi, lo], axis=0))
        esend[j, 0] = whole[:N]
        esend[j, 1] = whole[N:]

    def send_estimate(j):
        @pl.when(jnp.logical_not(estimate_stays(j)))
        def _():
            estimate(j).start()

        @pl.when(estimate_stays(j))
        def _():
            estimate_here(j).start()

    def backward(b, step, last):
        for i in range(2):
            cre = jnp.zeros((48, 128), f32)
            cim = jnp.zeros((48, 128), f32)
            den = jnp.full((48, 128), DAMPING, f32)
            for f in range(FRAMES * i, FRAMES * (i + 1)):
                tre, tim = tra[b, f, :48], tra[b, f, 48:]
                dre, dim = dat[f, :48], dat[f, 48:]
                cre = cre + (dre * tre + dim * tim)
                cim = cim + (dim * tre - dre * tim)
                den = den + (tre * tre + tim * tim)
            ere, eim = cre / den, cim / den
            for f in range(FRAMES * i, FRAMES * (i + 1)):
                tre, tim = tra[b, f, :48], tra[b, f, 48:]
                mre = dat[f, :48] - (ere * tre - eim * tim)
                mim = dat[f, 48:] - (ere * tim + eim * tre)
                gsc[f * 48 : f * 48 + 48, :128] = ere * mre + eim * mim
                gsc[f * 48 : f * 48 + 48, 128:] = ere * mim - eim * mre
            if last:
                fill_estimate(2 * b + i, ere, eim)
        if last:
            send_estimate(2 * b)
            send_estimate(2 * b + 1)
        gsc[...] = right(gsc[...], tab("t12"))
        for f in range(0, ITEMS, 2):
            pair = []
            for g in (f, f + 1):
                part = gsc[g * 48 : g * 48 + 48, :]
                pair.append(jnp.concatenate([part[:, :128], part[:, 128:]], axis=0))
            grad = left(tab("l13"), jnp.concatenate(pair, axis=1))[:N]
            pair = []
            for g in (0, 1):
                one = grad[:, 128 * g : 128 * g + 128]
                pair.append(
                    jnp.concatenate([one * foc[b, f + g, :N], one * foc[b, f + g, N:]], axis=0)
                )
            both = left(tab("l15"), jnp.concatenate(pair, axis=1))
            for g in (0, 1):
                re, im = (both[k : k + 48, 128 * g : 128 * g + 128] for k in (0, 48))
                for h in range(2):
                    rows = slice(XP * h, XP * h + XP)
                    hsc[2 * h, pl.ds(f + g, XP, ITEMS), :] = re[rows]
                    hsc[2 * h + 1, pl.ds(f + g, XP, ITEMS), :] = im[rows]
        sides = []
        for h in range(2):
            hi, lo = split(jnp.concatenate([hsc[2 * h], hsc[2 * h + 1]], axis=1))
            one = dot(jnp.concatenate([hi, lo], axis=1), tab("t16p"))
            sides.append(one[:, :128] + one[:, 128:])
        gre = jnp.where(low_lanes, sides[0], pltpu.roll(sides[1], 64, 1))
        gim = jnp.where(low_lanes, pltpu.roll(sides[0], 64, 1), sides[1])
        grad = gim * pup[b, 0] - gre * pup[b, 1]
        gab = fine(grad, tab("t18")) * tab("along")
        acc = gab[:ITEMS]
        for i in range(1, XP):
            acc = acc + gab[i * ITEMS : (i + 1) * ITEMS]
        curs[b] = curs[b] - step * fine(acc, tab("m2"))

    def first_half(j, _):
        forward(j)
        return 0

    @pl.when(me_pat < GROUPS - 1)
    def _():
        halo.wait_recv()

    lane = lax.broadcasted_iota(jnp.int32, (N, 128), 1)
    top = me_pat * SH

    def pixels(b, q):
        return pltpu.make_async_remote_copy(
            src_ref=send.at[b, q],
            dst_ref=recv.at[b, me_frm],
            send_sem=msg_send.at[b, q],
            recv_sem=msg_recv.at[b, me_frm],
            device_id={"frm": q, "pat": me_pat},
            device_id_type=MESH,
        )

    def pixels_from(b, q):
        return pltpu.make_async_remote_copy(
            src_ref=send.at[b, q],
            dst_ref=recv.at[b, q],
            send_sem=msg_send.at[b, q],
            recv_sem=msg_recv.at[b, q],
            device_id={"frm": q, "pat": me_pat},
            device_id_type=MESH,
        )

    def patch(slot):
        p = slots[slot]
        row = jnp.clip(anchors[0, p] - top, 0, SH - 1)
        col = anchors[1, p]
        tile = jnp.clip(lax.shift_right_logical(col, 7), 0, 15)
        off = col & 127
        a = strip[tile, pl.ds(row, N), :]
        b = strip[jnp.minimum(tile + 1, 15), pl.ds(row, N), :]
        turn = (128 - off) & 127
        return jnp.where(lane < 128 - off, pltpu.roll(a, turn, 1), pltpu.roll(b, turn, 1))

    def cut(n, _):
        b, q = lax.div(n, FRAMES), lax.rem(me_frm + 1 + lax.rem(n, FRAMES), FRAMES)
        one = patch(PER * q + 2 * b)
        two = pltpu.roll(patch(PER * q + 2 * b + 1), N, 1)
        upper = jnp.where(lane < N, one, two)
        lower = jnp.where(
            lane[:48] < 64,
            two[:48],
            pltpu.roll(jnp.concatenate([two[48:], two[80:]], axis=0), 64, 1),
        )

        @pl.when(q != me_frm)
        def _():
            send[b, q, :N] = upper
            send[b, q, N:] = lower
            pixels(b, q).start()

        @pl.when(q == me_frm)
        def _():
            recv[b, me_frm, :N] = upper
            recv[b, me_frm, N:] = lower

        return 0

    loop(0, TEAMS * FRAMES, cut, 0)
    loop(0, TEAMS, first_half, 0)

    def work(b, _):
        def arrived(i, _):
            pixels_from(b, lax.rem(me_frm + i, FRAMES)).wait_recv()
            return 0

        loop(1, FRAMES, arrived, 0)
        window = tab("window")
        parts, steps = [], []
        for i in range(2):
            total = jnp.zeros((N, 128), f32)
            for f in range(FRAMES):
                if i == 0:
                    part = recv[b, f, :N]
                else:
                    rest = recv[b, f, N:]
                    part = jnp.concatenate([rest, pltpu.roll(rest, 64, 1)[:40]], axis=0)
                    part = pltpu.roll(jnp.where(lane < N, part, recv[b, f, :N]), 40, 1)
                part = jnp.where(lane < N, part, 0.0) * window
                total = total + part * part
                parts.append(part)
            energy = jnp.sum(total) * float(N * N)
            steps.append((STEP * FRAMES) / (jnp.zeros((FRAMES, 128), f32) + energy))
        for f, one in half_spectra(jnp.concatenate(parts, axis=0)):
            re, im = one[:48], one[48:]
            cos, sin = ramp[f % FRAMES, 0], ramp[f % FRAMES, 1]
            dat[f, :48] = re * cos - im * sin
            dat[f, 48:] = re * sin + im * cos
        step = jnp.concatenate(steps, axis=0)
        for t in range(ITERS):
            if t > 0:
                forward(b)
            backward(b, step, t == ITERS - 1)
        for i in range(2):
            for f in range(FRAMES):
                row = FRAMES * i + f
                nsend[f, pl.ds(2 * b + i, 1), :] = curs[b, row : row + 1, :]
        return 0

    nsend[...] = jnp.zeros((FRAMES, 8, 128), f32)
    loop(0, TEAMS, work, 0)

    def give(i, _):
        q = lax.rem(me_frm + i, FRAMES)
        to_peer(nsend, nrecv, n_send, n_recv, q).start()
        return 0

    loop(1, FRAMES, give, 0)
    nrecv[me_frm] = nsend[me_frm]

    def end_estimate(j, _):
        stays = estimate_stays(j)

        @pl.when(jnp.logical_not(stays))
        def _():
            estimate(j).wait_send()

        @pl.when(stays)
        def _():
            estimate_here(j).wait()

        return 0

    def end_pixels(n, _):
        j, q = lax.div(n, FRAMES), lax.rem(n, FRAMES)

        @pl.when(q != me_frm)
        def _():
            pixels(j, q).wait_send()

        return 0

    loop(0, TEAMS * FRAMES, end_pixels, 0)
    drain(csend, crecv, c_send, c_recv)

    @pl.when(me_pat > 0)
    def _():
        halo.wait_send()

    take(nsend, nrecv, n_send, n_recv)

    index = lax.broadcasted_iota(jnp.int32, (PPS, 128), 0)
    placed = jnp.zeros((PPS, 128), f32)
    for n in range(PPS):
        row = nrecv[n // PER, n % PER : n % PER + 1, :]
        placed = jnp.where(index == slots[n], row, placed)
    out[...] = placed
    loop(0, PER, end_estimate, 0)
    drain(nsend, nrecv, n_send, n_recv)

    def estimate_from(k, _):
        source = 2 * me_frm + lax.div(k, 2)

        @pl.when(jnp.logical_not(same & (source == me_pat)))
        def _():
            pltpu.make_async_remote_copy(
                src_ref=esend.at[k],
                dst_ref=obj.at[k],
                send_sem=e_send.at[k],
                recv_sem=e_recv.at[k],
                device_id={"frm": half, "pat": source},
                device_id_type=MESH,
            ).wait_recv()

        return 0

    loop(0, 4, estimate_from, 0)


def shards(frames, shifts, coefficients, anchors, assign):
    arrays = packed()[0]
    hbm = pl.BlockSpec(memory_space=pltpu.HBM)
    sems = pltpu.SemaphoreType.DMA
    obj, new = pl.pallas_call(
        kernel,
        in_specs=[hbm] * (5 + len(arrays)),
        out_specs=[hbm, pl.BlockSpec(memory_space=pltpu.VMEM)],
        out_shape=[
            jax.ShapeDtypeStruct((PER, 2, N, 128), f32),
            jax.ShapeDtypeStruct((PPS, 128), f32),
        ],
        scratch_shapes=[pltpu.VMEM(a.shape, a.dtype) for a in arrays]
        + [
            pltpu.SMEM((1, 2), f32),
            pltpu.VMEM((1, PPS, MODES), f32),
            pltpu.SMEM((2, PPS), jnp.int32),
            pltpu.SMEM((PPS,), jnp.int32),
            pltpu.SMEM((PPS,), jnp.int32),
            pltpu.VMEM((16, SH + N, 128), f32),
            pltpu.VMEM((TEAMS, FRAMES, ROWS, 128), f32),
            pltpu.VMEM((TEAMS, FRAMES, ROWS, 128), f32),
            pltpu.VMEM((FRAMES, 8, 128), f32),
            pltpu.VMEM((FRAMES, 8, 128), f32),
            pltpu.VMEM((FRAMES, 8, 128), f32),
            pltpu.VMEM((FRAMES, 8, 128), f32),
            pltpu.VMEM((PER, 2, N, 128), f32),
            pltpu.VMEM((FRAMES, 2, 48, 128), f32),
            pltpu.VMEM((TEAMS, ITEMS, 128), f32),
            pltpu.VMEM((TEAMS, 2, XP * ITEMS, 128), f32),
            pltpu.VMEM((TEAMS, ITEMS, 176, 128), f32),
            pltpu.VMEM((TEAMS, ITEMS, 96, 128), f32),
            pltpu.VMEM((ITEMS, 96, 128), f32),
            pltpu.VMEM((4, XP * ITEMS, 128), f32),
            pltpu.VMEM((ITEMS * N, 256), f32),
            pltpu.VMEM((ITEMS * 48, 256), f32),
            pltpu.VMEM((4, XP * ITEMS, 128), f32),
            sems((4,)),
            sems((len(arrays),)),
            sems((16,)),
            sems,
            sems,
            sems((TEAMS, FRAMES)),
            sems((TEAMS, FRAMES)),
            sems((FRAMES,)),
            sems((FRAMES,)),
            sems((FRAMES,)),
            sems((FRAMES,)),
            sems((PER,)),
            sems((PER,)),
            sems((PER,)),
        ],
        compiler_params=pltpu.CompilerParams(
            collective_id=0, has_side_effects=True, vmem_limit_bytes=56 << 20
        ),
        name="deconvolve",
    )(frames, shifts, coefficients, anchors.T, assign, *[jnp.asarray(a) for a in arrays])
    return new[None, :, :MODES], obj[:, :, :, :N].reshape(PER, 2, N * N)


def solution(mesh):
    in_specs = (
        P("frm", "pat", None),
        P("frm", None),
        P("frm", "pat", None),
        P("pat", None),
        P("pat"),
    )
    out_specs = (P("frm", "pat", None), P(("pat", "frm"), None, None))
    return jax.shard_map(shards, mesh=mesh, in_specs=in_specs, out_specs=out_specs, check_vma=False)
```
